32 devices in a mesh: dp: 8 (over z, y), fsdp: 4 (over x, core).
Axes of the slice: x: 2, y: 2, z: 4, core: 2. Of those that a mesh axis runs over, the one named last changes fastest.
Arguments:
- frames: bfloat16 [4, 48, 32, 1536], P('fsdp', 'dp'), may hold values from -6 to 6
- ln_gain: float32 [1536], replicated, may hold values from 0.5 to 1.5
- w_in: bfloat16 [1536, 3072], P(('dp', 'fsdp')), may hold values from -0.15625 to 0.15625
- depth_kernel: float32 [31, 1536], replicated, may hold values from -1 to 1
- bn_scale: float32 [1536], replicated, may hold values from 0.5 to 1.5
- bn_shift: float32 [1536], replicated, may hold values from -3 to 3
- w_out: bfloat16 [1536, 1536], P(('dp', 'fsdp')), may hold values from -0.15625 to 0.15625
- lengths: int32 [4, 8, 6], P('fsdp'), may hold values from 0 to 32, as said below
- destinations: int32 [4, 8, 6], P('fsdp'), may hold values from 0 to 7, as said below
- offsets: int32 [4, 8, 6], P('fsdp'), may hold values from 0 to 32, as said below
Outputs:
- encoded: bfloat16 [4, 16, 32, 1536], P('fsdp', 'dp')
The draws below stay inside these ranges and needn't reach their ends.
Inputs may be any that keep to these rules, and one draw needn't show every extreme that they name: lengths: live slots come first in a loader and hold half of 32 to 32 frames; 0 marks an empty slot. In each group the busiest loader has all 6 slots live, the group has 16 live utterances, and one of them has 32 frames. destinations: within a group a loader sends at most one live utterance to a device, and every device receives exactly 2 live utterances. Empty slots hold 0. offsets: multiples of 32; the 2 live utterances received by one device have distinct offsets. Empty slots hold 0.
All inputs are finite; a program needn't handle non-finite values.
Results may differ from the reference program's by a relative error of at most 0.003.
Values may be sent and summed in bfloat16 or wider, within the bound.
No kernel may reach another device: no remote copies, remote signals or barrier semaphores. Data moves between devices by JAX's collectives and lax.ppermute only.
A program may use at most 128 MiB of HBM per device.

```python
import jax
import jax.numpy as jnp
from jax import lax

D = 1536
KERNEL = 31
MAXLEN = 32
RSLOT = 2
UTT = 6
N_DP = 8
N_FSDP = 4


def group_tables(group_key):
    key_one, key_two, key_three = jax.random.split(group_key, 3)
    base_counts = jnp.full((N_DP,), RSLOT, dtype=jnp.int32)
    base_counts = base_counts.at[0].set(UTT)
    base_counts = base_counts.at[1:1 + 2 * RSLOT].set(RSLOT - 1)
    order = jax.random.permutation(key_one, N_DP)
    counts = base_counts[order]
    slot_ids = jnp.arange(UTT, dtype=jnp.int32)
    live_mask = slot_ids[None, :] < counts[:, None]
    starts = jnp.cumsum(counts) - counts
    stream_index = starts[:, None] + slot_ids[None, :]
    device_order = jax.random.permutation(key_two, N_DP).astype(jnp.int32)
    dest_table = jnp.where(live_mask, device_order[stream_index % N_DP], 0)
    off_table = jnp.where(live_mask, stream_index // N_DP * MAXLEN, 0)
    raw_lengths = jax.random.randint(key_three, (N_DP, UTT), MAXLEN // 2, MAXLEN + 1)
    forced = (counts[:, None] == UTT) & (slot_ids[None, :] == 0)
    raw_lengths = jnp.where(forced, MAXLEN, raw_lengths)
    len_table = jnp.where(live_mask, raw_lengths, 0)
    return (len_table.astype(jnp.int32), dest_table.astype(jnp.int32), off_table.astype(jnp.int32))


def all_tables(key):
    group_keys = jax.random.split(jax.random.fold_in(key, 71), N_FSDP)
    return jax.vmap(group_tables)(group_keys)


def draw_lengths(key, part):
    return all_tables(key)[0]


def draw_destinations(key, part):
    return all_tables(key)[1]


def draw_offsets(key, part):
    return all_tables(key)[2]


def block_scale(stream_key, shape, pieces, smallest, high):
    gain = 1.0
    for position, parts in pieces:
        draws = jax.random.uniform(jax.random.fold_in(jax.random.fold_in(stream_key, 6), position), (parts,), jnp.float32, smallest / len(pieces), high / len(pieces))
        gain = gain * jnp.repeat(jnp.exp(draws), shape[position] // parts).reshape((-1,) + (1,) * (len(shape) - 1 - position))
    return gain


def bell_draw(rng, shape, deviation, reach, cuts=(), kind=jnp.bfloat16):
    loudness = block_scale(rng, shape, cuts, -0.22, 0.18) if cuts else 1.0
    array = jax.random.normal(rng, shape, jnp.float32) * deviation * loudness
    return jnp.minimum(jnp.maximum(array, -reach), reach).astype(kind)


def setup_inputs(seed: int = 0) -> dict:
    keys = jax.random.split(jax.random.key(seed), 11)
    frames = bell_draw(keys[0], (N_FSDP, N_DP * UTT, MAXLEN, D), 1.0, 6.0, ((0, 4), (1, 8)))
    ln_gain = jnp.clip(1.0 + 0.1 * jax.random.normal(keys[1], (D,), jnp.float32), 0.5, 1.5)
    w_in = bell_draw(keys[2], (D, 2 * D), D ** -0.5, 0.15625, ((0, 32),))
    depth_kernel = bell_draw(keys[3], (KERNEL, D), KERNEL ** -0.5, 1.0, (), jnp.float32)
    bn_scale = jnp.clip(1.0 + 0.1 * jax.random.normal(keys[4], (D,), jnp.float32), 0.5, 1.5)
    bn_shift = bell_draw(keys[5], (D,), 0.5, 3.0, (), jnp.float32)
    w_out = bell_draw(keys[6], (D, D), D ** -0.5, 0.15625, ((0, 32),))
    lengths = draw_lengths(jax.random.fold_in(keys[10], 71), 0)
    destinations = draw_destinations(jax.random.fold_in(keys[10], 71), 0)
    offsets = draw_offsets(jax.random.fold_in(keys[10], 71), 0)
    return {"frames": frames, "ln_gain": ln_gain, "w_in": w_in, "depth_kernel": depth_kernel, "bn_scale": bn_scale, "bn_shift": bn_shift, "w_out": w_out, "lengths": lengths, "destinations": destinations, "offsets": offsets}


def conv_module(blocks, utt_lengths, ln_gain, w_in, depth_kernel, bn_scale, bn_shift, w_out):
    block_count, frames_len, feature_width = blocks.shape
    wide_rows = blocks.reshape(block_count * frames_len, feature_width).astype(jnp.float32)
    row_mean = lax.optimization_barrier(jnp.mean(wide_rows, axis=1, keepdims=True))
    centred = wide_rows - row_mean
    row_var = lax.optimization_barrier(jnp.mean(centred * centred, axis=1, keepdims=True))
    normed = (centred * lax.rsqrt(row_var + 1e-05) * ln_gain).astype(jnp.bfloat16)
    glu_in = jnp.dot(normed, w_in, preferred_element_type=jnp.float32)
    gated_units = glu_in[:, :feature_width] * jax.nn.sigmoid(glu_in[:, feature_width:])
    gated_units = gated_units.reshape(block_count, frames_len, feature_width)
    valid_mask = jnp.arange(frames_len, dtype=jnp.int32)[None, :] < utt_lengths[:, None]
    gated_units = jnp.where(valid_mask[:, :, None], gated_units, jnp.zeros((), gated_units.dtype))
    side_reach = (KERNEL - 1) // 2
    padded = jnp.pad(gated_units, ((0, 0), (side_reach, side_reach), (0, 0)))
    convolved = padded[:, 0:frames_len, :] * depth_kernel[0]
    for kernel_tap in range(1, KERNEL):
        convolved = convolved + padded[:, kernel_tap:kernel_tap + frames_len, :] * depth_kernel[kernel_tap]
    shifted = convolved * bn_scale + bn_shift
    activated = (shifted * jax.nn.sigmoid(shifted)).astype(jnp.bfloat16)
    activated = activated.reshape(block_count * frames_len, feature_width)
    mixed_out = wide_rows + jnp.dot(activated, w_out, preferred_element_type=jnp.float32)
    mixed_out = mixed_out.reshape(block_count, frames_len, feature_width)
    mixed_out = jnp.where(valid_mask[:, :, None], mixed_out, jnp.zeros((), mixed_out.dtype))
    return mixed_out.astype(jnp.bfloat16)

def reference(frames, ln_gain, w_in, depth_kernel, bn_scale, bn_shift, w_out, lengths, destinations, offsets):

    def one_group(group_data):
        group_frames, tab_len, tab_dest, tab_off = group_data
        key_table = jnp.where(tab_len > 0, tab_dest * RSLOT + tab_off // MAXLEN, -1).reshape(-1)
        targets = jnp.arange(N_DP * RSLOT, dtype=jnp.int32)
        match_table = (key_table[None, :] == targets[:, None]).astype(jnp.int32)
        slot_numbers = jnp.arange(N_DP * UTT, dtype=jnp.int32)
        source = lax.optimization_barrier(jnp.sum(match_table * slot_numbers[None, :], axis=1)).astype(jnp.int32)
        recv_len = lax.optimization_barrier(jnp.sum(match_table * tab_len.reshape(-1)[None, :], axis=1)).astype(jnp.int32)
        blocks = jnp.take(group_frames, source, axis=0)
        return conv_module(blocks, recv_len, ln_gain, w_in, depth_kernel, bn_scale, bn_shift, w_out)
    return lax.map(one_group, (frames, lengths, destinations, offsets))
```

```python
import functools

import jax
import jax.numpy as jnp
from jax import lax
from jax.experimental import pallas as pl
from jax.experimental.pallas import tpu as pltpu
from jax.sharding import PartitionSpec as P

ANY = pl.BlockSpec(memory_space=pl.ANY)
SMEM = pl.BlockSpec(memory_space=pltpu.SMEM)
VMEM = pl.BlockSpec(memory_space=pltpu.VMEM)
BF16 = jnp.bfloat16
F32 = jnp.float32


def call(kernel, out_shape, in_specs, out_specs, scratch, flops=0, moved=0):
    return pl.pallas_call(
        kernel,
        out_shape=out_shape,
        in_specs=in_specs,
        out_specs=out_specs,
        scratch_shapes=scratch,
        cost_estimate=pl.CostEstimate(flops=flops, bytes_accessed=moved, transcendentals=0),
        compiler_params=pltpu.CompilerParams(vmem_limit_bytes=48 * 1024 * 1024),
    )


def send_kernel(place, tab_len, tab_dest, frames, *refs):
    outs, sems = refs[:-1], refs[-1]
    me = place[0]
    copies = []
    for number, out in enumerate(outs):
        target = jnp.bitwise_xor(me, number + 1)

        def look(slot, found):
            hit = jnp.logical_and(tab_dest[me, slot] == target, tab_len[me, slot] > 0)
            return jnp.where(hit, slot, found)

        slot = lax.fori_loop(0, frames.shape[0], look, jnp.int32(0))
        copy = pltpu.make_async_copy(frames.at[slot], out, sems.at[number])
        copy.start()
        copies.append(copy)
    for copy in copies:
        copy.wait()


def norm_kernel(recv, place, tab_len, tab_dest, tab_off, gain, frames, *refs):
    arrived = refs[: tab_len.shape[0] - 1]
    kept, normed, lens, block, sems = refs[tab_len.shape[0] - 1 :]
    slots, long = frames.shape[0], frames.shape[1]
    me = place[0]
    for number in range(recv):

        def look(at, found):
            source, slot = at // slots, lax.rem(at, slots)
            length = tab_len[source, slot]
            hit = jnp.logical_and(
                jnp.logical_and(tab_dest[source, slot] == me, length > 0),
                tab_off[source, slot] == number * long,
            )
            return (
                jnp.where(hit, source, found[0]),
                jnp.where(hit, slot, found[1]),
                jnp.where(hit, length, found[2]),
            )

        zero = jnp.int32(0)
        source, slot, length = lax.fori_loop(
            0, tab_len.shape[0] * slots, look, (zero, zero, zero)
        )
        lens[number] = length
        shift = jnp.bitwise_xor(source, me)

        @pl.when(shift == 0)
        def _():
            pltpu.make_async_copy(frames.at[slot], block.at[number], sems.at[number]).start()

        for other, ref in enumerate(arrived):

            @pl.when(shift == other + 1)
            def _():
                pltpu.make_async_copy(ref, block.at[number], sems.at[number]).start()

    for number in range(recv):
        pltpu.make_async_copy(frames.at[0], block.at[number], sems.at[number]).wait()
        rows = block[number]
        kept[number] = rows
        wide = rows.astype(F32)
        mean = jnp.mean(wide, axis=1, keepdims=True)
        centred = wide - mean
        var = jnp.mean(centred * centred, axis=1, keepdims=True)
        value = centred * lax.rsqrt(var + 1e-05) * gain[...]
        steps = lax.broadcasted_iota(jnp.int32, value.shape, 0)
        normed[number] = jnp.where(steps < lens[number], value, 0.0).astype(BF16)


def glu_conv_kernel(parts, pieces, where, taps, scale, shift, *refs):
    normed, weights = refs[:parts], refs[parts : parts + pieces]
    outs = refs[parts + pieces : 2 * parts + pieces]
    rows_buf, w_buf, glu_buf, pad_buf, row_sems, w_sems = refs[2 * parts + pieces :]
    recv, long, width = normed[0].shape
    tall = recv * long
    depth = weights[0].shape[1]
    copies = []
    for number, ref in enumerate(normed):
        for slot in range(recv):
            copies.append(
                pltpu.make_async_copy(
                    ref.at[slot],
                    rows_buf.at[pl.ds(number * tall + slot * long, long)],
                    row_sems.at[number * recv + slot],
                )
            )
    for number, ref in enumerate(weights):
        for inner in range(ref.shape[0]):
            start = where[number, inner] * depth
            if depth % 16 == 0:
                start = pl.multiple_of(start, 16)
            else:
                start = 0
            copies.append(
                pltpu.make_async_copy(
                    ref.at[inner], w_buf.at[pl.ds(start, depth)], w_sems.at[number, inner]
                )
            )
    for copy in copies:
        copy.start()
    for copy in copies:
        copy.wait()
    glu_in = jnp.dot(rows_buf[...], w_buf[...], preferred_element_type=F32)
    chans = glu_in.shape[1] // 2
    glu_buf[...] = glu_in[:, :chans] * jax.nn.sigmoid(glu_in[:, chans:])
    reach = (taps.shape[0] - 1) // 2
    pad_buf[...] = jnp.zeros(pad_buf.shape, F32)
    for number, out in enumerate(outs):

        def utterance(slot, carry):
            start = pl.multiple_of(number * tall + slot * long, long)
            pad_buf[pl.ds(16, long), :] = glu_buf[pl.ds(start, long), :]
            total = pad_buf[pl.ds(16 - reach, long), :] * taps[0:1, :]
            for tap in range(1, taps.shape[0]):
                total = total + pad_buf[pl.ds(16 - reach + tap, long), :] * taps[tap : tap + 1, :]
            moved = total * scale[...] + shift[...]
            out[slot] = (moved * jax.nn.sigmoid(moved)).astype(BF16)
            return carry

        lax.fori_loop(0, recv, utterance, 0)


def mix_kernel(parts, pieces, where, lens, chip, kept, *refs):
    acts, weights = refs[:parts], refs[parts : parts + pieces]
    out, w_buf, w_sems = refs[parts + pieces :]
    recv, long, width = kept.shape
    depth = weights[0].shape[1]
    chans = acts[0].shape[2]
    copies = []
    for number, ref in enumerate(weights):
        for inner in range(ref.shape[0]):
            start = where[number, inner] * depth
            if depth % 16 == 0:
                start = pl.multiple_of(start, 16)
            else:
                start = 0
            copies.append(
                pltpu.make_async_copy(
                    ref.at[inner], w_buf.at[pl.ds(start, depth)], w_sems.at[number, inner]
                )
            )
    for copy in copies:
        copy.start()
    for copy in copies:
        copy.wait()
    total = kept[...].reshape(recv * long, width).astype(F32)
    for number, ref in enumerate(acts):
        first = jnp.bitwise_xor(chip[0], number) * chans
        total = total + jnp.dot(
            ref[...].reshape(recv * long, chans),
            w_buf[pl.ds(pl.multiple_of(first, 16), chans), :],
            preferred_element_type=F32,
        )
    total = total.reshape(recv, long, width)
    for number in range(recv):
        steps = lax.broadcasted_iota(jnp.int32, (long, width), 0)
        out[number] = jnp.where(steps < lens[number], total[number], 0.0).astype(out.dtype)


def shards(
    frames, ln_gain, w_in, depth_kernel, bn_scale, bn_shift, w_out, lengths, destinations, offsets
):
    dp_count, fsdp_count = lax.axis_size("dp"), lax.axis_size("fsdp")
    chips = (fsdp_count // 2) ** 2
    planes = dp_count * fsdp_count // (2 * chips)
    dp_index = lax.axis_index("dp")
    number = dp_index * fsdp_count + lax.axis_index("fsdp")
    core = number % 2
    chip = (number // 2) % chips
    plane = number // (2 * chips)
    all_devices = range(dp_count * fsdp_count)
    slots = lengths.shape[2]
    recv = slots // 3
    _, _, long, width = frames.shape
    depth = w_in.shape[0]
    chans = width // chips
    taps = depth_kernel.shape[0]

    def swap(array, mask):
        return lax.ppermute(array, ("dp", "fsdp"), [(at, at ^ mask) for at in all_devices])

    def climb(array):
        step = 2 * chips
        return lax.ppermute(
            array, ("dp", "fsdp"), [(at, (at + step) % len(all_devices)) for at in all_devices]
        )

    place = dp_index.astype(jnp.int32)[None]
    tab_len, tab_dest, tab_off = lengths[0], destinations[0], offsets[0]
    block = jax.ShapeDtypeStruct((long, width), BF16)
    chosen = call(
        send_kernel,
        [block] * (dp_count - 1),
        [SMEM, SMEM, SMEM, ANY],
        [ANY] * (dp_count - 1),
        [pltpu.SemaphoreType.DMA((dp_count - 1,))],
    )(place, tab_len, tab_dest, frames[0])
    arrived = [
        lax.ppermute(part, "dp", [(at, at ^ (mask + 1)) for at in range(dp_count)])
        for mask, part in enumerate(chosen)
    ]

    halves = w_in.reshape(depth, 2, width)

    def columns(owner):
        part = lax.dynamic_slice_in_dim(halves, owner * chans, chans, 2)
        return part.reshape(depth, 2 * chans)

    ring = jnp.stack(
        [columns(chip)] + [swap(columns(chip ^ mask), 2 * mask) for mask in range(1, chips)]
    )
    in_own = [ring]
    out_ring = w_out
    out_own = [out_ring]
    for _ in range(planes - 1):
        out_ring = climb(out_ring)
        out_own.append(out_ring)
    for _ in range(planes - 1):
        ring = climb(ring)
        in_own.append(ring)
    in_parts = in_own + [swap(part, 1) for part in in_own]

    out_stack = jnp.stack(out_own)
    out_plane = [out_stack] + [swap(out_stack, 2 * mask) for mask in range(1, chips)]
    out_parts = out_plane + [swap(part, 1) for part in out_plane]

    ring_plane = (plane - jnp.arange(planes)) % planes
    ring_chip = chip ^ jnp.arange(chips)
    rows_of = (ring_plane[:, None] * chips + ring_chip[None, :]) * 2
    in_where = jnp.concatenate([rows_of + core, rows_of + (1 - core)], 0).astype(jnp.int32)
    out_where = jnp.concatenate([rows_of.T + core, rows_of.T + (1 - core)], 0).astype(jnp.int32)
    if depth % 16:
        flat_in = jnp.concatenate(in_parts, 0)
        flat_out = jnp.concatenate(out_parts, 0)
        in_parts = [jnp.zeros_like(flat_in).at[in_where.reshape(-1)].set(flat_in)]
        out_parts = [jnp.zeros_like(flat_out).at[out_where.reshape(-1)].set(flat_out)]
        in_parts = [in_parts[0].reshape(1, width, 2 * chans)]
        out_parts = [out_parts[0].reshape(1, width, width)]
        in_where = out_where = jnp.zeros((1, 1), jnp.int32)

    utts = jax.ShapeDtypeStruct((recv, long, width), BF16)
    kept, normed, lens = call(
        functools.partial(norm_kernel, recv),
        [utts, utts, jax.ShapeDtypeStruct((recv,), jnp.int32)],
        [SMEM, SMEM, SMEM, SMEM, VMEM] + [ANY] * dp_count,
        [VMEM, VMEM, SMEM],
        [pltpu.VMEM((recv, long, width), BF16), pltpu.SemaphoreType.DMA((recv,))],
    )(place, tab_len, tab_dest, tab_off, ln_gain[None], frames[0], *arrived)

    all_normed = [normed] + [swap(normed, 2 * mask) for mask in range(1, chips)]

    def own_channels(array):
        return lax.dynamic_slice_in_dim(array, chip * chans, chans, array.ndim - 1)

    acts = call(
        functools.partial(glu_conv_kernel, chips, len(in_parts)),
        [jax.ShapeDtypeStruct((recv, long, chans), BF16)] * chips,
        [SMEM, VMEM, VMEM, VMEM] + [ANY] * (chips + len(in_parts)),
        [VMEM] * chips,
        [
            pltpu.VMEM((chips * recv * long, width), BF16),
            pltpu.VMEM((width, 2 * chans), BF16),
            pltpu.VMEM((chips * recv * long, chans), F32),
            pltpu.VMEM((long + 32, chans), F32),
            pltpu.SemaphoreType.DMA((chips * recv,)),
            pltpu.SemaphoreType.DMA(in_where.shape),
        ],
        flops=4 * chips * recv * long * width * chans,
        moved=4 * width * chans,
    )(
        in_where,
        own_channels(depth_kernel),
        own_channels(bn_scale[None]),
        own_channels(bn_shift[None]),
        *all_normed,
        *in_parts,
    )

    back = [acts[0]] + [swap(acts[mask], 2 * mask) for mask in range(1, chips)]
    result = call(
        functools.partial(mix_kernel, chips, len(out_parts)),
        utts,
        [SMEM, SMEM, SMEM, VMEM] + [VMEM] * chips + [ANY] * len(out_parts),
        VMEM,
        [pltpu.VMEM((width, width), BF16), pltpu.SemaphoreType.DMA(out_where.shape)],
        flops=2 * recv * long * width * width,
        moved=2 * width * width,
    )(out_where, lens, chip.astype(jnp.int32)[None], kept, *back, *out_parts)
    return result[None]


def solution(mesh):
    return jax.shard_map(
        shards,
        mesh=mesh,
        in_specs=(
            P("fsdp", "dp", None, None),
            P(),
            P(("dp", "fsdp"), None),
            P(),
            P(),
            P(),
            P(("dp", "fsdp"), None),
            P("fsdp", None, None),
            P("fsdp", None, None),
            P("fsdp", None, None),
        ),
        out_specs=P("fsdp", "dp", None, None),
        check_vma=False,
    )
```

```python
import functools
import math

import jax
import jax.numpy as jnp
from jax import lax
from jax.experimental import pallas as pl
from jax.experimental.pallas import tpu as pltpu
from jax.sharding import PartitionSpec as P

SMEM = pl.BlockSpec(memory_space=pltpu.SMEM)
VMEM = pl.BlockSpec(memory_space=pltpu.VMEM)
BF16 = jnp.bfloat16
F32 = jnp.float32


def call(kernel, out_shape, in_specs, out_specs, operands, scratch=(), flops=0):
    shapes = list(operands) + list(jax.tree.leaves(out_shape)) + list(scratch)
    total = sum(math.prod(shape.shape) * shape.dtype.itemsize for shape in shapes)
    return pl.pallas_call(
        kernel,
        out_shape=out_shape,
        in_specs=in_specs,
        out_specs=out_specs,
        scratch_shapes=[pltpu.VMEM(shape.shape, shape.dtype) for shape in scratch],
        cost_estimate=pl.CostEstimate(flops=flops, bytes_accessed=total, transcendentals=0),
        compiler_params=pltpu.CompilerParams(
            vmem_limit_bytes=min(total + total // 2 + 4 * 2**20, 60 * 2**20)
        ),
    )(*operands)


def like(dtype, *shape):
    return jax.ShapeDtypeStruct(shape, dtype)


def send_kernel(place, tab_len, tab_dest, frames, out):
    me = place[0]
    slots = frames.shape[0]

    def send(target, carry):
        found = jnp.int32(0)
        for slot in range(slots):
            hit = jnp.logical_and(tab_dest[me, slot] == target, tab_len[me, slot] > 0)
            found = jnp.where(hit, slot, found)
        out[target] = frames[found]
        return carry

    lax.fori_loop(0, out.shape[0], send, 0)


def table_kernel(
    long, planes, place, chip, tab_len, tab_dest, tab_off, taps, scale, shift, sources, lens, table
):
    source_count, slots = tab_len.shape
    me = place[0]

    def look(source, carry):
        for slot in range(slots):

            @pl.when(jnp.logical_and(tab_dest[source, slot] == me, tab_len[source, slot] > 0))
            def _():
                number = tab_off[source, slot] // long
                sources[number] = source
                lens[number] = tab_len[source, slot]

        return carry

    lax.fori_loop(0, source_count, look, 0)
    width, chans = scale.shape[1], table.shape[1]
    chips = width // chans
    run = chans // planes
    whole = jnp.concatenate([taps[...], scale[...], shift[...]], axis=0)
    for owner in range(chips):

        @pl.when(chip[0] == owner)
        def _():
            starts = [(plane * chips + owner) * run for plane in range(planes)]
            table[...] = jnp.concatenate([whole[:, at : at + run] for at in starts], axis=1)


def norm_kernel(sources, lens, gain, arrived, kept, normed):
    for number in range(kept.shape[0]):
        rows = arrived[sources[number]]
        kept[number] = rows
        wide = rows.astype(F32)
        mean = jnp.mean(wide, axis=1, keepdims=True)
        centred = wide - mean
        var = jnp.mean(centred * centred, axis=1, keepdims=True)
        value = centred * lax.rsqrt(var + 1e-05) * gain[...]
        steps = lax.broadcasted_iota(jnp.int32, value.shape, 0)
        normed[number] = jnp.where(steps < lens[number], value, 0.0).astype(BF16)


def split_kernel(planes, chip, weights, *refs):
    outs, buf = refs[:-1], refs[-1]
    chips = len(outs)
    width = weights.shape[1] // 2
    run = width // (planes * chips)
    for owner in range(chips):
        parts = [
            weights[:, pl.ds(half * width + (plane * chips + owner) * run, run)]
            for half in range(2)
            for plane in range(planes)
        ]
        buf[owner] = jnp.concatenate(parts, axis=1)
    for number, out in enumerate(outs):
        out[...] = buf[jnp.bitwise_xor(chip[0], number)]


def conv_rows(block, taps):
    long, chans = block.shape
    count = taps.shape[0]
    front = (count - 1) // 2
    groups = long // 8
    pieces = [block[8 * at : 8 * at + 8, :] for at in range(groups)]
    total = None
    for residue in range(8):
        rows = []
        for at in range(groups + 1):
            value = None
            for step in range(-(count // 8) - 1, count // 8 + 2):
                tap = 8 * step + residue + front - 16
                source = at + step - 2
                if 0 <= tap < count and 0 <= source < groups:
                    term = pieces[source] * taps[tap : tap + 1, :]
                    value = term if value is None else value + term
            rows.append(jnp.zeros((8, chans), F32) if value is None else value)
        whole = jnp.concatenate(rows, axis=0)[residue : residue + long, :]
        total = whole if total is None else total + whole
    return total


def main_kernel(parts, pieces, where, kept, table, *refs):
    normed, weights = refs[:parts], refs[parts : parts + pieces]
    own, outs = refs[parts + pieces], refs[parts + pieces + 1 : 2 * parts + pieces]
    rows_buf, in_buf, out_buf, glu_buf, act_buf = refs[2 * parts + pieces :]
    recv, long, width = kept.shape
    tall = recv * long
    chans = table.shape[1]
    taps = table[: table.shape[0] - 2, :]
    scale, shift = table[table.shape[0] - 2 : table.shape[0] - 1, :], table[table.shape[0] - 1 :, :]
    for number, ref in enumerate(normed):
        rows_buf[pl.ds(number * tall, tall), :] = ref[...].reshape(tall, width)
    if pieces == 2:
        w_in, w_out = weights
    else:
        w_in, w_out = in_buf, out_buf
        depth, wide = weights[0].shape[1:]
        for number, ref in enumerate(weights):
            for inner in range(parts):
                start = pl.multiple_of(where[number, inner] * depth, 16)
                in_buf[pl.ds(start, depth), :] = ref[inner]
            start = pl.multiple_of(where[number, parts] * depth, 16)
            for half in range(width // wide):
                out_buf[pl.ds(start, depth), half * wide : half * wide + wide] = ref[parts + half]
    glu_in = jnp.dot(rows_buf[...], w_in[...], preferred_element_type=F32)
    glu_buf[...] = glu_in[:, :chans] * jax.nn.sigmoid(glu_in[:, chans:])

    def utterance(at, carry):
        start = pl.multiple_of(at * long, long)
        moved = conv_rows(glu_buf[pl.ds(start, long), :], taps) * scale + shift
        act_buf[pl.ds(start, long), :] = (moved * jax.nn.sigmoid(moved)).astype(BF16)
        return carry

    lax.fori_loop(0, parts * recv, utterance, 0)
    batch = min(parts, 4)
    for first in range(0, parts, batch):
        mixed = jnp.dot(
            act_buf[pl.ds(first * tall, batch * tall), :],
            w_out[...],
            preferred_element_type=F32,
        )
        for number in range(first, first + batch):
            part = mixed[(number - first) * tall : (number - first + 1) * tall, :]
            part = part.reshape(recv, long, width)
            if number == 0:
                own[...] = kept[...].astype(F32) + part
            else:
                outs[number - 1][...] = part.astype(BF16)


def shards(
    frames, ln_gain, w_in, depth_kernel, bn_scale, bn_shift, w_out, lengths, destinations, offsets
):
    dp_count, fsdp_count = lax.axis_size("dp"), lax.axis_size("fsdp")
    chips = (fsdp_count // 2) ** 2
    planes = dp_count * fsdp_count // (2 * chips)
    dp_index = lax.axis_index("dp")
    number = dp_index * fsdp_count + lax.axis_index("fsdp")
    core = number % 2
    chip = (number // 2) % chips
    plane = number // (2 * chips)
    devices = dp_count * fsdp_count
    recv = lengths.shape[2] // 3
    _, _, long, width = frames.shape
    depth = w_in.shape[0]
    chans = width // chips
    wide = 2 * chans
    run = 2 * depth
    taps = depth_kernel.shape[0]

    def swap(array, mask):
        return lax.ppermute(array, ("dp", "fsdp"), [(at, at ^ mask) for at in range(devices)])

    def climb(array):
        pairs = [(at, (at + 2 * chips) % devices) for at in range(devices)]
        return lax.ppermute(array, ("dp", "fsdp"), pairs)

    place = dp_index.astype(jnp.int32)[None]
    chip_place = chip.astype(jnp.int32)[None]
    tab_len, tab_dest, tab_off = lengths[0], destinations[0], offsets[0]

    if depth % 16 == 0:
        split = call(
            functools.partial(split_kernel, planes),
            [like(BF16, depth, wide)] * chips,
            [SMEM, VMEM],
            [VMEM] * chips,
            (chip_place, w_in),
            [like(BF16, chips, depth, wide)],
        )
    else:
        by_owner = w_in.reshape(depth, 2, planes, chips, run).transpose(3, 0, 1, 2, 4)
        by_owner = by_owner.reshape(chips, depth, wide)
        split = [
            lax.dynamic_index_in_dim(by_owner, chip ^ mask, 0, keepdims=False)
            for mask in range(chips)
        ]
    columns = [split[0]] + [swap(split[mask], 2 * mask) for mask in range(1, chips)]
    halves = [w_out[:, at : at + wide] for at in range(0, width, wide)]
    ring = jnp.stack(columns + halves)

    send = call(
        send_kernel,
        like(BF16, dp_count, long, width),
        [SMEM, SMEM, SMEM, VMEM],
        VMEM,
        (place, tab_len, tab_dest, frames[0]),
    )
    ring, send = lax.optimization_barrier((ring, send))
    arrived = lax.all_to_all(send, "dp", split_axis=0, concat_axis=0, tiled=True)
    sources, lens, table = call(
        functools.partial(table_kernel, long, planes),
        [like(jnp.int32, recv), like(jnp.int32, recv), like(F32, taps + 2, chans)],
        [SMEM] * 5 + [VMEM] * 3,
        [SMEM, SMEM, VMEM],
        (place, chip_place, tab_len, tab_dest, tab_off)
        + (depth_kernel, bn_scale[None], bn_shift[None]),
    )

    rings = [ring]
    for _ in range(planes - 1):
        rings.append(climb(rings[-1]))
    pieces = rings + [swap(part, 1) for part in rings]

    ring_plane = (plane - jnp.arange(planes)) % planes
    ring_chip = chip ^ jnp.arange(chips)
    in_rows = (ring_plane[:, None] * chips + ring_chip[None, :]) * 2
    where = jnp.concatenate([in_rows, ring_plane[:, None] * 2], 1)
    where = jnp.concatenate([where + core, where + 1 - core], 0).astype(jnp.int32)
    if depth % 16:
        together = jnp.stack(pieces)
        flat = together[:, :chips].reshape(-1, depth, wide)
        all_in = jnp.zeros_like(flat).at[where[:, :chips].reshape(-1)].set(flat)
        flat = together[:, chips:].transpose(0, 2, 1, 3).reshape(-1, depth, width)
        all_out = jnp.zeros_like(flat).at[where[:, chips]].set(flat)
        pieces = [all_in.reshape(width, wide), all_out.reshape(chans, width)]

    utts = like(BF16, recv, long, width)
    kept, normed = call(
        norm_kernel,
        [utts, utts],
        [SMEM, SMEM, VMEM, VMEM],
        [VMEM, VMEM],
        (sources, lens, ln_gain[None], arrived),
    )
    normed = [normed] + [swap(normed, 2 * mask) for mask in range(1, chips)]

    tall = chips * recv * long
    own, *partial_sums = call(
        functools.partial(main_kernel, chips, len(pieces)),
        [like(F32, recv, long, width)] + [utts] * (chips - 1),
        [SMEM] + [VMEM] * (2 + chips + len(pieces)),
        [VMEM] * chips,
        (where, kept, table, *normed, *pieces),
        [
            like(BF16, tall, width),
            like(BF16, width, wide),
            like(BF16, chans, width),
            like(F32, tall, chans),
            like(BF16, tall, chans),
        ],
        flops=6 * tall * width * chans,
    )
    for mask, part in enumerate(partial_sums, 1):
        own = own + swap(part, 2 * mask).astype(F32)
    live = jnp.arange(long, dtype=jnp.int32)[None, :, None] < lens[:, None, None]
    return jnp.where(live, own, 0.0).astype(BF16)[None]


def solution(mesh):
    return jax.shard_map(
        shards,
        mesh=mesh,
        in_specs=(
            P("fsdp", "dp", None, None),
            P(),
            P(("dp", "fsdp"), None),
            P(),
            P(),
            P(),
            P(("dp", "fsdp"), None),
            P("fsdp", None, None),
            P("fsdp", None, None),
            P("fsdp", None, None),
        ),
        out_specs=P("fsdp", "dp", None, None),
        check_vma=False,
    )
```

```python
import functools
import math

import jax
import jax.numpy as jnp
from jax import lax
from jax.experimental import pallas as pl
from jax.experimental.pallas import tpu as pltpu
from jax.sharding import PartitionSpec as P

QUAD = 4
SMEM = pl.BlockSpec(memory_space=pltpu.SMEM)
VMEM = pl.BlockSpec(memory_space=pltpu.VMEM)
BF16 = jnp.bfloat16
F32 = jnp.float32


def call(kernel, out_shape, in_specs, out_specs, operands, scratch=(), flops=0):
    shapes = list(operands) + list(jax.tree.leaves(out_shape)) + list(scratch)
    total = sum(math.prod(shape.shape) * shape.dtype.itemsize for shape in shapes)
    return pl.pallas_call(
        kernel,
        out_shape=out_shape,
        in_specs=in_specs,
        out_specs=out_specs,
        scratch_shapes=[pltpu.VMEM(shape.shape, shape.dtype) for shape in scratch],
        cost_estimate=pl.CostEstimate(flops=flops, bytes_accessed=total, transcendentals=0),
        compiler_params=pltpu.CompilerParams(
            vmem_limit_bytes=min(total + total // 2 + 4 * 2**20, 60 * 2**20)
        ),
    )(*operands)


def like(dtype, *shape):
    return jax.ShapeDtypeStruct(shape, dtype)


def send_kernel(place, tab_len, tab_dest, frames, *outs):
    me = place[0]
    for number, out in enumerate(outs):
        for far in range(out.shape[0]):
            target = jnp.bitwise_xor(me, far * QUAD + number)
            found = jnp.int32(0)
            for slot in range(frames.shape[0]):
                hit = jnp.logical_and(tab_dest[me, slot] == target, tab_len[me, slot] > 0)
                found = jnp.where(hit, slot, found)
            out[far] = frames[found]


def merge_kernel(place, tab_len, tab_dest, tab_off, *refs):
    arrived, outs = refs[:QUAD], refs[QUAD:]
    me = place[0]
    long = arrived[0].shape[1]
    for far, out in enumerate(outs, 1):
        for number, ref in enumerate(arrived):
            source = jnp.bitwise_xor(me, number)
            target = jnp.bitwise_xor(me, far * QUAD)
            start = jnp.int32(-1)
            for slot in range(tab_len.shape[1]):
                hit = jnp.logical_and(
                    tab_dest[source, slot] == target, tab_len[source, slot] > 0
                )
                start = jnp.where(hit, tab_off[source, slot], start)

            @pl.when(start >= 0)
            def _():
                out[start // long] = ref[far]


def table_kernel(
    long, highs, place, quad, tab_len, tab_dest, tab_off, taps, scale, shift, sources, lens, table
):
    source_count, slots = tab_len.shape
    me = place[0]

    def look(source, carry):
        for slot in range(slots):

            @pl.when(jnp.logical_and(tab_dest[source, slot] == me, tab_len[source, slot] > 0))
            def _():
                number = tab_off[source, slot] // long
                sources[number] = source
                lens[number] = tab_len[source, slot]

        return carry

    lax.fori_loop(0, source_count, look, 0)
    run = scale.shape[1] // (highs * QUAD)
    whole = jnp.concatenate([taps[...], scale[...], shift[...]], axis=0)
    for owner in range(QUAD):

        @pl.when(quad[0] == owner)
        def _():
            starts = [(high * QUAD + owner) * run for high in range(highs)]
            table[...] = jnp.concatenate([whole[:, at : at + run] for at in starts], axis=1)


def norm_kernel(place, sources, lens, gain, *refs):
    near, far, (kept, normed) = refs[:QUAD], refs[QUAD:-2], refs[-2:]
    for number in range(kept.shape[0]):
        shift = jnp.bitwise_xor(sources[number], place[0])
        for other, ref in enumerate(near):

            @pl.when(shift == other)
            def _():
                kept[number] = ref[0]

        for other, ref in enumerate(far, 1):

            @pl.when(shift // QUAD == other)
            def _():
                kept[number] = ref[number]

        wide = kept[number].astype(F32)
        mean = jnp.mean(wide, axis=1, keepdims=True)
        centred = wide - mean
        var = jnp.mean(centred * centred, axis=1, keepdims=True)
        value = centred * lax.rsqrt(var + 1e-05) * gain[...]
        steps = lax.broadcasted_iota(jnp.int32, value.shape, 0)
        normed[number] = jnp.where(steps < lens[number], value, 0.0).astype(BF16)


def split_kernel(highs, quad, weights, *refs):
    outs, buf = refs[:-1], refs[-1]
    width = weights.shape[1] // 2
    run = width // (highs * QUAD)
    for owner in range(QUAD):
        parts = [
            weights[:, pl.ds(half * width + (high * QUAD + owner) * run, run)]
            for half in range(2)
            for high in range(highs)
        ]
        buf[owner] = jnp.concatenate(parts, axis=1)
    for number, out in enumerate(outs):
        out[...] = buf[jnp.bitwise_xor(quad[0], number)]


def conv_rows(block, taps):
    long, chans = block.shape
    count = taps.shape[0]
    front = (count - 1) // 2
    groups = long // 8
    pieces = [block[8 * at : 8 * at + 8, :] for at in range(groups)]
    total = None
    for residue in range(8):
        rows = []
        for at in range(groups + 1):
            value = None
            for step in range(-(count // 8) - 1, count // 8 + 2):
                tap = 8 * step + residue + front - 16
                source = at + step - 2
                if 0 <= tap < count and 0 <= source < groups:
                    term = pieces[source] * taps[tap : tap + 1, :]
                    value = term if value is None else value + term
            rows.append(jnp.zeros((8, chans), F32) if value is None else value)
        whole = jnp.concatenate(rows, axis=0)[residue : residue + long, :]
        total = whole if total is None else total + whole
    return total


def main_kernel(pieces, where, kept, table, *refs):
    normed, weights = refs[:QUAD], refs[QUAD : QUAD + pieces]
    own, outs = refs[QUAD + pieces], refs[QUAD + pieces + 1 : 2 * QUAD + pieces]
    rows_buf, in_buf, out_buf, glu_buf, act_buf = refs[2 * QUAD + pieces :]
    recv, long, width = kept.shape
    tall = recv * long
    chans = table.shape[1]
    taps = table[: table.shape[0] - 2, :]
    scale, shift = table[table.shape[0] - 2 : table.shape[0] - 1, :], table[table.shape[0] - 1 :, :]
    for number, ref in enumerate(normed):
        rows_buf[pl.ds(number * tall, tall), :] = ref[...].reshape(tall, width)
    if pieces == 2:
        w_in, w_out = weights
    else:
        w_in, w_out = in_buf, out_buf
        depth, wide = weights[0].shape[1:]
        for number, ref in enumerate(weights):
            for inner in range(QUAD):
                start = pl.multiple_of(where[number, inner] * depth, 16)
                in_buf[pl.ds(start, depth), :] = ref[inner]
            start = pl.multiple_of(where[number, QUAD] * depth, 16)
            for half in range(width // wide):
                out_buf[pl.ds(start, depth), half * wide : half * wide + wide] = ref[QUAD + half]
    glu_in = jnp.dot(rows_buf[...], w_in[...], preferred_element_type=F32)
    glu_buf[...] = glu_in[:, :chans] * jax.nn.sigmoid(glu_in[:, chans:])

    def utterance(at, carry):
        start = pl.multiple_of(at * long, long)
        moved = conv_rows(glu_buf[pl.ds(start, long), :], taps) * scale + shift
        act_buf[pl.ds(start, long), :] = (moved * jax.nn.sigmoid(moved)).astype(BF16)
        return carry

    lax.fori_loop(0, QUAD * recv, utterance, 0)
    mixed = jnp.dot(act_buf[...], w_out[...], preferred_element_type=F32)
    mixed = mixed.reshape(QUAD, recv, long, width)
    own[...] = kept[...].astype(F32) + mixed[0]
    for number, out in enumerate(outs, 1):
        out[...] = mixed[number].astype(BF16)


def shards(
    frames, ln_gain, w_in, depth_kernel, bn_scale, bn_shift, w_out, lengths, destinations, offsets
):
    dp_count, fsdp_count = lax.axis_size("dp"), lax.axis_size("fsdp")
    devices = dp_count * fsdp_count
    highs = dp_count // QUAD
    dp_index = lax.axis_index("dp")
    quad = dp_index % QUAD
    line = dp_index // QUAD * fsdp_count + lax.axis_index("fsdp")
    slots = lengths.shape[2]
    recv = slots // 3
    _, _, long, width = frames.shape
    depth = w_in.shape[0]
    chans = width // QUAD
    wide = 2 * chans
    taps = depth_kernel.shape[0]

    def swap(array, high=0, quad=0, fsdp=0):
        mask = (high * QUAD + quad) * fsdp_count + fsdp
        return lax.ppermute(array, ("dp", "fsdp"), [(at, at ^ mask) for at in range(devices)])

    def quad_swap(arrays):
        return [arrays[0]] + [swap(arrays[mask], quad=mask) for mask in range(1, QUAD)]

    place = dp_index.astype(jnp.int32)[None]
    quad_place = quad.astype(jnp.int32)[None]
    tab_len, tab_dest, tab_off = lengths[0], destinations[0], offsets[0]

    if depth % 16 == 0:
        split = call(
            functools.partial(split_kernel, highs),
            [like(BF16, depth, wide)] * QUAD,
            [SMEM, VMEM],
            [VMEM] * QUAD,
            (quad_place, w_in),
            [like(BF16, QUAD, depth, wide)],
        )
    else:
        by_owner = w_in.reshape(depth, 2, highs, QUAD, chans // highs).transpose(3, 0, 1, 2, 4)
        by_owner = by_owner.reshape(QUAD, depth, wide)
        split = [
            lax.dynamic_index_in_dim(by_owner, quad ^ mask, 0, keepdims=False)
            for mask in range(QUAD)
        ]
    halves = [w_out[:, at : at + wide] for at in range(0, width, wide)]
    pieces = [jnp.stack(quad_swap(split) + halves)]
    shifts = [0]
    bits = [1 << at for at in range((highs * fsdp_count).bit_length() - 1)]
    high_bits = [bit for bit in reversed(bits) if bit >= fsdp_count]
    chip_bits = [bit for bit in reversed(bits) if 1 < bit < fsdp_count]
    for bit in high_bits:
        pieces = pieces + [swap(part, high=bit // fsdp_count) for part in pieces]
        shifts = shifts + [shift ^ bit for shift in shifts]

    near = call(
        send_kernel,
        [like(BF16, highs, long, width)] * QUAD,
        [SMEM, SMEM, SMEM, VMEM],
        [VMEM] * QUAD,
        (place, tab_len, tab_dest, frames[0]),
    )
    near = quad_swap(near)
    utts = like(BF16, recv, long, width)
    far = call(
        merge_kernel,
        [utts] * (highs - 1),
        [SMEM] * 4 + [VMEM] * QUAD,
        [VMEM] * (highs - 1),
        (place, tab_len, tab_dest, tab_off, *near),
    )
    far = [swap(part, high=mask) for mask, part in enumerate(far, 1)]
    pieces[1:], _ = lax.optimization_barrier((pieces[1:], far))
    chip_first = [swap(pieces[0], fsdp=bit) for bit in chip_bits[:1]]
    early = [swap(part, fsdp=1) for part in pieces[:1] + chip_first]
    far, _ = lax.optimization_barrier((far, early))
    sources, lens, table = call(
        functools.partial(table_kernel, long, highs),
        [like(jnp.int32, recv), like(jnp.int32, recv), like(F32, taps + 2, chans)],
        [SMEM] * 5 + [VMEM] * 3,
        [SMEM, SMEM, VMEM],
        (place, quad_place, tab_len, tab_dest, tab_off)
        + (depth_kernel, bn_scale[None], bn_shift[None]),
    )
    kept, normed = call(
        norm_kernel,
        [utts, utts],
        [SMEM] * 3 + [VMEM] * (QUAD + highs),
        [VMEM, VMEM],
        (place, sources, lens, ln_gain[None], *near, *far),
    )
    for bit in chip_bits:
        first = chip_first if bit == chip_bits[0] else []
        pieces = pieces + first + [swap(part, fsdp=bit) for part in pieces[len(first) :]]
        shifts = shifts + [shift ^ bit for shift in shifts]
    ends = len(shifts) // 2 + 1
    normed = quad_swap([normed] * QUAD)
    pieces[ends:], _ = lax.optimization_barrier((pieces[ends:], normed[1]))
    cored = [swap(part, fsdp=1) for part in pieces]
    cored[0], cored[len(shifts) // 2] = early[0], early[-1]
    pieces = pieces + cored
    shifts = shifts + [shift ^ 1 for shift in shifts]
    out_rows = line ^ jnp.array(shifts)
    in_rows = out_rows // fsdp_count * QUAD
    in_rows = in_rows[:, None] + (quad ^ jnp.arange(QUAD))[None, :]
    in_rows = in_rows * fsdp_count + (out_rows % fsdp_count)[:, None]
    where = jnp.concatenate([in_rows, out_rows[:, None]], 1).astype(jnp.int32)
    if depth % 16:
        together = jnp.stack(pieces)
        flat = together[:, :QUAD].reshape(-1, depth, wide)
        all_in = jnp.zeros_like(flat).at[where[:, :QUAD].reshape(-1)].set(flat)
        flat = together[:, QUAD:].transpose(0, 2, 1, 3).reshape(-1, depth, width)
        all_out = jnp.zeros_like(flat).at[where[:, QUAD]].set(flat)
        pieces = [all_in.reshape(width, wide), all_out.reshape(chans, width)]

    tall = QUAD * recv * long
    partial_sums = call(
        functools.partial(main_kernel, len(pieces)),
        [like(F32, recv, long, width)] + [utts] * (QUAD - 1),
        [SMEM] + [VMEM] * (2 + QUAD + len(pieces)),
        [VMEM] * QUAD,
        (where, kept, table, *normed, *pieces),
        [
            like(BF16, tall, width),
            like(BF16, width, wide),
            like(BF16, chans, width),
            like(F32, tall, chans),
            like(BF16, tall, chans),
        ],
        flops=6 * tall * width * chans,
    )
    own, *others = quad_swap(partial_sums)
    for part in others:
        own = own + part.astype(F32)
    live = jnp.arange(long, dtype=jnp.int32)[None, :, None] < lens[:, None, None]
    return jnp.where(live, own, 0.0).astype(BF16)[None]


def solution(mesh):
    return jax.shard_map(
        shards,
        mesh=mesh,
        in_specs=(
            P("fsdp", "dp", None, None),
            P(),
            P(("dp", "fsdp"), None),
            P(),
            P(),
            P(),
            P(("dp", "fsdp"), None),
            P("fsdp", None, None),
            P("fsdp", None, None),
            P("fsdp", None, None),
        ),
        out_specs=P("fsdp", "dp", None, None),
        check_vma=False,
    )
```

```python
import functools
import math

import jax
import jax.numpy as jnp
from jax import lax
from jax.experimental import pallas as pl
from jax.experimental.pallas import tpu as pltpu
from jax.sharding import PartitionSpec as P

QUAD = 4
SMEM = pl.BlockSpec(memory_space=pltpu.SMEM)
VMEM = pl.BlockSpec(memory_space=pltpu.VMEM)
BF16 = jnp.bfloat16
F32 = jnp.float32


def call(kernel, out_shape, in_specs, out_specs, operands, scratch=(), flops=0):
    shapes = list(operands) + list(jax.tree.leaves(out_shape)) + list(scratch)
    total = sum(math.prod(shape.shape) * shape.dtype.itemsize for shape in shapes)
    return pl.pallas_call(
        kernel,
        out_shape=out_shape,
        in_specs=in_specs,
        out_specs=out_specs,
        scratch_shapes=[pltpu.VMEM(shape.shape, shape.dtype) for shape in scratch],
        cost_estimate=pl.CostEstimate(flops=flops, bytes_accessed=total, transcendentals=0),
        compiler_params=pltpu.CompilerParams(
            vmem_limit_bytes=min(total + total // 2 + 4 * 2**20, 60 * 2**20)
        ),
    )(*operands)


def like(dtype, *shape):
    return jax.ShapeDtypeStruct(shape, dtype)


class Tables:
    def __init__(self, ref, sources):
        self.ref = ref
        self.slots = ref.shape[0] // (3 * sources)
        self.size = sources * self.slots

    def live_for(self, source, slot, target):
        at = source * self.slots + slot
        return jnp.logical_and(self.ref[self.size + at] == target, self.ref[at] > 0)

    def length(self, source, slot):
        return self.ref[source * self.slots + slot]

    def offset(self, source, slot):
        return self.ref[2 * self.size + source * self.slots + slot]


def own_columns(highs, weights, owner, width):
    run = width // (highs * QUAD)
    parts = [
        weights[:, pl.ds(half * width + (high * QUAD + owner) * run, run)]
        for half in range(2)
        for high in range(highs)
    ]
    return jnp.concatenate(parts, axis=1)


def send_kernel(sources, place, packed, weights, frames, *refs):
    outs, buf = refs[:-1], refs[-1]
    tables = Tables(packed, sources)
    me = place[0]
    highs = sources // QUAD
    long, width = frames.shape[1:]
    wide = outs[0].shape[1]
    for owner in range(QUAD):
        buf[owner] = own_columns(highs, weights, owner, width)
    for number, out in enumerate(outs):
        for far in range(highs):
            target = jnp.bitwise_xor(me, far * QUAD + number)
            found = jnp.int32(0)
            for slot in range(tables.slots):
                found = jnp.where(tables.live_for(me, slot, target), slot, found)
            for half in range(width // wide):
                start = (far * (width // wide) + half) * long
                out[start : start + long, :] = frames[found, :, half * wide : half * wide + wide]
        start = highs * (width // wide) * long
        out[start:, :] = buf[jnp.bitwise_xor(lax.rem(me, QUAD), number)]


def fetch(out, number, ref, far):
    long, width = out.shape[1:]
    wide = ref.shape[1]
    for half in range(width // wide):
        start = (far * (width // wide) + half) * long
        out[number, :, half * wide : half * wide + wide] = ref[start : start + long, :]


def merge_kernel(sources, place, packed, last, *refs):
    arrived, outs, piece = refs[:QUAD], refs[QUAD:-1], refs[-1]
    tables = Tables(packed, sources)
    me = place[0]
    depth, wide = piece.shape[1:]
    for far, out in enumerate(outs, 1):
        long = out.shape[1]
        for number, ref in enumerate(arrived):
            source = jnp.bitwise_xor(me, number)
            target = jnp.bitwise_xor(me, far * QUAD)
            start = jnp.int32(-1)
            for slot in range(tables.slots):
                hit = tables.live_for(source, slot, target)
                start = jnp.where(hit, tables.offset(source, slot), start)

            @pl.when(start >= 0)
            def _():
                fetch(out, start // long, ref, far)

    for number, ref in enumerate(arrived):
        piece[number] = ref[ref.shape[0] - depth :, :]
    for half in range(piece.shape[0] - QUAD):
        piece[QUAD + half] = last[:, half * wide : half * wide + wide]


def split_kernel(highs, place, weights, *refs):
    outs, buf = refs[:-1], refs[-1]
    for owner in range(QUAD):
        buf[owner] = own_columns(highs, weights, owner, weights.shape[1] // 3)
    for number, out in enumerate(outs):
        out[...] = buf[jnp.bitwise_xor(lax.rem(place[0], QUAD), number)]


def stack_kernel(both, *refs):
    columns, piece = refs[:-1], refs[-1]
    wide = piece.shape[2]
    last = both.at[:, both.shape[1] // 3 * 2 :]
    for number, ref in enumerate(columns):
        piece[number] = ref[...]
    for half in range(piece.shape[0] - QUAD):
        piece[QUAD + half] = last[:, half * wide : half * wide + wide]


def table_kernel(source_count, long, place, packed, small, sources, lens, table, gain):
    tables = Tables(packed, source_count)
    highs = source_count // QUAD
    me = place[0]

    def look(source, carry):
        for slot in range(tables.slots):

            @pl.when(tables.live_for(source, slot, me))
            def _():
                number = tables.offset(source, slot) // long
                sources[number] = source
                lens[number] = tables.length(source, slot)

        return carry

    lax.fori_loop(0, source_count, look, 0)
    count, width = small.shape
    run = width // (highs * QUAD)
    whole = small[...]
    gain[...] = whole[count - 1 :, :]
    for owner in range(QUAD):

        @pl.when(lax.rem(me, QUAD) == owner)
        def _():
            starts = [(high * QUAD + owner) * run for high in range(highs)]
            parts = [whole[: count - 1, at : at + run] for at in starts]
            table[...] = jnp.concatenate(parts, axis=1)


def norm_kernel(place, sources, lens, gain, *refs):
    near, far, (kept, normed) = refs[:QUAD], refs[QUAD:-2], refs[-2:]
    for number in range(kept.shape[0]):
        shift = jnp.bitwise_xor(sources[number], place[0])
        for other, ref in enumerate(near):

            @pl.when(shift == other)
            def _():
                fetch(kept, number, ref, 0)

        for other, ref in enumerate(far, 1):

            @pl.when(shift // QUAD == other)
            def _():
                kept[number] = ref[number]

        wide = kept[number].astype(F32)
        mean = jnp.mean(wide, axis=1, keepdims=True)
        centred = wide - mean
        var = jnp.mean(centred * centred, axis=1, keepdims=True)
        value = centred * lax.rsqrt(var + 1e-05) * gain[...]
        steps = lax.broadcasted_iota(jnp.int32, value.shape, 0)
        normed[number] = jnp.where(steps < lens[number], value, 0.0).astype(BF16)


def conv_rows(block, taps):
    long, chans = block.shape
    count = taps.shape[0]
    front = (count - 1) // 2
    groups = long // 8
    pieces = [block[8 * at : 8 * at + 8, :] for at in range(groups)]
    total = None
    for residue in range(8):
        rows = []
        for at in range(groups + 1):
            value = None
            for step in range(-(count // 8) - 1, count // 8 + 2):
                tap = 8 * step + residue + front - 16
                source = at + step - 2
                if 0 <= tap < count and 0 <= source < groups:
                    term = pieces[source] * taps[tap : tap + 1, :]
                    value = term if value is None else value + term
            rows.append(jnp.zeros((8, chans), F32) if value is None else value)
        whole = jnp.concatenate(rows, axis=0)[residue : residue + long, :]
        total = whole if total is None else total + whole
    return total


def main_kernel(pieces, where, kept, table, *refs):
    normed, weights = refs[:QUAD], refs[QUAD : QUAD + pieces]
    own, outs = refs[QUAD + pieces], refs[QUAD + pieces + 1 : 2 * QUAD + pieces]
    rows_buf, in_buf, out_buf, glu_buf, act_buf = refs[2 * QUAD + pieces :]
    recv, long, width = kept.shape
    tall = recv * long
    chans = table.shape[1]
    taps = table[: table.shape[0] - 2, :]
    scale, shift = table[table.shape[0] - 2 : table.shape[0] - 1, :], table[table.shape[0] - 1 :, :]
    for number, ref in enumerate(normed):
        rows_buf[pl.ds(number * tall, tall), :] = ref[...].reshape(tall, width)
    if pieces == 2:
        w_in, w_out = weights
    else:
        w_in, w_out = in_buf, out_buf
        depth, wide = weights[0].shape[1:]
        for number, ref in enumerate(weights):
            for inner in range(QUAD):
                start = pl.multiple_of(where[number, inner] * depth, 16)
                in_buf[pl.ds(start, depth), :] = ref[inner]
            start = pl.multiple_of(where[number, QUAD] * depth, 16)
            for half in range(width // wide):
                out_buf[pl.ds(start, depth), half * wide : half * wide + wide] = ref[QUAD + half]
    glu_in = jnp.dot(rows_buf[...], w_in[...], preferred_element_type=F32)
    glu_buf[...] = glu_in[:, :chans] * jax.nn.sigmoid(glu_in[:, chans:])

    def utterance(at, carry):
        start = pl.multiple_of(at * long, long)
        moved = conv_rows(glu_buf[pl.ds(start, long), :], taps) * scale + shift
        act_buf[pl.ds(start, long), :] = (moved * jax.nn.sigmoid(moved)).astype(BF16)
        return carry

    lax.fori_loop(0, QUAD * recv, utterance, 0)
    mixed = jnp.dot(act_buf[...], w_out[...], preferred_element_type=F32)
    mixed = mixed.reshape(QUAD, recv, long, width)
    own[...] = kept[...].astype(F32) + mixed[0]
    for number, out in enumerate(outs, 1):
        out[...] = mixed[number].astype(BF16)


def shards(
    frames, ln_gain, w_in, depth_kernel, bn_scale, bn_shift, w_out, lengths, destinations, offsets
):
    dp_count, fsdp_count = lax.axis_size("dp"), lax.axis_size("fsdp")
    devices = dp_count * fsdp_count
    highs = dp_count // QUAD
    dp_index = lax.axis_index("dp")
    quad = dp_index % QUAD
    line = dp_index // QUAD * fsdp_count + lax.axis_index("fsdp")
    recv = lengths.shape[2] // 3
    _, _, long, width = frames.shape
    depth = w_in.shape[0]
    chans = width // QUAD
    wide = 2 * chans
    taps = depth_kernel.shape[0]

    def swap(array, high=0, quad=0, fsdp=0):
        mask = (high * QUAD + quad) * fsdp_count + fsdp
        return lax.ppermute(array, ("dp", "fsdp"), [(at, at ^ mask) for at in range(devices)])

    def quad_swap(arrays):
        return [arrays[0]] + [swap(arrays[mask], quad=mask) for mask in range(1, QUAD)]

    def gated(arrays, others):
        return lax.optimization_barrier((arrays, others))[0]

    place = dp_index.astype(jnp.int32)[None]
    packed = jnp.stack([lengths[0], destinations[0], offsets[0]]).reshape(-1)
    small = jnp.concatenate([depth_kernel, bn_scale[None], bn_shift[None], ln_gain[None]])
    count = width // wide
    bits = [1 << at for at in range((highs * fsdp_count).bit_length() - 1)]
    chip_bits = [bit for bit in reversed(bits) if 1 < bit < fsdp_count]

    both = jnp.concatenate([w_in, w_out], axis=1)
    far_rows = [swap(both, high=mask) for mask in range(1, highs)]

    near = call(
        functools.partial(send_kernel, dp_count),
        [like(BF16, highs * count * long + depth, wide)] * QUAD,
        [SMEM, SMEM, VMEM, VMEM],
        [VMEM] * QUAD,
        (place, packed, w_in, frames[0]),
        [like(BF16, QUAD, depth, wide)],
    )
    near = quad_swap(near)
    sources, lens, table, gain = call(
        functools.partial(table_kernel, dp_count, long),
        [like(jnp.int32, recv)] * 2 + [like(F32, taps + 2, chans), like(F32, 1, width)],
        [SMEM] * 2 + [VMEM],
        [SMEM, SMEM, VMEM, VMEM],
        (place, packed, small),
    )
    utts = like(BF16, recv, long, width)
    block = like(BF16, QUAD + count, depth, wide)
    *far, piece = call(
        functools.partial(merge_kernel, dp_count),
        [utts] * (highs - 1) + [block],
        [SMEM] * 2 + [VMEM] * (1 + QUAD),
        [VMEM] * highs,
        (gated(place, (lens, gain)), packed, w_out, *near),
    )
    pieces = [piece]
    shifts = [mask * fsdp_count for mask in range(highs)]
    far_rows = gated(far_rows, far)
    far = [swap(part, high=mask) for mask, part in enumerate(far, 1)]
    for part in far_rows:
        columns = call(
            functools.partial(split_kernel, highs),
            [like(BF16, depth, wide)] * QUAD,
            [SMEM, VMEM],
            [VMEM] * QUAD,
            (place, part),
            [like(BF16, QUAD, depth, wide)],
        )
        pieces.append(
            call(
                stack_kernel,
                block,
                [VMEM] * (1 + QUAD),
                VMEM,
                (part, *gated(quad_swap(columns), far)),
            )
        )
    early = len(pieces)
    cored = [swap(part, fsdp=1) for part in pieces]
    far = gated(far, (pieces, cored[:1]))
    for bit in chip_bits:
        pieces = pieces + [swap(part, fsdp=bit) for part in pieces]
        shifts = shifts + [shift ^ bit for shift in shifts]

    kept, normed = call(
        norm_kernel,
        [utts, utts],
        [SMEM] * 3 + [VMEM] * (QUAD + highs),
        [VMEM, VMEM],
        (place, sources, lens, gain, *near, *far),
    )
    normed = quad_swap([normed] * QUAD)
    late = pieces[early:]
    crossed = swap(jnp.stack(gated(late, normed[1:3])), fsdp=1)
    pieces = pieces + cored + [crossed[at] for at in range(len(late))]
    shifts = shifts + [shift ^ 1 for shift in shifts]

    out_rows = line ^ jnp.array(shifts)
    in_rows = out_rows // fsdp_count * QUAD
    in_rows = in_rows[:, None] + (quad ^ jnp.arange(QUAD))[None, :]
    in_rows = in_rows * fsdp_count + (out_rows % fsdp_count)[:, None]
    where = jnp.concatenate([in_rows, out_rows[:, None]], 1).astype(jnp.int32)
    if depth % 16:
        together = jnp.stack(pieces)
        flat = together[:, :QUAD].reshape(-1, depth, wide)
        all_in = jnp.zeros_like(flat).at[where[:, :QUAD].reshape(-1)].set(flat)
        flat = together[:, QUAD:].transpose(0, 2, 1, 3).reshape(-1, depth, width)
        all_out = jnp.zeros_like(flat).at[where[:, QUAD]].set(flat)
        pieces = [all_in.reshape(width, wide), all_out.reshape(chans, width)]

    tall = QUAD * recv * long
    partial_sums = call(
        functools.partial(main_kernel, len(pieces)),
        [like(F32, recv, long, width)] + [utts] * (QUAD - 1),
        [SMEM] + [VMEM] * (2 + QUAD + len(pieces)),
        [VMEM] * QUAD,
        (where, kept, table, *normed, *pieces),
        [
            like(BF16, tall, width),
            like(BF16, width, wide),
            like(BF16, chans, width),
            like(F32, tall, chans),
            like(BF16, tall, chans),
        ],
        flops=6 * tall * width * chans,
    )
    own, *others = quad_swap(partial_sums)
    for part in others:
        own = own + part.astype(F32)
    live = jnp.arange(long, dtype=jnp.int32)[None, :, None] < lens[:, None, None]
    return jnp.where(live, own, 0.0).astype(BF16)[None]


def solution(mesh):
    return jax.shard_map(
        shards,
        mesh=mesh,
        in_specs=(
            P("fsdp", "dp", None, None),
            P(),
            P(("dp", "fsdp"), None),
            P(),
            P(),
            P(),
            P(("dp", "fsdp"), None),
            P("fsdp", None, None),
            P("fsdp", None, None),
            P("fsdp", None, None),
        ),
        out_specs=P("fsdp", "dp", None, None),
        check_vma=False,
    )
```

```python
import functools
import math

import jax
import jax.numpy as jnp
from jax import lax
from jax.experimental import pallas as pl
from jax.experimental.pallas import tpu as pltpu
from jax.sharding import PartitionSpec as P

QUAD = 4
SMEM = pl.BlockSpec(memory_space=pltpu.SMEM)
VMEM = pl.BlockSpec(memory_space=pltpu.VMEM)
BF16 = jnp.bfloat16
F32 = jnp.float32


def call(kernel, out_shape, in_specs, out_specs, operands, scratch=(), flops=0):
    shapes = list(operands) + list(jax.tree.leaves(out_shape)) + list(scratch)
    total = sum(math.prod(shape.shape) * shape.dtype.itemsize for shape in shapes)
    return pl.pallas_call(
        kernel,
        out_shape=out_shape,
        in_specs=in_specs,
        out_specs=out_specs,
        scratch_shapes=[pltpu.VMEM(shape.shape, shape.dtype) for shape in scratch],
        cost_estimate=pl.CostEstimate(flops=flops, bytes_accessed=total, transcendentals=0),
        compiler_params=pltpu.CompilerParams(
            vmem_limit_bytes=min(total + total // 2 + 4 * 2**20, 60 * 2**20)
        ),
    )(*operands)


def like(dtype, *shape):
    return jax.ShapeDtypeStruct(shape, dtype)


class Tables:
    def __init__(self, ref, sources):
        self.ref = ref
        self.slots = ref.shape[0] // (3 * sources)
        self.size = sources * self.slots

    def live_for(self, source, slot, target):
        at = source * self.slots + slot
        return jnp.logical_and(self.ref[self.size + at] == target, self.ref[at] > 0)

    def length(self, source, slot):
        return self.ref[source * self.slots + slot]

    def offset(self, source, slot):
        return self.ref[2 * self.size + source * self.slots + slot]


def own_columns(highs, weights, owner):
    width = weights.shape[1] // 2
    run = width // (highs * QUAD)
    parts = [
        weights[:, pl.ds(half * width + (high * QUAD + owner) * run, run)]
        for half in range(2)
        for high in range(highs)
    ]
    return jnp.concatenate(parts, axis=1)


def send_kernel(place, packed, frames, out):
    tables = Tables(packed, out.shape[0])
    me = place[0]

    def send(target, carry):
        found = jnp.int32(0)
        for slot in range(tables.slots):
            found = jnp.where(tables.live_for(me, slot, target), slot, found)
        out[target] = frames[found]
        return carry

    lax.fori_loop(0, out.shape[0], send, 0)


def split_kernel(highs, place, weights, *refs):
    outs, buf = refs[:-1], refs[-1]
    for owner in range(QUAD):
        buf[owner] = own_columns(highs, weights, owner)
    for number, out in enumerate(outs):
        out[...] = buf[jnp.bitwise_xor(lax.rem(place[0], QUAD), number)]


def stack_kernel(*refs):
    parts, out = refs[:-1], refs[-1]
    wide = out.shape[2]
    at = 0
    for ref in parts:
        if len(ref.shape) == 3:
            out[at : at + ref.shape[0]] = ref[...]
            at += ref.shape[0]
        else:
            for first in range(0, ref.shape[1], wide):
                out[at] = ref[:, first : first + wide]
                at += 1


def table_kernel(source_count, long, place, packed, small, sources, lens, table, gain):
    tables = Tables(packed, source_count)
    highs = source_count // QUAD
    me = place[0]

    def look(source, carry):
        for slot in range(tables.slots):

            @pl.when(tables.live_for(source, slot, me))
            def _():
                number = tables.offset(source, slot) // long
                sources[number] = source
                lens[number] = tables.length(source, slot)

        return carry

    lax.fori_loop(0, source_count, look, 0)
    count, width = small.shape
    run = width // (highs * QUAD)
    whole = small[...]
    gain[...] = whole[count - 1 :, :]
    for owner in range(QUAD):

        @pl.when(lax.rem(me, QUAD) == owner)
        def _():
            starts = [(high * QUAD + owner) * run for high in range(highs)]
            parts = [whole[: count - 1, at : at + run] for at in starts]
            table[...] = jnp.concatenate(parts, axis=1)


def norm_kernel(sources, lens, gain, arrived, kept, normed):
    for number in range(kept.shape[0]):
        rows = arrived[sources[number]]
        kept[number] = rows
        wide = rows.astype(F32)
        mean = jnp.mean(wide, axis=1, keepdims=True)
        centred = wide - mean
        var = jnp.mean(centred * centred, axis=1, keepdims=True)
        value = centred * lax.rsqrt(var + 1e-05) * gain[...]
        steps = lax.broadcasted_iota(jnp.int32, value.shape, 0)
        normed[number] = jnp.where(steps < lens[number], value, 0.0).astype(BF16)


def conv_rows(block, taps):
    long, chans = block.shape
    count = taps.shape[0]
    front = (count - 1) // 2
    groups = long // 8
    pieces = [block[8 * at : 8 * at + 8, :] for at in range(groups)]
    total = None
    for residue in range(8):
        rows = []
        for at in range(groups + 1):
            value = None
            for step in range(-(count // 8) - 1, count // 8 + 2):
                tap = 8 * step + residue + front - 16
                source = at + step - 2
                if 0 <= tap < count and 0 <= source < groups:
                    term = pieces[source] * taps[tap : tap + 1, :]
                    value = term if value is None else value + term
            rows.append(jnp.zeros((8, chans), F32) if value is None else value)
        whole = jnp.concatenate(rows, axis=0)[residue : residue + long, :]
        total = whole if total is None else total + whole
    return total


def main_kernel(layout, where, kept, table, *refs):
    pieces = max(len(layout), 2)
    chans = table.shape[1]
    taps = table[: table.shape[0] - 2, :]
    scale, shift = table[table.shape[0] - 2 : table.shape[0] - 1, :], table[table.shape[0] - 1 :, :]
    normed, weights = refs[:QUAD], refs[QUAD : QUAD + pieces]
    own, outs = refs[QUAD + pieces], refs[QUAD + pieces + 1 : 2 * QUAD + pieces]
    rows_buf, in_buf, out_buf, glu_buf, act_buf = refs[2 * QUAD + pieces :]
    recv, long, width = kept.shape
    tall = recv * long
    for number, ref in enumerate(normed):
        rows_buf[pl.ds(number * tall, tall), :] = ref[...].reshape(tall, width)
    if layout:
        w_in, w_out = in_buf, out_buf
        depth, wide = weights[0].shape[1:]
        for ref, slabs in zip(weights, layout):
            for at, (kind, other, number) in enumerate(slabs):
                if kind == "in":
                    start = pl.multiple_of(where[other, number] * depth, 16)
                    in_buf[pl.ds(start, depth), :] = ref[at]
                else:
                    start = pl.multiple_of(where[other, QUAD] * depth, 16)
                    first = number * wide
                    out_buf[pl.ds(start, depth), first : first + wide] = ref[at]
    else:
        w_in, w_out = weights
    glu_in = jnp.dot(rows_buf[...], w_in[...], preferred_element_type=F32)
    glu_buf[...] = glu_in[:, :chans] * jax.nn.sigmoid(glu_in[:, chans:])

    def utterance(at, carry):
        start = pl.multiple_of(at * long, long)
        moved = conv_rows(glu_buf[pl.ds(start, long), :], taps) * scale + shift
        act_buf[pl.ds(start, long), :] = (moved * jax.nn.sigmoid(moved)).astype(BF16)
        return carry

    lax.fori_loop(0, QUAD * recv, utterance, 0)
    mixed = jnp.dot(act_buf[...], w_out[...], preferred_element_type=F32)
    mixed = mixed.reshape(QUAD, recv, long, width)
    own[...] = kept[...].astype(F32) + mixed[0]
    for number, out in enumerate(outs, 1):
        out[...] = mixed[number].astype(BF16)


def shards(
    frames, ln_gain, w_in, depth_kernel, bn_scale, bn_shift, w_out, lengths, destinations, offsets
):
    dp_count, fsdp_count = lax.axis_size("dp"), lax.axis_size("fsdp")
    devices = dp_count * fsdp_count
    highs = dp_count // QUAD
    dp_index = lax.axis_index("dp")
    quad = dp_index % QUAD
    line = dp_index // QUAD * fsdp_count + lax.axis_index("fsdp")
    recv = lengths.shape[2] // 3
    _, _, long, width = frames.shape
    depth = w_in.shape[0]
    chans = width // QUAD
    wide = 2 * chans
    taps = depth_kernel.shape[0]

    def swap(array, high=0, quad=0, fsdp=0):
        mask = (high * QUAD + quad) * fsdp_count + fsdp
        return lax.ppermute(array, ("dp", "fsdp"), [(at, at ^ mask) for at in range(devices)])

    def quad_swap(arrays):
        return [arrays[0]] + [swap(arrays[mask], quad=mask) for mask in range(1, QUAD)]

    def gated(arrays, others):
        return lax.optimization_barrier((arrays, others))[0]

    place = dp_index.astype(jnp.int32)[None]
    packed = jnp.stack([lengths[0], destinations[0], offsets[0]]).reshape(-1)
    small = jnp.concatenate([depth_kernel, bn_scale[None], bn_shift[None], ln_gain[None]])
    count = width // wide
    bits = [1 << at for at in range((highs * fsdp_count).bit_length() - 1)]
    chip_bits = [bit for bit in reversed(bits) if 1 < bit < fsdp_count]

    send = call(
        send_kernel,
        like(BF16, dp_count, long, width),
        [SMEM, SMEM, VMEM],
        VMEM,
        (place, packed, frames[0]),
    )
    arrived = lax.all_to_all(send, "dp", split_axis=0, concat_axis=0, tiled=True)
    sources, lens, table, gain = call(
        functools.partial(table_kernel, dp_count, long),
        [like(jnp.int32, recv)] * 2 + [like(F32, taps + 2, chans), like(F32, 1, width)],
        [SMEM] * 2 + [VMEM],
        [SMEM, SMEM, VMEM, VMEM],
        (place, packed, small),
    )
    utts = like(BF16, recv, long, width)
    def stack(*parts):
        slabs = sum(part.size // (depth * wide) for part in parts)
        return call(
            stack_kernel, like(BF16, slabs, depth, wide), [VMEM] * len(parts), VMEM, parts
        )

    def share_columns(rows):
        columns = call(
            functools.partial(split_kernel, highs),
            [like(BF16, depth, wide)] * QUAD,
            [SMEM, VMEM],
            [VMEM] * QUAD,
            (place, rows),
            [like(BF16, QUAD, depth, wide)],
        )
        return stack(*quad_swap(columns))

    ins = {0: share_columns(gated(w_in, send))}
    far_in = [swap(ins[0], high=mask) for mask in range(1, highs)]
    late_out = gated(w_out, ins[0])
    outs = {0: w_out}

    def share_chips(shifts):
        for bit in chip_bits:
            for shift in list(shifts):
                ins[shift ^ bit] = swap(ins[shift], fsdp=bit)
                outs[shift ^ bit] = swap(outs[shift], fsdp=bit)
                shifts.append(shift ^ bit)

    share_chips([0])
    early_cores = [swap(ins[shift], fsdp=1) for shift in ins]
    far_out = [swap(late_out, high=mask) for mask in range(1, highs)]
    arrived = gated(arrived, early_cores)
    kept, normed = call(
        norm_kernel,
        [utts, utts],
        [SMEM] * 2 + [VMEM] * 2,
        [VMEM, VMEM],
        (sources, lens, gain, arrived),
    )
    for mask, (rows, last) in enumerate(zip(far_in, far_out), 1):
        outs[mask * fsdp_count] = last
        ins[mask * fsdp_count] = rows
    normed = quad_swap([normed] * QUAD)
    share_chips([mask * fsdp_count for mask in range(1, highs)])
    early = [shift for shift in ins if shift < fsdp_count]
    late = [shift for shift in ins if shift >= fsdp_count]
    pieces = [ins[shift] for shift in early]
    last = [ins[shift] for shift in late] + [outs[shift] for shift in outs]
    pieces.append(stack(*gated(last, normed)))
    pieces = pieces + early_cores + [swap(pieces[-1], fsdp=1)]
    layout = []
    for core in range(2):
        for group in [[shift] for shift in early] + [late]:
            layout.append([("in", at ^ core, number) for at in group for number in range(QUAD)])
        layout[-1] += [("out", at ^ core, half) for at in outs for half in range(count)]

    out_rows = line ^ jnp.arange(highs * fsdp_count)
    in_rows = out_rows // fsdp_count * QUAD
    in_rows = in_rows[:, None] + (quad ^ jnp.arange(QUAD))[None, :]
    in_rows = in_rows * fsdp_count + (out_rows % fsdp_count)[:, None]
    where = jnp.concatenate([in_rows, out_rows[:, None]], 1).astype(jnp.int32)
    if depth % 16:
        slabs = {
            name: part[at]
            for part, names in zip(pieces, layout)
            for at, name in enumerate(names)
        }
        sides = range(highs * fsdp_count)
        flat = jnp.stack([slabs["in", at, number] for at in sides for number in range(QUAD)])
        all_in = jnp.zeros_like(flat).at[where[:, :QUAD].reshape(-1)].set(flat)
        flat = jnp.stack(
            [
                jnp.concatenate([slabs["out", at, half] for half in range(count)], axis=1)
                for at in sides
            ]
        )
        all_out = jnp.zeros_like(flat).at[where[:, QUAD]].set(flat)
        pieces = [all_in.reshape(width, wide), all_out.reshape(chans, width)]
        layout = []

    tall = QUAD * recv * long
    partial_sums = call(
        functools.partial(main_kernel, layout),
        [like(F32, recv, long, width)] + [utts] * (QUAD - 1),
        [SMEM] + [VMEM] * (2 + QUAD + len(pieces)),
        [VMEM] * QUAD,
        (where, kept, table, *normed, *pieces),
        [
            like(BF16, tall, width),
            like(BF16, width, wide),
            like(BF16, chans, width),
            like(F32, tall, chans),
            like(BF16, tall, chans),
        ],
        flops=6 * tall * width * chans,
    )
    own, *others = quad_swap(partial_sums)
    for part in others:
        own = own + part.astype(F32)
    live = jnp.arange(long, dtype=jnp.int32)[None, :, None] < lens[:, None, None]
    return jnp.where(live, own, 0.0).astype(BF16)[None]


def solution(mesh):
    return jax.shard_map(
        shards,
        mesh=mesh,
        in_specs=(
            P("fsdp", "dp", None, None),
            P(),
            P(("dp", "fsdp"), None),
            P(),
            P(),
            P(),
            P(("dp", "fsdp"), None),
            P("fsdp", None, None),
            P("fsdp", None, None),
            P("fsdp", None, None),
        ),
        out_specs=P("fsdp", "dp", None, None),
        check_vma=False,
    )
```

```python
import functools
import math

import jax
import jax.numpy as jnp
from jax import lax
from jax.experimental import pallas as pl
from jax.experimental.pallas import tpu as pltpu
from jax.sharding import PartitionSpec as P

SMEM = pl.BlockSpec(memory_space=pltpu.SMEM)
VMEM = pl.BlockSpec(memory_space=pltpu.VMEM)
BF16 = jnp.bfloat16
F32 = jnp.float32


def call(kernel, out_shape, in_specs, out_specs, operands, scratch=(), flops=0):
    shapes = list(operands) + list(jax.tree.leaves(out_shape)) + list(scratch)
    total = sum(math.prod(shape.shape) * shape.dtype.itemsize for shape in shapes)
    return pl.pallas_call(
        kernel,
        out_shape=out_shape,
        in_specs=in_specs,
        out_specs=out_specs,
        scratch_shapes=[pltpu.VMEM(shape.shape, shape.dtype) for shape in scratch],
        cost_estimate=pl.CostEstimate(flops=flops, bytes_accessed=total, transcendentals=0),
        compiler_params=pltpu.CompilerParams(
            vmem_limit_bytes=min(total + total // 2 + 4 * 2**20, 60 * 2**20)
        ),
    )(*operands)


def like(dtype, *shape):
    return jax.ShapeDtypeStruct(shape, dtype)


class Tables:
    def __init__(self, ref, sources):
        self.ref = ref
        self.slots = ref.shape[0] // (3 * sources)
        self.size = sources * self.slots

    def live_for(self, source, slot, target):
        at = source * self.slots + slot
        return jnp.logical_and(self.ref[self.size + at] == target, self.ref[at] > 0)

    def length(self, source, slot):
        return self.ref[source * self.slots + slot]

    def offset(self, source, slot):
        return self.ref[2 * self.size + source * self.slots + slot]


def own_columns(planes, chips, weights, owner):
    width = weights.shape[1] // 2
    run = width // (planes * chips)
    parts = [
        weights[:, pl.ds(half * width + (plane * chips + owner) * run, run)]
        for half in range(2)
        for plane in range(planes)
    ]
    return jnp.concatenate(parts, axis=1)


def send_kernel(place, packed, frames, out):
    tables = Tables(packed, out.shape[0])
    me = place[0]

    def send(target, carry):
        found = jnp.int32(0)
        for slot in range(tables.slots):
            found = jnp.where(tables.live_for(me, slot, target), slot, found)
        out[target] = frames[found]
        return carry

    lax.fori_loop(0, out.shape[0], send, 0)


def split_kernel(planes, chip, weights, *refs):
    outs, buf = refs[:-1], refs[-1]
    for owner in range(len(outs)):
        buf[owner] = own_columns(planes, len(outs), weights, owner)
    for number, out in enumerate(outs):
        out[...] = buf[jnp.bitwise_xor(chip[0], number)]


def table_kernel(
    source_count, long, planes, chips, place, chip, packed, small, sources, lens, table, gain
):
    tables = Tables(packed, source_count)
    me = place[0]

    def look(source, carry):
        for slot in range(tables.slots):

            @pl.when(tables.live_for(source, slot, me))
            def _():
                number = tables.offset(source, slot) // long
                sources[number] = source
                lens[number] = tables.length(source, slot)

        return carry

    lax.fori_loop(0, source_count, look, 0)
    count, width = small.shape
    run = width // (planes * chips)
    whole = small[...]
    gain[...] = whole[count - 1 :, :]
    for owner in range(chips):

        @pl.when(chip[0] == owner)
        def _():
            starts = [(plane * chips + owner) * run for plane in range(planes)]
            parts = [whole[: count - 1, at : at + run] for at in starts]
            table[...] = jnp.concatenate(parts, axis=1)


def norm_kernel(sources, lens, gain, arrived, kept, normed):
    for number in range(kept.shape[0]):
        rows = arrived[sources[number]]
        kept[number] = rows
        wide = rows.astype(F32)
        mean = jnp.mean(wide, axis=1, keepdims=True)
        centred = wide - mean
        var = jnp.mean(centred * centred, axis=1, keepdims=True)
        value = centred * lax.rsqrt(var + 1e-05) * gain[...]
        steps = lax.broadcasted_iota(jnp.int32, value.shape, 0)
        normed[number] = jnp.where(steps < lens[number], value, 0.0).astype(BF16)


def conv_rows(block, taps):
    long, chans = block.shape
    count = taps.shape[0]
    front = (count - 1) // 2
    groups = long // 8
    pieces = [block[8 * at : 8 * at + 8, :] for at in range(groups)]
    total = None
    for residue in range(8):
        rows = []
        for at in range(groups + 1):
            value = None
            for step in range(-(count // 8) - 1, count // 8 + 2):
                tap = 8 * step + residue + front - 16
                source = at + step - 2
                if 0 <= tap < count and 0 <= source < groups:
                    term = pieces[source] * taps[tap : tap + 1, :]
                    value = term if value is None else value + term
            rows.append(jnp.zeros((8, chans), F32) if value is None else value)
        whole = jnp.concatenate(rows, axis=0)[residue : residue + long, :]
        total = whole if total is None else total + whole
    return total


def main_kernel(chips, layout, where, kept, table, *refs):
    pieces = max(len(layout), 2)
    chans = table.shape[1]
    taps = table[: table.shape[0] - 2, :]
    scale, shift = table[table.shape[0] - 2 : table.shape[0] - 1, :], table[table.shape[0] - 1 :, :]
    normed, weights = refs[:chips], refs[chips : chips + pieces]
    own, outs = refs[chips + pieces], refs[chips + pieces + 1 : 2 * chips + pieces]
    rows_buf, in_buf, out_buf, glu_buf, act_buf = refs[2 * chips + pieces :]
    recv, long, width = kept.shape
    tall = recv * long
    for number, ref in enumerate(normed):
        rows_buf[pl.ds(number * tall, tall), :] = ref[...].reshape(tall, width)
    if layout:
        w_in, w_out = in_buf, out_buf
        depth, wide = weights[0].shape[1:]
        for ref, slabs in zip(weights, layout):
            for at, (kind, other, number) in enumerate(slabs):
                if kind == "in":
                    start = pl.multiple_of(where[other, number] * depth, 16)
                    in_buf[pl.ds(start, depth), :] = ref[at]
                else:
                    start = pl.multiple_of(where[other, chips] * depth, 16)
                    first = number * wide
                    out_buf[pl.ds(start, depth), first : first + wide] = ref[at]
    else:
        w_in, w_out = weights
    glu_in = jnp.dot(rows_buf[...], w_in[...], preferred_element_type=F32)
    glu_buf[...] = glu_in[:, :chans] * jax.nn.sigmoid(glu_in[:, chans:])

    def utterance(at, carry):
        start = pl.multiple_of(at * long, long)
        moved = conv_rows(glu_buf[pl.ds(start, long), :], taps) * scale + shift
        act_buf[pl.ds(start, long), :] = (moved * jax.nn.sigmoid(moved)).astype(BF16)
        return carry

    lax.fori_loop(0, chips * recv, utterance, 0)
    batch = min(chips, 4)
    for first in range(0, chips, batch):
        act = act_buf[pl.ds(first * tall, batch * tall), :]
        mixed = jnp.dot(act, w_out[...], preferred_element_type=F32)
        mixed = mixed.reshape(batch, recv, long, width)
        for number in range(batch):
            if first + number == 0:
                own[...] = kept[...].astype(F32) + mixed[0]
            else:
                outs[first + number - 1][...] = mixed[number].astype(BF16)


def shards(
    frames, ln_gain, w_in, depth_kernel, bn_scale, bn_shift, w_out, lengths, destinations, offsets
):
    dp_count, fsdp_count = lax.axis_size("dp"), lax.axis_size("fsdp")
    devices = dp_count * fsdp_count
    chips = (fsdp_count // 2) ** 2
    planes = devices // (2 * chips)
    dp_index = lax.axis_index("dp")
    number = dp_index * fsdp_count + lax.axis_index("fsdp")
    core = number % 2
    chip = (number // 2) % chips
    plane = number // (2 * chips)
    recv = lengths.shape[2] // 3
    _, _, long, width = frames.shape
    depth = w_in.shape[0]
    chans = width // chips
    wide = 2 * chans
    count = width // wide
    taps = depth_kernel.shape[0]

    def swap(array, mask):
        return lax.ppermute(array, ("dp", "fsdp"), [(at, at ^ mask) for at in range(devices)])

    def chip_swap(arrays):
        return [arrays[0]] + [swap(arrays[mask], 2 * mask) for mask in range(1, chips)]

    def climb(array):
        pairs = [(at, (at + 2 * chips) % devices) for at in range(devices)]
        return lax.ppermute(array, ("dp", "fsdp"), pairs)

    def gated(arrays, others):
        return lax.optimization_barrier((arrays, others))[0]

    place = dp_index.astype(jnp.int32)[None]
    chip_place = chip.astype(jnp.int32)[None]
    packed = jnp.stack([lengths[0], destinations[0], offsets[0]]).reshape(-1)
    small = jnp.concatenate([depth_kernel, bn_scale[None], bn_shift[None], ln_gain[None]])

    first_out = jnp.stack([w_out[:, at : at + wide] for at in range(0, width, wide)])
    next_out = climb(first_out)

    if depth % 16 == 0:
        split = call(
            functools.partial(split_kernel, planes),
            [like(BF16, depth, wide)] * chips,
            [SMEM, VMEM],
            [VMEM] * chips,
            (chip_place, w_in),
            [like(BF16, chips, depth, wide)],
        )
    else:
        by_owner = w_in.reshape(depth, 2, planes, chips, 2 * depth).transpose(3, 0, 1, 2, 4)
        by_owner = by_owner.reshape(chips, depth, wide)
        split = [
            lax.dynamic_index_in_dim(by_owner, chip ^ mask, 0, keepdims=False)
            for mask in range(chips)
        ]
    columns = chip_swap(split)

    send = call(
        send_kernel,
        like(BF16, dp_count, long, width),
        [SMEM, SMEM, VMEM],
        VMEM,
        (place, packed, frames[0]),
    )
    arrived = lax.all_to_all(send, "dp", split_axis=0, concat_axis=0, tiled=True)
    columns = gated(columns, send)
    ring = jnp.concatenate([jnp.stack(columns), next_out])
    sources, lens, table, gain = call(
        functools.partial(table_kernel, dp_count, long, planes, chips),
        [like(jnp.int32, recv)] * 2 + [like(F32, taps + 2, chans), like(F32, 1, width)],
        [SMEM] * 3 + [VMEM],
        [SMEM, SMEM, VMEM, VMEM],
        (place, chip_place, packed, small),
    )

    pieces = [first_out, ring]
    for _ in range(planes - 2):
        pieces.append(climb(pieces[-1]))
    crossed = [swap(part, 1) for part in pieces[:-1]]
    utts = like(BF16, recv, long, width)
    kept, normed = call(
        norm_kernel,
        [utts, utts],
        [SMEM] * 2 + [VMEM] * 2,
        [VMEM, VMEM],
        (sources, lens, gain, gated(arrived, crossed)),
    )
    last = climb(gated(pieces[-1], normed)[:chips])
    normed = chip_swap([normed] * chips)
    crossed.append(swap(pieces[-1], 1))
    crossed.append(swap(gated(last, normed), 1))
    pieces = pieces + [last] + crossed

    layout = []
    for side in range(2):
        first = side * planes
        layout.append([("out", first, half) for half in range(count)])
        for step in range(planes):
            layout.append([("in", first + step, at) for at in range(chips)])
            if step + 1 < planes:
                layout[-1] += [("out", first + step + 1, half) for half in range(count)]
    ring_plane = (plane - jnp.arange(planes)) % planes
    in_rows = (ring_plane[:, None] * chips + (chip ^ jnp.arange(chips))[None, :]) * 2
    where = jnp.concatenate([in_rows, ring_plane[:, None] * 2], 1)
    where = jnp.concatenate([where + core, where + 1 - core], 0).astype(jnp.int32)
    if depth % 16:
        slabs = {
            name: part[at]
            for part, names in zip(pieces, layout)
            for at, name in enumerate(names)
        }
        sides = range(2 * planes)
        flat = jnp.stack([slabs["in", at, number] for at in sides for number in range(chips)])
        all_in = jnp.zeros_like(flat).at[where[:, :chips].reshape(-1)].set(flat)
        flat = jnp.stack(
            [
                jnp.concatenate([slabs["out", at, half] for half in range(count)], axis=1)
                for at in sides
            ]
        )
        all_out = jnp.zeros_like(flat).at[where[:, chips]].set(flat)
        pieces = [all_in.reshape(width, wide), all_out.reshape(chans, width)]
        layout = []

    tall = chips * recv * long
    partial_sums = call(
        functools.partial(main_kernel, chips, layout),
        [like(F32, recv, long, width)] + [utts] * (chips - 1),
        [SMEM] + [VMEM] * (2 + chips + len(pieces)),
        [VMEM] * chips,
        (where, kept, table, *normed, *pieces),
        [
            like(BF16, tall, width),
            like(BF16, width, wide),
            like(BF16, chans, width),
            like(F32, tall, chans),
            like(BF16, tall, chans),
        ],
        flops=6 * tall * width * chans,
    )
    own, *others = chip_swap(partial_sums)
    for part in others:
        own = own + part.astype(F32)
    live = jnp.arange(long, dtype=jnp.int32)[None, :, None] < lens[:, None, None]
    return jnp.where(live, own, 0.0).astype(BF16)[None]


def solution(mesh):
    return jax.shard_map(
        shards,
        mesh=mesh,
        in_specs=(
            P("fsdp", "dp", None, None),
            P(),
            P(("dp", "fsdp"), None),
            P(),
            P(),
            P(),
            P(("dp", "fsdp"), None),
            P("fsdp", None, None),
            P("fsdp", None, None),
            P("fsdp", None, None),
        ),
        out_specs=P("fsdp", "dp", None, None),
        check_vma=False,
    )
```

```python
import functools
import math

import jax
import jax.numpy as jnp
from jax import lax
from jax.experimental import pallas as pl
from jax.experimental.pallas import tpu as pltpu
from jax.sharding import PartitionSpec as P

QUAD = 4
SMEM = pl.BlockSpec(memory_space=pltpu.SMEM)
VMEM = pl.BlockSpec(memory_space=pltpu.VMEM)
BF16 = jnp.bfloat16
F32 = jnp.float32


def call(kernel, out_shape, in_specs, out_specs, operands, scratch=(), flops=0):
    shapes = list(operands) + list(jax.tree.leaves(out_shape)) + list(scratch)
    total = sum(math.prod(shape.shape) * shape.dtype.itemsize for shape in shapes)
    return pl.pallas_call(
        kernel,
        out_shape=out_shape,
        in_specs=in_specs,
        out_specs=out_specs,
        scratch_shapes=[pltpu.VMEM(shape.shape, shape.dtype) for shape in scratch],
        cost_estimate=pl.CostEstimate(flops=flops, bytes_accessed=total, transcendentals=0),
        compiler_params=pltpu.CompilerParams(
            vmem_limit_bytes=min(total + total // 2 + 4 * 2**20, 60 * 2**20)
        ),
    )(*operands)


def like(dtype, *shape):
    return jax.ShapeDtypeStruct(shape, dtype)


class Tables:
    def __init__(self, ref, sources):
        self.ref = ref
        self.slots = ref.shape[0] // (3 * sources)
        self.size = sources * self.slots

    def live_for(self, source, slot, target):
        at = source * self.slots + slot
        return jnp.logical_and(self.ref[self.size + at] == target, self.ref[at] > 0)

    def length(self, source, slot):
        return self.ref[source * self.slots + slot]

    def offset(self, source, slot):
        return self.ref[2 * self.size + source * self.slots + slot]


def own_columns(highs, weights, owner):
    width = weights.shape[1] // 2
    run = width // (highs * QUAD)
    parts = [
        weights[:, pl.ds(half * width + (high * QUAD + owner) * run, run)]
        for half in range(2)
        for high in range(highs)
    ]
    return jnp.concatenate(parts, axis=1)


def send_kernel(sources, place, packed, frames, *outs):
    tables = Tables(packed, sources)
    me = place[0]
    for number, out in enumerate(outs):
        for far in range(out.shape[0]):
            target = jnp.bitwise_xor(me, far * QUAD + number)
            found = jnp.int32(0)
            for slot in range(tables.slots):
                found = jnp.where(tables.live_for(me, slot, target), slot, found)
            out[far] = frames[found]


def merge_kernel(sources, place, packed, *refs):
    arrived, outs = refs[:QUAD], refs[QUAD:]
    tables = Tables(packed, sources)
    me = place[0]
    for far, out in enumerate(outs, 1):
        long = out.shape[1]
        for number, ref in enumerate(arrived):
            source = jnp.bitwise_xor(me, number)
            target = jnp.bitwise_xor(me, far * QUAD)
            start = jnp.int32(-1)
            for slot in range(tables.slots):
                hit = tables.live_for(source, slot, target)
                start = jnp.where(hit, tables.offset(source, slot), start)

            @pl.when(start >= 0)
            def _():
                out[start // long] = ref[far]


def split_kernel(highs, place, weights, *refs):
    outs, buf = refs[:-1], refs[-1]
    for owner in range(QUAD):
        buf[owner] = own_columns(highs, weights, owner)
    for number, out in enumerate(outs):
        out[...] = buf[jnp.bitwise_xor(lax.rem(place[0], QUAD), number)]


def table_kernel(source_count, long, place, packed, small, sources, lens, table, gain):
    tables = Tables(packed, source_count)
    highs = source_count // QUAD
    me = place[0]

    def look(source, carry):
        for slot in range(tables.slots):

            @pl.when(tables.live_for(source, slot, me))
            def _():
                number = tables.offset(source, slot) // long
                sources[number] = source
                lens[number] = tables.length(source, slot)

        return carry

    lax.fori_loop(0, source_count, look, 0)
    count, width = small.shape
    run = width // (highs * QUAD)
    whole = small[...]
    gain[...] = whole[count - 1 :, :]
    for owner in range(QUAD):

        @pl.when(lax.rem(me, QUAD) == owner)
        def _():
            starts = [(high * QUAD + owner) * run for high in range(highs)]
            parts = [whole[: count - 1, at : at + run] for at in starts]
            table[...] = jnp.concatenate(parts, axis=1)


def norm_kernel(place, sources, lens, gain, *refs):
    near, far, (kept, normed) = refs[:QUAD], refs[QUAD:-2], refs[-2:]
    for number in range(kept.shape[0]):
        shift = jnp.bitwise_xor(sources[number], place[0])
        for other, ref in enumerate(near):

            @pl.when(shift == other)
            def _():
                kept[number] = ref[0]

        for other, ref in enumerate(far, 1):

            @pl.when(shift // QUAD == other)
            def _():
                kept[number] = ref[number]

        wide = kept[number].astype(F32)
        mean = jnp.mean(wide, axis=1, keepdims=True)
        centred = wide - mean
        var = jnp.mean(centred * centred, axis=1, keepdims=True)
        value = centred * lax.rsqrt(var + 1e-05) * gain[...]
        steps = lax.broadcasted_iota(jnp.int32, value.shape, 0)
        normed[number] = jnp.where(steps < lens[number], value, 0.0).astype(BF16)


def conv_rows(block, taps):
    long, chans = block.shape
    count = taps.shape[0]
    front = (count - 1) // 2
    groups = long // 8
    pieces = [block[8 * at : 8 * at + 8, :] for at in range(groups)]
    total = None
    for residue in range(8):
        rows = []
        for at in range(groups + 1):
            value = None
            for step in range(-(count // 8) - 1, count // 8 + 2):
                tap = 8 * step + residue + front - 16
                source = at + step - 2
                if 0 <= tap < count and 0 <= source < groups:
                    term = pieces[source] * taps[tap : tap + 1, :]
                    value = term if value is None else value + term
            rows.append(jnp.zeros((8, chans), F32) if value is None else value)
        whole = jnp.concatenate(rows, axis=0)[residue : residue + long, :]
        total = whole if total is None else total + whole
    return total


def main_kernel(pieces, where, kept, table, *refs):
    normed, weights = refs[:QUAD], refs[QUAD : QUAD + pieces]
    own, outs = refs[QUAD + pieces], refs[QUAD + pieces + 1 : 2 * QUAD + pieces]
    rows_buf, in_buf, out_buf, glu_buf, act_buf = refs[2 * QUAD + pieces :]
    recv, long, width = kept.shape
    tall = recv * long
    chans = table.shape[1]
    taps = table[: table.shape[0] - 2, :]
    scale, shift = table[table.shape[0] - 2 : table.shape[0] - 1, :], table[table.shape[0] - 1 :, :]
    for number, ref in enumerate(normed):
        rows_buf[pl.ds(number * tall, tall), :] = ref[...].reshape(tall, width)
    if pieces == 2:
        w_in, w_out = weights
    else:
        w_in, w_out = in_buf, out_buf
        depth, wide = weights[0].shape[1:]
        for number, ref in enumerate(weights):
            for inner in range(QUAD):
                start = pl.multiple_of(where[number, inner] * depth, 16)
                in_buf[pl.ds(start, depth), :] = ref[inner]
            start = pl.multiple_of(where[number, QUAD] * depth, 16)
            for half in range(width // wide):
                out_buf[pl.ds(start, depth), half * wide : half * wide + wide] = ref[QUAD + half]
    glu_in = jnp.dot(rows_buf[...], w_in[...], preferred_element_type=F32)
    glu_buf[...] = glu_in[:, :chans] * jax.nn.sigmoid(glu_in[:, chans:])

    def utterance(at, carry):
        start = pl.multiple_of(at * long, long)
        moved = conv_rows(glu_buf[pl.ds(start, long), :], taps) * scale + shift
        act_buf[pl.ds(start, long), :] = (moved * jax.nn.sigmoid(moved)).astype(BF16)
        return carry

    lax.fori_loop(0, QUAD * recv, utterance, 0)
    mixed = jnp.dot(act_buf[...], w_out[...], preferred_element_type=F32)
    mixed = mixed.reshape(QUAD, recv, long, width)
    own[...] = kept[...].astype(F32) + mixed[0]
    for number, out in enumerate(outs, 1):
        out[...] = mixed[number].astype(BF16)


def shards(
    frames, ln_gain, w_in, depth_kernel, bn_scale, bn_shift, w_out, lengths, destinations, offsets
):
    dp_count, fsdp_count = lax.axis_size("dp"), lax.axis_size("fsdp")
    devices = dp_count * fsdp_count
    highs = dp_count // QUAD
    dp_index = lax.axis_index("dp")
    quad = dp_index % QUAD
    line = dp_index // QUAD * fsdp_count + lax.axis_index("fsdp")
    recv = lengths.shape[2] // 3
    _, _, long, width = frames.shape
    depth = w_in.shape[0]
    chans = width // QUAD
    wide = 2 * chans
    taps = depth_kernel.shape[0]

    def swap(array, high=0, quad=0, fsdp=0):
        mask = (high * QUAD + quad) * fsdp_count + fsdp
        return lax.ppermute(array, ("dp", "fsdp"), [(at, at ^ mask) for at in range(devices)])

    def quad_swap(arrays):
        return [arrays[0]] + [swap(arrays[mask], quad=mask) for mask in range(1, QUAD)]

    def gated(arrays, others):
        return lax.optimization_barrier((arrays, others))[0]

    place = dp_index.astype(jnp.int32)[None]
    packed = jnp.stack([lengths[0], destinations[0], offsets[0]]).reshape(-1)
    small = jnp.concatenate([depth_kernel, bn_scale[None], bn_shift[None], ln_gain[None]])
    bits = [1 << at for at in range((highs * fsdp_count).bit_length() - 1)]
    chip_bits = [bit for bit in reversed(bits) if 1 < bit < fsdp_count]

    if depth % 16 == 0:
        split = call(
            functools.partial(split_kernel, highs),
            [like(BF16, depth, wide)] * QUAD,
            [SMEM, VMEM],
            [VMEM] * QUAD,
            (place, w_in),
            [like(BF16, QUAD, depth, wide)],
        )
    else:
        by_owner = w_in.reshape(depth, 2, highs, QUAD, chans // highs).transpose(3, 0, 1, 2, 4)
        by_owner = by_owner.reshape(QUAD, depth, wide)
        split = [
            lax.dynamic_index_in_dim(by_owner, quad ^ mask, 0, keepdims=False)
            for mask in range(QUAD)
        ]
    columns = quad_swap(split)

    near = call(
        functools.partial(send_kernel, dp_count),
        [like(BF16, highs, long, width)] * QUAD,
        [SMEM, SMEM, VMEM],
        [VMEM] * QUAD,
        (place, packed, frames[0]),
    )
    near = quad_swap(near)
    columns = gated(columns, near[1])
    sources, lens, table, gain = call(
        functools.partial(table_kernel, dp_count, long),
        [like(jnp.int32, recv)] * 2 + [like(F32, taps + 2, chans), like(F32, 1, width)],
        [SMEM] * 2 + [VMEM],
        [SMEM, SMEM, VMEM, VMEM],
        (place, packed, small),
    )
    utts = like(BF16, recv, long, width)
    far = call(
        functools.partial(merge_kernel, dp_count),
        [utts] * (highs - 1),
        [SMEM] * 2 + [VMEM] * QUAD,
        [VMEM] * (highs - 1),
        (gated(place, (lens, gain)), packed, *near),
    )
    far = [swap(part, high=mask) for mask, part in enumerate(far, 1)]

    halves = [w_out[:, at : at + wide] for at in range(0, width, wide)]
    pieces = [jnp.stack(columns + halves)]
    shifts = [mask * fsdp_count for mask in range(highs)]
    pieces += gated([swap(pieces[0], high=mask) for mask in range(1, highs)], far)
    chip_first = [swap(pieces[0], fsdp=bit) for bit in chip_bits[:1]]
    early = [swap(part, fsdp=1) for part in pieces[:1] + chip_first]
    far = gated(far, early)
    kept, normed = call(
        norm_kernel,
        [utts, utts],
        [SMEM] * 3 + [VMEM] * (QUAD + highs),
        [VMEM, VMEM],
        (place, sources, lens, gain, *near, *far),
    )
    for bit in chip_bits:
        first = chip_first if bit == chip_bits[0] else []
        pieces = pieces + first + [swap(part, fsdp=bit) for part in pieces[len(first) :]]
        shifts = shifts + [shift ^ bit for shift in shifts]
    normed = quad_swap([normed] * QUAD)
    ends = len(shifts) // 2 + 1
    pieces[ends:] = gated(pieces[ends:], normed)
    cored = [swap(part, fsdp=1) for part in pieces]
    cored[0], cored[len(shifts) // 2] = early[0], early[-1]
    pieces = pieces + cored
    shifts = shifts + [shift ^ 1 for shift in shifts]

    out_rows = line ^ jnp.array(shifts)
    in_rows = out_rows // fsdp_count * QUAD
    in_rows = in_rows[:, None] + (quad ^ jnp.arange(QUAD))[None, :]
    in_rows = in_rows * fsdp_count + (out_rows % fsdp_count)[:, None]
    where = jnp.concatenate([in_rows, out_rows[:, None]], 1).astype(jnp.int32)
    if depth % 16:
        together = jnp.stack(pieces)
        flat = together[:, :QUAD].reshape(-1, depth, wide)
        all_in = jnp.zeros_like(flat).at[where[:, :QUAD].reshape(-1)].set(flat)
        flat = together[:, QUAD:].transpose(0, 2, 1, 3).reshape(-1, depth, width)
        all_out = jnp.zeros_like(flat).at[where[:, QUAD]].set(flat)
        pieces = [all_in.reshape(width, wide), all_out.reshape(chans, width)]

    tall = QUAD * recv * long
    partial_sums = call(
        functools.partial(main_kernel, len(pieces)),
        [like(F32, recv, long, width)] + [utts] * (QUAD - 1),
        [SMEM] + [VMEM] * (2 + QUAD + len(pieces)),
        [VMEM] * QUAD,
        (where, kept, table, *normed, *pieces),
        [
            like(BF16, tall, width),
            like(BF16, width, wide),
            like(BF16, chans, width),
            like(F32, tall, chans),
            like(BF16, tall, chans),
        ],
        flops=6 * tall * width * chans,
    )
    own, *others = quad_swap(partial_sums)
    for part in others:
        own = own + part.astype(F32)
    live = jnp.arange(long, dtype=jnp.int32)[None, :, None] < lens[:, None, None]
    return jnp.where(live, own, 0.0).astype(BF16)[None]


def solution(mesh):
    return jax.shard_map(
        shards,
        mesh=mesh,
        in_specs=(
            P("fsdp", "dp", None, None),
            P(),
            P(("dp", "fsdp"), None),
            P(),
            P(),
            P(),
            P(("dp", "fsdp"), None),
            P("fsdp", None, None),
            P("fsdp", None, None),
            P("fsdp", None, None),
        ),
        out_specs=P("fsdp", "dp", None, None),
        check_vma=False,
    )
```

```python
import functools
import math

import jax
import jax.numpy as jnp
from jax import lax
from jax.experimental import pallas as pl
from jax.experimental.pallas import tpu as pltpu
from jax.sharding import PartitionSpec as P

QUAD = 4
SMEM = pl.BlockSpec(memory_space=pltpu.SMEM)
VMEM = pl.BlockSpec(memory_space=pltpu.VMEM)
BF16 = jnp.bfloat16
F32 = jnp.float32


def call(kernel, out_shape, in_specs, out_specs, operands, scratch=(), flops=0):
    shapes = list(operands) + list(jax.tree.leaves(out_shape)) + list(scratch)
    total = sum(math.prod(shape.shape) * shape.dtype.itemsize for shape in shapes)
    return pl.pallas_call(
        kernel,
        out_shape=out_shape,
        in_specs=in_specs,
        out_specs=out_specs,
        scratch_shapes=[pltpu.VMEM(shape.shape, shape.dtype) for shape in scratch],
        cost_estimate=pl.CostEstimate(flops=flops, bytes_accessed=total, transcendentals=0),
        compiler_params=pltpu.CompilerParams(
            vmem_limit_bytes=min(total + total // 2 + 4 * 2**20, 60 * 2**20)
        ),
    )(*operands)


def like(dtype, *shape):
    return jax.ShapeDtypeStruct(shape, dtype)


class Tables:
    def __init__(self, ref, sources):
        self.ref = ref
        self.slots = ref.shape[0] // (3 * sources)
        self.size = sources * self.slots

    def live_for(self, source, slot, target):
        at = source * self.slots + slot
        return jnp.logical_and(self.ref[self.size + at] == target, self.ref[at] > 0)

    def length(self, source, slot):
        return self.ref[source * self.slots + slot]

    def offset(self, source, slot):
        return self.ref[2 * self.size + source * self.slots + slot]


def own_columns(highs, weights, owner):
    width = weights.shape[1] // 2
    run = width // (highs * QUAD)
    parts = [
        weights[:, pl.ds(half * width + (high * QUAD + owner) * run, run)]
        for half in range(2)
        for high in range(highs)
    ]
    return jnp.concatenate(parts, axis=1)


def send_kernel(sources, place, packed, weights, frames, *refs):
    outs, buf = refs[:-1], refs[-1]
    tables = Tables(packed, sources)
    me = place[0]
    highs = sources // QUAD
    long, width = frames.shape[1:]
    wide = outs[0].shape[1]
    for owner in range(QUAD):
        buf[owner] = own_columns(highs, weights, owner)
    for number, out in enumerate(outs):
        for far in range(highs):
            target = jnp.bitwise_xor(me, far * QUAD + number)
            found = jnp.int32(0)
            for slot in range(tables.slots):
                found = jnp.where(tables.live_for(me, slot, target), slot, found)
            for half in range(width // wide):
                start = (far * (width // wide) + half) * long
                out[start : start + long, :] = frames[found, :, half * wide : half * wide + wide]
        start = highs * (width // wide) * long
        out[start:, :] = buf[jnp.bitwise_xor(lax.rem(me, QUAD), number)]


def fetch(out, number, ref, far):
    long, width = out.shape[1:]
    wide = ref.shape[1]
    for half in range(width // wide):
        start = (far * (width // wide) + half) * long
        out[number, :, half * wide : half * wide + wide] = ref[start : start + long, :]


def merge_kernel(sources, place, packed, *refs):
    arrived, outs, piece = refs[:QUAD], refs[QUAD:-1], refs[-1]
    tables = Tables(packed, sources)
    me = place[0]
    depth, wide = piece.shape[1:]
    for far, out in enumerate(outs, 1):
        long = out.shape[1]
        for number, ref in enumerate(arrived):
            source = jnp.bitwise_xor(me, number)
            target = jnp.bitwise_xor(me, far * QUAD)
            start = jnp.int32(-1)
            for slot in range(tables.slots):
                hit = tables.live_for(source, slot, target)
                start = jnp.where(hit, tables.offset(source, slot), start)

            @pl.when(start >= 0)
            def _():
                fetch(out, start // long, ref, far)

    for number, ref in enumerate(arrived):
        piece[number] = ref[ref.shape[0] - depth :, :]


def stack_kernel(*refs):
    parts, out = refs[:-1], refs[-1]
    wide = out.shape[2]
    at = 0
    for ref in parts:
        if len(ref.shape) == 3:
            out[at : at + ref.shape[0]] = ref[...]
            at += ref.shape[0]
        else:
            for first in range(0, ref.shape[1], wide):
                out[at] = ref[:, first : first + wide]
                at += 1


def table_kernel(source_count, long, place, packed, small, sources, lens, table, gain):
    tables = Tables(packed, source_count)
    highs = source_count // QUAD
    me = place[0]

    def look(source, carry):
        for slot in range(tables.slots):

            @pl.when(tables.live_for(source, slot, me))
            def _():
                number = tables.offset(source, slot) // long
                sources[number] = source
                lens[number] = tables.length(source, slot)

        return carry

    lax.fori_loop(0, source_count, look, 0)
    count, width = small.shape
    run = width // (highs * QUAD)
    whole = small[...]
    gain[...] = whole[count - 1 :, :]
    for owner in range(QUAD):

        @pl.when(lax.rem(me, QUAD) == owner)
        def _():
            starts = [(high * QUAD + owner) * run for high in range(highs)]
            parts = [whole[: count - 1, at : at + run] for at in starts]
            table[...] = jnp.concatenate(parts, axis=1)


def norm_kernel(place, sources, lens, gain, *refs):
    near, far, (kept, normed) = refs[:QUAD], refs[QUAD:-2], refs[-2:]
    for number in range(kept.shape[0]):
        shift = jnp.bitwise_xor(sources[number], place[0])
        for other, ref in enumerate(near):

            @pl.when(shift == other)
            def _():
                fetch(kept, number, ref, 0)

        for other, ref in enumerate(far, 1):

            @pl.when(shift // QUAD == other)
            def _():
                kept[number] = ref[number]

        wide = kept[number].astype(F32)
        mean = jnp.mean(wide, axis=1, keepdims=True)
        centred = wide - mean
        var = jnp.mean(centred * centred, axis=1, keepdims=True)
        value = centred * lax.rsqrt(var + 1e-05) * gain[...]
        steps = lax.broadcasted_iota(jnp.int32, value.shape, 0)
        normed[number] = jnp.where(steps < lens[number], value, 0.0).astype(BF16)


def conv_rows(block, taps):
    long, chans = block.shape
    count = taps.shape[0]
    front = (count - 1) // 2
    groups = long // 8
    pieces = [block[8 * at : 8 * at + 8, :] for at in range(groups)]
    total = None
    for residue in range(8):
        rows = []
        for at in range(groups + 1):
            value = None
            for step in range(-(count // 8) - 1, count // 8 + 2):
                tap = 8 * step + residue + front - 16
                source = at + step - 2
                if 0 <= tap < count and 0 <= source < groups:
                    term = pieces[source] * taps[tap : tap + 1, :]
                    value = term if value is None else value + term
            rows.append(jnp.zeros((8, chans), F32) if value is None else value)
        whole = jnp.concatenate(rows, axis=0)[residue : residue + long, :]
        total = whole if total is None else total + whole
    return total


def main_kernel(layout, where, kept, table, *refs):
    pieces = max(len(layout), 2)
    chans = table.shape[1]
    taps = table[: table.shape[0] - 2, :]
    scale, shift = table[table.shape[0] - 2 : table.shape[0] - 1, :], table[table.shape[0] - 1 :, :]
    normed, weights = refs[:QUAD], refs[QUAD : QUAD + pieces]
    own, outs = refs[QUAD + pieces], refs[QUAD + pieces + 1 : 2 * QUAD + pieces]
    rows_buf, in_buf, out_buf, glu_buf, act_buf = refs[2 * QUAD + pieces :]
    recv, long, width = kept.shape
    tall = recv * long
    for number, ref in enumerate(normed):
        rows_buf[pl.ds(number * tall, tall), :] = ref[...].reshape(tall, width)
    if layout:
        w_in, w_out = in_buf, out_buf
        depth, wide = weights[0].shape[1:]
        for ref, slabs in zip(weights, layout):
            for at, (kind, other, number) in enumerate(slabs):
                if kind == "in":
                    start = pl.multiple_of(where[other, number] * depth, 16)
                    in_buf[pl.ds(start, depth), :] = ref[at]
                else:
                    start = pl.multiple_of(where[other, QUAD] * depth, 16)
                    first = number * wide
                    out_buf[pl.ds(start, depth), first : first + wide] = ref[at]
    else:
        w_in, w_out = weights
    glu_in = jnp.dot(rows_buf[...], w_in[...], preferred_element_type=F32)
    glu_buf[...] = glu_in[:, :chans] * jax.nn.sigmoid(glu_in[:, chans:])

    def utterance(at, carry):
        start = pl.multiple_of(at * long, long)
        moved = conv_rows(glu_buf[pl.ds(start, long), :], taps) * scale + shift
        act_buf[pl.ds(start, long), :] = (moved * jax.nn.sigmoid(moved)).astype(BF16)
        return carry

    lax.fori_loop(0, QUAD * recv, utterance, 0)
    mixed = jnp.dot(act_buf[...], w_out[...], preferred_element_type=F32)
    mixed = mixed.reshape(QUAD, recv, long, width)
    own[...] = kept[...].astype(F32) + mixed[0]
    for number, out in enumerate(outs, 1):
        out[...] = mixed[number].astype(BF16)


def shards(
    frames, ln_gain, w_in, depth_kernel, bn_scale, bn_shift, w_out, lengths, destinations, offsets
):
    dp_count, fsdp_count = lax.axis_size("dp"), lax.axis_size("fsdp")
    devices = dp_count * fsdp_count
    highs = dp_count // QUAD
    dp_index = lax.axis_index("dp")
    quad = dp_index % QUAD
    line = dp_index // QUAD * fsdp_count + lax.axis_index("fsdp")
    recv = lengths.shape[2] // 3
    _, _, long, width = frames.shape
    depth = w_in.shape[0]
    chans = width // QUAD
    wide = 2 * chans
    taps = depth_kernel.shape[0]

    def swap(array, high=0, quad=0, fsdp=0):
        mask = (high * QUAD + quad) * fsdp_count + fsdp
        return lax.ppermute(array, ("dp", "fsdp"), [(at, at ^ mask) for at in range(devices)])

    def quad_swap(arrays):
        return [arrays[0]] + [swap(arrays[mask], quad=mask) for mask in range(1, QUAD)]

    def gated(arrays, others):
        return lax.optimization_barrier((arrays, others))[0]

    place = dp_index.astype(jnp.int32)[None]
    packed = jnp.stack([lengths[0], destinations[0], offsets[0]]).reshape(-1)
    small = jnp.concatenate([depth_kernel, bn_scale[None], bn_shift[None], ln_gain[None]])
    bits = [1 << at for at in range((highs * fsdp_count).bit_length() - 1)]
    chip_bits = [bit for bit in reversed(bits) if 1 < bit < fsdp_count]

    count = width // wide

    outs = {0: w_out}

    def share_chips(parts, first):
        for bit in chip_bits:
            for shift in [shift for shift in parts if (shift >= fsdp_count) == first]:
                parts[shift ^ bit] = swap(parts[shift], fsdp=bit)

    for mask in range(1, highs):
        outs[mask * fsdp_count] = swap(w_out, high=mask)
    share_chips(outs, False)

    near = call(
        functools.partial(send_kernel, dp_count),
        [like(BF16, highs * count * long + depth, wide)] * QUAD,
        [SMEM, SMEM, VMEM, VMEM],
        [VMEM] * QUAD,
        (place, packed, w_in, frames[0]),
        [like(BF16, QUAD, depth, wide)],
    )
    near = quad_swap(near)
    sources, lens, table, gain = call(
        functools.partial(table_kernel, dp_count, long),
        [like(jnp.int32, recv)] * 2 + [like(F32, taps + 2, chans), like(F32, 1, width)],
        [SMEM] * 2 + [VMEM],
        [SMEM, SMEM, VMEM, VMEM],
        (place, packed, small),
    )
    utts = like(BF16, recv, long, width)
    *far, own_in = call(
        functools.partial(merge_kernel, dp_count),
        [utts] * (highs - 1) + [like(BF16, QUAD, depth, wide)],
        [SMEM] * 2 + [VMEM] * QUAD,
        [VMEM] * highs,
        (gated(place, (lens, gain, outs)), packed, *near),
    )
    far = [swap(part, high=mask) for mask, part in enumerate(far, 1)]

    ins = {0: own_in}
    far_in = [swap(own_in, high=mask) for mask in range(1, highs)]
    share_chips(ins, False)
    early = list(ins)
    share_chips(outs, True)
    order = sorted(outs)
    stacked = call(
        stack_kernel,
        like(BF16, len(order) * count, depth, wide),
        [VMEM] * len(order),
        VMEM,
        [outs[shift] for shift in order],
    )
    crossed = {shift: swap(ins[shift], fsdp=1) for shift in early}
    crossed_out = swap(stacked, fsdp=1)
    for mask, part in enumerate(gated(far_in, far), 1):
        ins[mask * fsdp_count] = part
    kept, normed = call(
        norm_kernel,
        [utts, utts],
        [SMEM] * 3 + [VMEM] * (QUAD + highs),
        [VMEM, VMEM],
        (place, sources, lens, gain, *near, *gated(far, (crossed, crossed_out))),
    )
    share_chips(ins, True)
    normed = quad_swap([normed] * QUAD)
    chip_mask = (fsdp_count - 1) ^ 1
    last = {at: ins[at] for at in ins if at & chip_mask and at not in early}
    last = gated(last, normed)
    for shift in ins:
        if shift not in crossed:
            crossed[shift] = swap(last.get(shift, ins[shift]), fsdp=1)
    pieces = list(ins.values()) + [stacked]
    layout = [[("in", shift, number) for number in range(QUAD)] for shift in ins]
    layout.append([("out", shift, half) for shift in order for half in range(count)])
    pieces += [crossed[shift] for shift in ins] + [crossed_out]
    layout += [[(kind, shift ^ 1, at) for kind, shift, at in slabs] for slabs in layout]

    out_rows = line ^ jnp.arange(highs * fsdp_count)
    in_rows = out_rows // fsdp_count * QUAD
    in_rows = in_rows[:, None] + (quad ^ jnp.arange(QUAD))[None, :]
    in_rows = in_rows * fsdp_count + (out_rows % fsdp_count)[:, None]
    where = jnp.concatenate([in_rows, out_rows[:, None]], 1).astype(jnp.int32)
    if depth % 16:
        slabs = {
            name: part[at]
            for part, names in zip(pieces, layout)
            for at, name in enumerate(names)
        }
        sides = range(highs * fsdp_count)
        flat = jnp.stack([slabs["in", at, number] for at in sides for number in range(QUAD)])
        all_in = jnp.zeros_like(flat).at[where[:, :QUAD].reshape(-1)].set(flat)
        flat = jnp.stack(
            [
                jnp.concatenate([slabs["out", at, half] for half in range(count)], axis=1)
                for at in sides
            ]
        )
        all_out = jnp.zeros_like(flat).at[where[:, QUAD]].set(flat)
        pieces = [all_in.reshape(width, wide), all_out.reshape(chans, width)]
        layout = []

    tall = QUAD * recv * long
    partial_sums = call(
        functools.partial(main_kernel, layout),
        [like(F32, recv, long, width)] + [utts] * (QUAD - 1),
        [SMEM] + [VMEM] * (2 + QUAD + len(pieces)),
        [VMEM] * QUAD,
        (where, kept, table, *normed, *pieces),
        [
            like(BF16, tall, width),
            like(BF16, width, wide),
            like(BF16, chans, width),
            like(F32, tall, chans),
            like(BF16, tall, chans),
        ],
        flops=6 * tall * width * chans,
    )
    own, *others = quad_swap(partial_sums)
    for part in others:
        own = own + part.astype(F32)
    live = jnp.arange(long, dtype=jnp.int32)[None, :, None] < lens[:, None, None]
    return jnp.where(live, own, 0.0).astype(BF16)[None]


def solution(mesh):
    return jax.shard_map(
        shards,
        mesh=mesh,
        in_specs=(
            P("fsdp", "dp", None, None),
            P(),
            P(("dp", "fsdp"), None),
            P(),
            P(),
            P(),
            P(("dp", "fsdp"), None),
            P("fsdp", None, None),
            P("fsdp", None, None),
            P("fsdp", None, None),
        ),
        out_specs=P("fsdp", "dp", None, None),
        check_vma=False,
    )
```

```python
import functools
import math

import jax
import jax.numpy as jnp
from jax import lax
from jax.experimental import pallas as pl
from jax.experimental.pallas import tpu as pltpu
from jax.sharding import PartitionSpec as P

QUAD = 4
SMEM = pl.BlockSpec(memory_space=pltpu.SMEM)
VMEM = pl.BlockSpec(memory_space=pltpu.VMEM)
BF16 = jnp.bfloat16
F32 = jnp.float32


def call(kernel, out_shape, in_specs, out_specs, operands, scratch=(), flops=0):
    shapes = list(operands) + list(jax.tree.leaves(out_shape)) + list(scratch)
    total = sum(math.prod(shape.shape) * shape.dtype.itemsize for shape in shapes)
    return pl.pallas_call(
        kernel,
        out_shape=out_shape,
        in_specs=in_specs,
        out_specs=out_specs,
        scratch_shapes=[pltpu.VMEM(shape.shape, shape.dtype) for shape in scratch],
        cost_estimate=pl.CostEstimate(flops=flops, bytes_accessed=total, transcendentals=0),
        compiler_params=pltpu.CompilerParams(
            vmem_limit_bytes=min(total + total // 2 + 4 * 2**20, 60 * 2**20)
        ),
    )(*operands)


def like(dtype, *shape):
    return jax.ShapeDtypeStruct(shape, dtype)


class Tables:
    def __init__(self, ref, sources):
        self.ref = ref
        self.slots = ref.shape[0] // (3 * sources)
        self.size = sources * self.slots

    def live_for(self, source, slot, target):
        at = source * self.slots + slot
        return jnp.logical_and(self.ref[self.size + at] == target, self.ref[at] > 0)

    def length(self, source, slot):
        return self.ref[source * self.slots + slot]

    def offset(self, source, slot):
        return self.ref[2 * self.size + source * self.slots + slot]


def own_columns(highs, weights, owner):
    width = weights.shape[1] // 2
    run = width // (highs * QUAD)
    parts = [
        weights[:, pl.ds(half * width + (high * QUAD + owner) * run, run)]
        for half in range(2)
        for high in range(highs)
    ]
    return jnp.concatenate(parts, axis=1)


def send_kernel(sources, place, packed, weights, frames, *refs):
    near, far, buf = refs[:QUAD], refs[QUAD:-1], refs[-1]
    tables = Tables(packed, sources)
    me = place[0]
    highs = sources // QUAD
    long, width = frames.shape[1:]
    wide = near[0].shape[1]
    for owner in range(QUAD):
        buf[owner] = own_columns(highs, weights, owner)
    for shift, out in enumerate(near + far):
        target = jnp.bitwise_xor(me, shift)
        found = jnp.int32(0)
        for slot in range(tables.slots):
            found = jnp.where(tables.live_for(me, slot, target), slot, found)
        if shift >= QUAD:
            out[...] = frames[found]
        else:
            for half in range(width // wide):
                first = half * wide
                out[half * long : (half + 1) * long, :] = frames[found, :, first : first + wide]
            out[width // wide * long :, :] = buf[jnp.bitwise_xor(lax.rem(me, QUAD), shift)]


def columns_kernel(*refs):
    arrived, piece = refs[:-1], refs[-1]
    for number, ref in enumerate(arrived):
        piece[number] = ref[ref.shape[0] - piece.shape[1] :, :]


def stack_kernel(*refs):
    parts, out = refs[:-1], refs[-1]
    wide = out.shape[2]
    at = 0
    for ref in parts:
        if len(ref.shape) == 3:
            out[at : at + ref.shape[0]] = ref[...]
            at += ref.shape[0]
        else:
            for first in range(0, ref.shape[1], wide):
                out[at] = ref[:, first : first + wide]
                at += 1


def table_kernel(source_count, long, place, packed, small, sources, lens, table, gain):
    tables = Tables(packed, source_count)
    highs = source_count // QUAD
    me = place[0]

    def look(source, carry):
        for slot in range(tables.slots):

            @pl.when(tables.live_for(source, slot, me))
            def _():
                number = tables.offset(source, slot) // long
                sources[number] = source
                lens[number] = tables.length(source, slot)

        return carry

    lax.fori_loop(0, source_count, look, 0)
    count, width = small.shape
    run = width // (highs * QUAD)
    whole = small[...]
    gain[...] = whole[count - 1 :, :]
    for owner in range(QUAD):

        @pl.when(lax.rem(me, QUAD) == owner)
        def _():
            starts = [(high * QUAD + owner) * run for high in range(highs)]
            parts = [whole[: count - 1, at : at + run] for at in starts]
            table[...] = jnp.concatenate(parts, axis=1)


def norm_kernel(place, sources, lens, gain, *refs):
    arrived, (kept, normed) = refs[:-2], refs[-2:]
    long, width = kept.shape[1:]
    for number in range(kept.shape[0]):
        shift = jnp.bitwise_xor(sources[number], place[0])
        for other, ref in enumerate(arrived):

            @pl.when(shift == other)
            def _():
                if other >= QUAD:
                    kept[number] = ref[...]
                else:
                    wide = ref.shape[1]
                    for half in range(width // wide):
                        rows = ref[half * long : (half + 1) * long, :]
                        kept[number, :, half * wide : (half + 1) * wide] = rows

        wide = kept[number].astype(F32)
        mean = jnp.mean(wide, axis=1, keepdims=True)
        centred = wide - mean
        var = jnp.mean(centred * centred, axis=1, keepdims=True)
        value = centred * lax.rsqrt(var + 1e-05) * gain[...]
        steps = lax.broadcasted_iota(jnp.int32, value.shape, 0)
        normed[number] = jnp.where(steps < lens[number], value, 0.0).astype(BF16)


def conv_rows(block, taps):
    long, chans = block.shape
    count = taps.shape[0]
    front = (count - 1) // 2
    groups = long // 8
    pieces = [block[8 * at : 8 * at + 8, :] for at in range(groups)]
    total = None
    for residue in range(8):
        rows = []
        for at in range(groups + 1):
            value = None
            for step in range(-(count // 8) - 1, count // 8 + 2):
                tap = 8 * step + residue + front - 16
                source = at + step - 2
                if 0 <= tap < count and 0 <= source < groups:
                    term = pieces[source] * taps[tap : tap + 1, :]
                    value = term if value is None else value + term
            rows.append(jnp.zeros((8, chans), F32) if value is None else value)
        whole = jnp.concatenate(rows, axis=0)[residue : residue + long, :]
        total = whole if total is None else total + whole
    return total


def main_kernel(layout, where, kept, table, *refs):
    pieces = max(len(layout), 2)
    chans = table.shape[1]
    taps = table[: table.shape[0] - 2, :]
    scale, shift = table[table.shape[0] - 2 : table.shape[0] - 1, :], table[table.shape[0] - 1 :, :]
    normed, weights = refs[:QUAD], refs[QUAD : QUAD + pieces]
    own, outs = refs[QUAD + pieces], refs[QUAD + pieces + 1 : 2 * QUAD + pieces]
    rows_buf, in_buf, out_buf, glu_buf, act_buf = refs[2 * QUAD + pieces :]
    recv, long, width = kept.shape
    tall = recv * long
    for number, ref in enumerate(normed):
        rows_buf[pl.ds(number * tall, tall), :] = ref[...].reshape(tall, width)
    if layout:
        w_in, w_out = in_buf, out_buf
        depth, wide = weights[0].shape[1:]
        for ref, slabs in zip(weights, layout):
            for at, (kind, other, number) in enumerate(slabs):
                if kind == "in":
                    start = pl.multiple_of(where[other, number] * depth, 16)
                    in_buf[pl.ds(start, depth), :] = ref[at]
                else:
                    start = pl.multiple_of(where[other, QUAD] * depth, 16)
                    first = number * wide
                    out_buf[pl.ds(start, depth), first : first + wide] = ref[at]
    else:
        w_in, w_out = weights
    glu_in = jnp.dot(rows_buf[...], w_in[...], preferred_element_type=F32)
    glu_buf[...] = glu_in[:, :chans] * jax.nn.sigmoid(glu_in[:, chans:])

    def utterance(at, carry):
        start = pl.multiple_of(at * long, long)
        moved = conv_rows(glu_buf[pl.ds(start, long), :], taps) * scale + shift
        act_buf[pl.ds(start, long), :] = (moved * jax.nn.sigmoid(moved)).astype(BF16)
        return carry

    lax.fori_loop(0, QUAD * recv, utterance, 0)
    mixed = jnp.dot(act_buf[...], w_out[...], preferred_element_type=F32)
    mixed = mixed.reshape(QUAD, recv, long, width)
    own[...] = kept[...].astype(F32) + mixed[0]
    for number, out in enumerate(outs, 1):
        out[...] = mixed[number].astype(BF16)


def shards(
    frames, ln_gain, w_in, depth_kernel, bn_scale, bn_shift, w_out, lengths, destinations, offsets
):
    dp_count, fsdp_count = lax.axis_size("dp"), lax.axis_size("fsdp")
    devices = dp_count * fsdp_count
    highs = dp_count // QUAD
    dp_index = lax.axis_index("dp")
    quad = dp_index % QUAD
    line = dp_index // QUAD * fsdp_count + lax.axis_index("fsdp")
    recv = lengths.shape[2] // 3
    _, _, long, width = frames.shape
    depth = w_in.shape[0]
    chans = width // QUAD
    wide = 2 * chans
    taps = depth_kernel.shape[0]

    def swap(array, high=0, quad=0, fsdp=0):
        mask = (high * QUAD + quad) * fsdp_count + fsdp
        return lax.ppermute(array, ("dp", "fsdp"), [(at, at ^ mask) for at in range(devices)])

    def quad_swap(arrays):
        return [arrays[0]] + [swap(arrays[mask], quad=mask) for mask in range(1, QUAD)]

    def gated(arrays, others):
        return lax.optimization_barrier((arrays, others))[0]

    place = dp_index.astype(jnp.int32)[None]
    packed = jnp.stack([lengths[0], destinations[0], offsets[0]]).reshape(-1)
    small = jnp.concatenate([depth_kernel, bn_scale[None], bn_shift[None], ln_gain[None]])
    bits = [1 << at for at in range((highs * fsdp_count).bit_length() - 1)]
    chip_bits = [bit for bit in reversed(bits) if 1 < bit < fsdp_count]

    count = width // wide

    sent = call(
        functools.partial(send_kernel, dp_count),
        [like(BF16, count * long + depth, wide)] * QUAD
        + [like(BF16, long, width)] * (dp_count - QUAD),
        [SMEM, SMEM, VMEM, VMEM],
        [VMEM] * dp_count,
        (place, packed, w_in, frames[0]),
        [like(BF16, QUAD, depth, wide)],
    )
    sent = list(sent)
    near = quad_swap(sent[:QUAD])
    later = QUAD + 2
    sent[later:] = gated(sent[later:], near[1])
    far = [
        swap(sent[shift], high=shift // QUAD, quad=shift % QUAD)
        for shift in range(QUAD, dp_count)
    ]

    w_out = gated(w_out, sent[:later])
    outs = {0: w_out}

    def share_chips(parts, first):
        for bit in chip_bits:
            for shift in [shift for shift in parts if (shift >= fsdp_count) == first]:
                parts[shift ^ bit] = swap(parts[shift], fsdp=bit)

    for mask in range(1, highs):
        outs[mask * fsdp_count] = swap(w_out, high=mask)
    share_chips(outs, False)
    share_chips(outs, True)
    sources, lens, table, gain = call(
        functools.partial(table_kernel, dp_count, long),
        [like(jnp.int32, recv)] * 2 + [like(F32, taps + 2, chans), like(F32, 1, width)],
        [SMEM] * 2 + [VMEM],
        [SMEM, SMEM, VMEM, VMEM],
        (place, packed, small),
    )

    own_in = call(
        columns_kernel,
        like(BF16, QUAD, depth, wide),
        [VMEM] * QUAD,
        VMEM,
        gated(near, (lens, gain)),
    )
    ins = {0: own_in}
    for mask in range(1, highs):
        ins[mask * fsdp_count] = swap(gated(own_in, far), high=mask)
    share_chips(ins, False)
    early = [shift for shift in ins if shift < fsdp_count]
    order = sorted(outs)
    stacked = call(
        stack_kernel,
        like(BF16, len(order) * count, depth, wide),
        [VMEM] * len(order),
        VMEM,
        [outs[shift] for shift in order],
    )
    crossed = {shift: swap(ins[shift], fsdp=1) for shift in early}
    crossed_out = swap(stacked, fsdp=1)
    utts = like(BF16, recv, long, width)
    kept, normed = call(
        norm_kernel,
        [utts, utts],
        [SMEM] * 3 + [VMEM] * (1 + dp_count),
        [VMEM, VMEM],
        (place, sources, lens, gain, *near, *gated(far, crossed)),
    )
    for shift in ins:
        if shift not in early:
            ins[shift] = gated(ins[shift], normed)
    share_chips(ins, True)
    normed = quad_swap([normed] * QUAD)
    chip_mask = (fsdp_count - 1) ^ 1
    last = {at: ins[at] for at in ins if at & chip_mask and at not in early}
    for shift in ins:
        if shift not in crossed and shift not in last:
            crossed[shift] = swap(ins[shift], fsdp=1)
    for shift, part in gated(last, (normed, crossed, crossed_out)).items():
        crossed[shift] = swap(part, fsdp=1)
    pieces = list(ins.values()) + [stacked]
    layout = [[("in", shift, number) for number in range(QUAD)] for shift in ins]
    layout.append([("out", shift, half) for shift in order for half in range(count)])
    pieces += [crossed[shift] for shift in ins] + [crossed_out]
    layout += [[(kind, shift ^ 1, at) for kind, shift, at in slabs] for slabs in layout]

    out_rows = line ^ jnp.arange(highs * fsdp_count)
    in_rows = out_rows // fsdp_count * QUAD
    in_rows = in_rows[:, None] + (quad ^ jnp.arange(QUAD))[None, :]
    in_rows = in_rows * fsdp_count + (out_rows % fsdp_count)[:, None]
    where = jnp.concatenate([in_rows, out_rows[:, None]], 1).astype(jnp.int32)
    if depth % 16:
        slabs = {
            name: part[at]
            for part, names in zip(pieces, layout)
            for at, name in enumerate(names)
        }
        sides = range(highs * fsdp_count)
        flat = jnp.stack([slabs["in", at, number] for at in sides for number in range(QUAD)])
        all_in = jnp.zeros_like(flat).at[where[:, :QUAD].reshape(-1)].set(flat)
        flat = jnp.stack(
            [
                jnp.concatenate([slabs["out", at, half] for half in range(count)], axis=1)
                for at in sides
            ]
        )
        all_out = jnp.zeros_like(flat).at[where[:, QUAD]].set(flat)
        pieces = [all_in.reshape(width, wide), all_out.reshape(chans, width)]
        layout = []

    tall = QUAD * recv * long
    partial_sums = call(
        functools.partial(main_kernel, layout),
        [like(F32, recv, long, width)] + [utts] * (QUAD - 1),
        [SMEM] + [VMEM] * (2 + QUAD + len(pieces)),
        [VMEM] * QUAD,
        (where, kept, table, *normed, *pieces),
        [
            like(BF16, tall, width),
            like(BF16, width, wide),
            like(BF16, chans, width),
            like(F32, tall, chans),
            like(BF16, tall, chans),
        ],
        flops=6 * tall * width * chans,
    )
    own, *others = quad_swap(partial_sums)
    for part in others:
        own = own + part.astype(F32)
    live = jnp.arange(long, dtype=jnp.int32)[None, :, None] < lens[:, None, None]
    return jnp.where(live, own, 0.0).astype(BF16)[None]


def solution(mesh):
    return jax.shard_map(
        shards,
        mesh=mesh,
        in_specs=(
            P("fsdp", "dp", None, None),
            P(),
            P(("dp", "fsdp"), None),
            P(),
            P(),
            P(),
            P(("dp", "fsdp"), None),
            P("fsdp", None, None),
            P("fsdp", None, None),
            P("fsdp", None, None),
        ),
        out_specs=P("fsdp", "dp", None, None),
        check_vma=False,
    )
```

```python
import functools
import math

import jax
import jax.numpy as jnp
from jax import lax
from jax.experimental import pallas as pl
from jax.experimental.pallas import tpu as pltpu
from jax.sharding import PartitionSpec as P

QUAD = 4
SMEM = pl.BlockSpec(memory_space=pltpu.SMEM)
VMEM = pl.BlockSpec(memory_space=pltpu.VMEM)
BF16 = jnp.bfloat16
F32 = jnp.float32


def call(kernel, out_shape, in_specs, out_specs, operands, scratch=(), flops=0):
    shapes = list(operands) + list(jax.tree.leaves(out_shape)) + list(scratch)
    total = sum(math.prod(shape.shape) * shape.dtype.itemsize for shape in shapes)
    return pl.pallas_call(
        kernel,
        out_shape=out_shape,
        in_specs=in_specs,
        out_specs=out_specs,
        scratch_shapes=[pltpu.VMEM(shape.shape, shape.dtype) for shape in scratch],
        cost_estimate=pl.CostEstimate(flops=flops, bytes_accessed=total, transcendentals=0),
        compiler_params=pltpu.CompilerParams(
            vmem_limit_bytes=min(total + total // 2 + 4 * 2**20, 60 * 2**20)
        ),
    )(*operands)


def like(dtype, *shape):
    return jax.ShapeDtypeStruct(shape, dtype)


class Tables:
    def __init__(self, ref, sources):
        self.ref = ref
        self.slots = ref.shape[0] // (3 * sources)
        self.size = sources * self.slots

    def live_for(self, source, slot, target):
        at = source * self.slots + slot
        return jnp.logical_and(self.ref[self.size + at] == target, self.ref[at] > 0)

    def length(self, source, slot):
        return self.ref[source * self.slots + slot]

    def offset(self, source, slot):
        return self.ref[2 * self.size + source * self.slots + slot]


def own_columns(highs, weights, owner):
    width = weights.shape[1] // 2
    run = width // (highs * QUAD)
    parts = [
        weights[:, pl.ds(half * width + (high * QUAD + owner) * run, run)]
        for half in range(2)
        for high in range(highs)
    ]
    return jnp.concatenate(parts, axis=1)


def send_kernel(sources, place, packed, weights, frames, *refs):
    near, far, buf = refs[:QUAD], refs[QUAD:-1], refs[-1]
    tables = Tables(packed, sources)
    me = place[0]
    highs = sources // QUAD
    long, width = frames.shape[1:]
    wide = near[0].shape[1]
    for owner in range(QUAD):
        buf[owner] = own_columns(highs, weights, owner)
    for shift, out in enumerate(near + far):
        target = jnp.bitwise_xor(me, shift)
        found = jnp.int32(0)
        for slot in range(tables.slots):
            found = jnp.where(tables.live_for(me, slot, target), slot, found)
        if shift >= QUAD:
            out[...] = frames[found]
        else:
            for half in range(width // wide):
                first = half * wide
                out[half * long : (half + 1) * long, :] = frames[found, :, first : first + wide]
            out[width // wide * long :, :] = buf[jnp.bitwise_xor(lax.rem(me, QUAD), shift)]


def columns_kernel(*refs):
    arrived, piece = refs[:-1], refs[-1]
    for number, ref in enumerate(arrived):
        piece[number] = ref[ref.shape[0] - piece.shape[1] :, :]


def stack_kernel(*refs):
    parts, out = refs[:-1], refs[-1]
    wide = out.shape[2]
    at = 0
    for ref in parts:
        if len(ref.shape) == 3:
            out[at : at + ref.shape[0]] = ref[...]
            at += ref.shape[0]
        else:
            for first in range(0, ref.shape[1], wide):
                out[at] = ref[:, first : first + wide]
                at += 1


def table_kernel(source_count, long, place, packed, small, sources, lens, table, gain):
    tables = Tables(packed, source_count)
    highs = source_count // QUAD
    me = place[0]

    def look(source, carry):
        for slot in range(tables.slots):

            @pl.when(tables.live_for(source, slot, me))
            def _():
                number = tables.offset(source, slot) // long
                sources[number] = source
                lens[number] = tables.length(source, slot)

        return carry

    lax.fori_loop(0, source_count, look, 0)
    count, width = small.shape
    run = width // (highs * QUAD)
    whole = small[...]
    gain[...] = whole[count - 1 :, :]
    for owner in range(QUAD):

        @pl.when(lax.rem(me, QUAD) == owner)
        def _():
            starts = [(high * QUAD + owner) * run for high in range(highs)]
            parts = [whole[: count - 1, at : at + run] for at in starts]
            table[...] = jnp.concatenate(parts, axis=1)


def norm_kernel(place, sources, lens, gain, *refs):
    arrived, (kept, normed) = refs[:-2], refs[-2:]
    long, width = kept.shape[1:]
    for number in range(kept.shape[0]):
        shift = jnp.bitwise_xor(sources[number], place[0])
        for other, ref in enumerate(arrived):

            @pl.when(shift == other)
            def _():
                if other >= QUAD:
                    kept[number] = ref[...]
                else:
                    wide = ref.shape[1]
                    for half in range(width // wide):
                        rows = ref[half * long : (half + 1) * long, :]
                        kept[number, :, half * wide : (half + 1) * wide] = rows

        wide = kept[number].astype(F32)
        mean = jnp.mean(wide, axis=1, keepdims=True)
        centred = wide - mean
        var = jnp.mean(centred * centred, axis=1, keepdims=True)
        value = centred * lax.rsqrt(var + 1e-05) * gain[...]
        steps = lax.broadcasted_iota(jnp.int32, value.shape, 0)
        normed[number] = jnp.where(steps < lens[number], value, 0.0).astype(BF16)


def conv_rows(block, taps):
    long, chans = block.shape
    count = taps.shape[0]
    front = (count - 1) // 2
    groups = long // 8
    pieces = [block[8 * at : 8 * at + 8, :] for at in range(groups)]
    total = None
    for residue in range(8):
        rows = []
        for at in range(groups + 1):
            value = None
            for step in range(-(count // 8) - 1, count // 8 + 2):
                tap = 8 * step + residue + front - 16
                source = at + step - 2
                if 0 <= tap < count and 0 <= source < groups:
                    term = pieces[source] * taps[tap : tap + 1, :]
                    value = term if value is None else value + term
            rows.append(jnp.zeros((8, chans), F32) if value is None else value)
        whole = jnp.concatenate(rows, axis=0)[residue : residue + long, :]
        total = whole if total is None else total + whole
    return total


def main_kernel(layout, where, kept, table, *refs):
    pieces = max(len(layout), 2)
    chans = table.shape[1]
    taps = table[: table.shape[0] - 2, :]
    scale, shift = table[table.shape[0] - 2 : table.shape[0] - 1, :], table[table.shape[0] - 1 :, :]
    normed, weights = refs[:QUAD], refs[QUAD : QUAD + pieces]
    own, outs = refs[QUAD + pieces], refs[QUAD + pieces + 1 : 2 * QUAD + pieces]
    rows_buf, in_buf, out_buf, glu_buf, act_buf = refs[2 * QUAD + pieces :]
    recv, long, width = kept.shape
    tall = recv * long
    for number, ref in enumerate(normed):
        rows_buf[pl.ds(number * tall, tall), :] = ref[...].reshape(tall, width)
    if layout:
        w_in, w_out = in_buf, out_buf
        depth, wide = weights[0].shape[1:]
        for ref, slabs in zip(weights, layout):
            for at, (kind, other, number) in enumerate(slabs):
                if kind == "in":
                    start = pl.multiple_of(where[other, number] * depth, 16)
                    in_buf[pl.ds(start, depth), :] = ref[at]
                else:
                    start = pl.multiple_of(where[other, QUAD] * depth, 16)
                    first = number * wide
                    out_buf[pl.ds(start, depth), first : first + wide] = ref[at]
    else:
        w_in, w_out = weights
    glu_in = jnp.dot(rows_buf[...], w_in[...], preferred_element_type=F32)
    glu_buf[...] = glu_in[:, :chans] * jax.nn.sigmoid(glu_in[:, chans:])

    def utterance(at, carry):
        start = pl.multiple_of(at * long, long)
        moved = conv_rows(glu_buf[pl.ds(start, long), :], taps) * scale + shift
        act_buf[pl.ds(start, long), :] = (moved * jax.nn.sigmoid(moved)).astype(BF16)
        return carry

    lax.fori_loop(0, QUAD * recv, utterance, 0)
    mixed = jnp.dot(act_buf[...], w_out[...], preferred_element_type=F32)
    mixed = mixed.reshape(QUAD, recv, long, width)
    own[...] = kept[...].astype(F32) + mixed[0]
    for number, out in enumerate(outs, 1):
        out[...] = mixed[number].astype(BF16)


def shards(
    frames, ln_gain, w_in, depth_kernel, bn_scale, bn_shift, w_out, lengths, destinations, offsets
):
    dp_count, fsdp_count = lax.axis_size("dp"), lax.axis_size("fsdp")
    devices = dp_count * fsdp_count
    highs = dp_count // QUAD
    dp_index = lax.axis_index("dp")
    quad = dp_index % QUAD
    line = dp_index // QUAD * fsdp_count + lax.axis_index("fsdp")
    recv = lengths.shape[2] // 3
    _, _, long, width = frames.shape
    depth = w_in.shape[0]
    chans = width // QUAD
    wide = 2 * chans
    taps = depth_kernel.shape[0]

    def swap(array, high=0, quad=0, fsdp=0):
        mask = (high * QUAD + quad) * fsdp_count + fsdp
        return lax.ppermute(array, ("dp", "fsdp"), [(at, at ^ mask) for at in range(devices)])

    def quad_swap(arrays):
        return [arrays[0]] + [swap(arrays[mask], quad=mask) for mask in range(1, QUAD)]

    def gated(arrays, others):
        return lax.optimization_barrier((arrays, others))[0]

    place = dp_index.astype(jnp.int32)[None]
    packed = jnp.stack([lengths[0], destinations[0], offsets[0]]).reshape(-1)
    small = jnp.concatenate([depth_kernel, bn_scale[None], bn_shift[None], ln_gain[None]])
    bits = [1 << at for at in range((highs * fsdp_count).bit_length() - 1)]
    chip_bits = [bit for bit in reversed(bits) if 1 < bit < fsdp_count]

    count = width // wide

    sent = call(
        functools.partial(send_kernel, dp_count),
        [like(BF16, count * long + depth, wide)] * QUAD
        + [like(BF16, long, width)] * (dp_count - QUAD),
        [SMEM, SMEM, VMEM, VMEM],
        [VMEM] * dp_count,
        (place, packed, w_in, frames[0]),
        [like(BF16, QUAD, depth, wide)],
    )
    sent = list(sent)
    near = quad_swap(sent[:QUAD])
    later = QUAD + 2
    sent[later:] = gated(sent[later:], near[1])
    far = [
        swap(sent[shift], high=shift // QUAD, quad=shift % QUAD)
        for shift in range(QUAD, dp_count)
    ]

    w_out = gated(w_out, sent[:later])
    outs = {0: w_out}

    def share_chips(parts, first):
        for bit in chip_bits:
            for shift in [shift for shift in parts if (shift >= fsdp_count) == first]:
                parts[shift ^ bit] = swap(parts[shift], fsdp=bit)

    for mask in range(1, highs):
        outs[mask * fsdp_count] = swap(w_out, high=mask)
    share_chips(outs, False)
    share_chips(outs, True)
    sources, lens, table, gain = call(
        functools.partial(table_kernel, dp_count, long),
        [like(jnp.int32, recv)] * 2 + [like(F32, taps + 2, chans), like(F32, 1, width)],
        [SMEM] * 2 + [VMEM],
        [SMEM, SMEM, VMEM, VMEM],
        (place, packed, small),
    )

    own_in = call(
        columns_kernel,
        like(BF16, QUAD, depth, wide),
        [VMEM] * QUAD,
        VMEM,
        gated(near, (lens, gain)),
    )
    ins = {0: own_in}
    for mask in range(1, highs):
        ins[mask * fsdp_count] = swap(gated(own_in, far), high=mask)
    share_chips(ins, False)
    early = [shift for shift in ins if shift < fsdp_count]
    order = sorted(outs)
    stacked = call(
        stack_kernel,
        like(BF16, len(order) * count, depth, wide),
        [VMEM] * len(order),
        VMEM,
        [outs[shift] for shift in order],
    )
    crossed = {shift: swap(ins[shift], fsdp=1) for shift in early}
    crossed_out = swap(stacked, fsdp=1)
    utts = like(BF16, recv, long, width)
    kept, normed = call(
        norm_kernel,
        [utts, utts],
        [SMEM] * 3 + [VMEM] * (1 + dp_count),
        [VMEM, VMEM],
        (place, sources, lens, gain, *near, *gated(far, crossed)),
    )
    share_chips(ins, True)
    normed = quad_swap([normed] * QUAD)
    chip_mask = (fsdp_count - 1) ^ 1
    last = {at: ins[at] for at in ins if at & chip_mask and at not in early}
    for shift in ins:
        if shift not in crossed and shift not in last:
            crossed[shift] = swap(ins[shift], fsdp=1)
    for shift, part in gated(last, (normed, crossed, crossed_out)).items():
        crossed[shift] = swap(part, fsdp=1)
    pieces = list(ins.values()) + [stacked]
    layout = [[("in", shift, number) for number in range(QUAD)] for shift in ins]
    layout.append([("out", shift, half) for shift in order for half in range(count)])
    pieces += [crossed[shift] for shift in ins] + [crossed_out]
    layout += [[(kind, shift ^ 1, at) for kind, shift, at in slabs] for slabs in layout]

    out_rows = line ^ jnp.arange(highs * fsdp_count)
    in_rows = out_rows // fsdp_count * QUAD
    in_rows = in_rows[:, None] + (quad ^ jnp.arange(QUAD))[None, :]
    in_rows = in_rows * fsdp_count + (out_rows % fsdp_count)[:, None]
    where = jnp.concatenate([in_rows, out_rows[:, None]], 1).astype(jnp.int32)
    if depth % 16:
        slabs = {
            name: part[at]
            for part, names in zip(pieces, layout)
            for at, name in enumerate(names)
        }
        sides = range(highs * fsdp_count)
        flat = jnp.stack([slabs["in", at, number] for at in sides for number in range(QUAD)])
        all_in = jnp.zeros_like(flat).at[where[:, :QUAD].reshape(-1)].set(flat)
        flat = jnp.stack(
            [
                jnp.concatenate([slabs["out", at, half] for half in range(count)], axis=1)
                for at in sides
            ]
        )
        all_out = jnp.zeros_like(flat).at[where[:, QUAD]].set(flat)
        pieces = [all_in.reshape(width, wide), all_out.reshape(chans, width)]
        layout = []

    tall = QUAD * recv * long
    partial_sums = call(
        functools.partial(main_kernel, layout),
        [like(F32, recv, long, width)] + [utts] * (QUAD - 1),
        [SMEM] + [VMEM] * (2 + QUAD + len(pieces)),
        [VMEM] * QUAD,
        (where, kept, table, *normed, *pieces),
        [
            like(BF16, tall, width),
            like(BF16, width, wide),
            like(BF16, chans, width),
            like(F32, tall, chans),
            like(BF16, tall, chans),
        ],
        flops=6 * tall * width * chans,
    )
    own, *others = quad_swap(partial_sums)
    for part in others:
        own = own + part.astype(F32)
    live = jnp.arange(long, dtype=jnp.int32)[None, :, None] < lens[:, None, None]
    return jnp.where(live, own, 0.0).astype(BF16)[None]


def solution(mesh):
    return jax.shard_map(
        shards,
        mesh=mesh,
        in_specs=(
            P("fsdp", "dp", None, None),
            P(),
            P(("dp", "fsdp"), None),
            P(),
            P(),
            P(),
            P(("dp", "fsdp"), None),
            P("fsdp", None, None),
            P("fsdp", None, None),
            P("fsdp", None, None),
        ),
        out_specs=P("fsdp", "dp", None, None),
        check_vma=False,
    )
```

```python
import functools
import math

import jax
import jax.numpy as jnp
from jax import lax
from jax.experimental import pallas as pl
from jax.experimental.pallas import tpu as pltpu
from jax.sharding import PartitionSpec as P

QUAD = 4
SMEM = pl.BlockSpec(memory_space=pltpu.SMEM)
VMEM = pl.BlockSpec(memory_space=pltpu.VMEM)
BF16 = jnp.bfloat16
F32 = jnp.float32


def call(kernel, out_shape, in_specs, out_specs, operands, scratch=(), flops=0):
    shapes = list(operands) + list(jax.tree.leaves(out_shape)) + list(scratch)
    total = sum(math.prod(shape.shape) * shape.dtype.itemsize for shape in shapes)
    return pl.pallas_call(
        kernel,
        out_shape=out_shape,
        in_specs=in_specs,
        out_specs=out_specs,
        scratch_shapes=[pltpu.VMEM(shape.shape, shape.dtype) for shape in scratch],
        cost_estimate=pl.CostEstimate(flops=flops, bytes_accessed=total, transcendentals=0),
        compiler_params=pltpu.CompilerParams(
            vmem_limit_bytes=min(total + total // 2 + 4 * 2**20, 60 * 2**20)
        ),
    )(*operands)


def like(dtype, *shape):
    return jax.ShapeDtypeStruct(shape, dtype)


class Tables:
    def __init__(self, ref, sources):
        self.ref = ref
        self.slots = ref.shape[0] // (3 * sources)
        self.size = sources * self.slots

    def live_for(self, source, slot, target):
        at = source * self.slots + slot
        return jnp.logical_and(self.ref[self.size + at] == target, self.ref[at] > 0)

    def length(self, source, slot):
        return self.ref[source * self.slots + slot]

    def offset(self, source, slot):
        return self.ref[2 * self.size + source * self.slots + slot]


def own_columns(highs, weights, owner):
    width = weights.shape[1] // 2
    run = width // (highs * QUAD)
    parts = [
        weights[:, pl.ds(half * width + (high * QUAD + owner) * run, run)]
        for half in range(2)
        for high in range(highs)
    ]
    return jnp.concatenate(parts, axis=1)


def send_kernel(sources, place, packed, weights, frames, *refs):
    outs, buf = refs[:-1], refs[-1]
    tables = Tables(packed, sources)
    me = place[0]
    highs = sources // QUAD
    long, width = frames.shape[1:]
    wide = outs[0].shape[1]
    for owner in range(QUAD):
        buf[owner] = own_columns(highs, weights, owner)
    for number, out in enumerate(outs):
        for far in range(highs):
            target = jnp.bitwise_xor(me, far * QUAD + number)
            found = jnp.int32(0)
            for slot in range(tables.slots):
                found = jnp.where(tables.live_for(me, slot, target), slot, found)
            for half in range(width // wide):
                start = (far * (width // wide) + half) * long
                out[start : start + long, :] = frames[found, :, half * wide : half * wide + wide]
        start = highs * (width // wide) * long
        out[start:, :] = buf[jnp.bitwise_xor(lax.rem(me, QUAD), number)]


def fetch(out, number, ref, start):
    long, width = out.shape[1:]
    wide = ref.shape[1]
    for half in range(width // wide):
        rows = ref[pl.ds(start + half * long, long), :]
        out[number, :, half * wide : half * wide + wide] = rows


def merge_kernel(sources, long, place, packed, *refs):
    arrived, outs, piece = refs[:QUAD], refs[QUAD:-1], refs[-1]
    tables = Tables(packed, sources)
    me = place[0]
    depth = piece.shape[1]
    size = (arrived[0].shape[0] - depth) * QUAD // sources
    for number, ref in enumerate(arrived):
        columns = ref[ref.shape[0] - depth :, :]
        piece[number] = columns
        for out in outs:
            out[number * depth : (number + 1) * depth, :] = columns
    for far, out in enumerate(outs, 1):
        for number, ref in enumerate(arrived):
            source = jnp.bitwise_xor(me, number)
            target = jnp.bitwise_xor(me, far * QUAD)
            start = jnp.int32(-1)
            for slot in range(tables.slots):
                hit = tables.live_for(source, slot, target)
                start = jnp.where(hit, tables.offset(source, slot), start)

            @pl.when(start >= 0)
            def _():
                at = pl.multiple_of(start // long * size + QUAD * depth, 8)
                out[pl.ds(at, size), :] = ref[far * size : (far + 1) * size, :]


def stack_kernel(*refs):
    parts, out = refs[:-1], refs[-1]
    wide = out.shape[2]
    at = 0
    for ref in parts:
        if len(ref.shape) == 3:
            out[at : at + ref.shape[0]] = ref[...]
            at += ref.shape[0]
        else:
            for first in range(0, ref.shape[1], wide):
                out[at] = ref[:, first : first + wide]
                at += 1


def table_kernel(source_count, long, place, packed, small, sources, lens, table, gain):
    tables = Tables(packed, source_count)
    highs = source_count // QUAD
    me = place[0]

    def look(source, carry):
        for slot in range(tables.slots):

            @pl.when(tables.live_for(source, slot, me))
            def _():
                number = tables.offset(source, slot) // long
                sources[number] = source
                lens[number] = tables.length(source, slot)

        return carry

    lax.fori_loop(0, source_count, look, 0)
    count, width = small.shape
    run = width // (highs * QUAD)
    whole = small[...]
    gain[...] = whole[count - 1 :, :]
    for owner in range(QUAD):

        @pl.when(lax.rem(me, QUAD) == owner)
        def _():
            starts = [(high * QUAD + owner) * run for high in range(highs)]
            parts = [whole[: count - 1, at : at + run] for at in starts]
            table[...] = jnp.concatenate(parts, axis=1)


def norm_kernel(first, place, sources, lens, gain, *refs):
    near, far, (kept, normed) = refs[:QUAD], refs[QUAD:-2], refs[-2:]
    size = kept.shape[1] * kept.shape[2] // near[0].shape[1]
    for number in range(kept.shape[0]):
        shift = jnp.bitwise_xor(sources[number], place[0])
        for other, ref in enumerate(near):

            @pl.when(shift == other)
            def _():
                fetch(kept, number, ref, 0)

        for other, ref in enumerate(far, 1):

            @pl.when(shift // QUAD == other)
            def _():
                fetch(kept, number, ref, first + number * size)

        wide = kept[number].astype(F32)
        mean = jnp.mean(wide, axis=1, keepdims=True)
        centred = wide - mean
        var = jnp.mean(centred * centred, axis=1, keepdims=True)
        value = centred * lax.rsqrt(var + 1e-05) * gain[...]
        steps = lax.broadcasted_iota(jnp.int32, value.shape, 0)
        normed[number] = jnp.where(steps < lens[number], value, 0.0).astype(BF16)


def conv_rows(block, taps):
    long, chans = block.shape
    count = taps.shape[0]
    front = (count - 1) // 2
    groups = long // 8
    pieces = [block[8 * at : 8 * at + 8, :] for at in range(groups)]
    total = None
    for residue in range(8):
        rows = []
        for at in range(groups + 1):
            value = None
            for step in range(-(count // 8) - 1, count // 8 + 2):
                tap = 8 * step + residue + front - 16
                source = at + step - 2
                if 0 <= tap < count and 0 <= source < groups:
                    term = pieces[source] * taps[tap : tap + 1, :]
                    value = term if value is None else value + term
            rows.append(jnp.zeros((8, chans), F32) if value is None else value)
        whole = jnp.concatenate(rows, axis=0)[residue : residue + long, :]
        total = whole if total is None else total + whole
    return total


def main_kernel(layout, where, kept, table, *refs):
    pieces = max(len(layout), 2)
    chans = table.shape[1]
    taps = table[: table.shape[0] - 2, :]
    scale, shift = table[table.shape[0] - 2 : table.shape[0] - 1, :], table[table.shape[0] - 1 :, :]
    normed, weights = refs[:QUAD], refs[QUAD : QUAD + pieces]
    own, outs = refs[QUAD + pieces], refs[QUAD + pieces + 1 : 2 * QUAD + pieces]
    rows_buf, in_buf, out_buf, glu_buf, act_buf = refs[2 * QUAD + pieces :]
    recv, long, width = kept.shape
    tall = recv * long
    for number, ref in enumerate(normed):
        rows_buf[pl.ds(number * tall, tall), :] = ref[...].reshape(tall, width)
    if layout:
        w_in, w_out = in_buf, out_buf
        depth, wide = weights[0].shape[1:]
        for ref, slabs in zip(weights, layout):
            for at, (kind, other, number) in enumerate(slabs):
                if kind == "in":
                    start = pl.multiple_of(where[other, number] * depth, 16)
                    in_buf[pl.ds(start, depth), :] = ref[at]
                else:
                    start = pl.multiple_of(where[other, QUAD] * depth, 16)
                    first = number * wide
                    out_buf[pl.ds(start, depth), first : first + wide] = ref[at]
    else:
        w_in, w_out = weights
    glu_in = jnp.dot(rows_buf[...], w_in[...], preferred_element_type=F32)
    glu_buf[...] = glu_in[:, :chans] * jax.nn.sigmoid(glu_in[:, chans:])

    def utterance(at, carry):
        start = pl.multiple_of(at * long, long)
        moved = conv_rows(glu_buf[pl.ds(start, long), :], taps) * scale + shift
        act_buf[pl.ds(start, long), :] = (moved * jax.nn.sigmoid(moved)).astype(BF16)
        return carry

    lax.fori_loop(0, QUAD * recv, utterance, 0)
    mixed = jnp.dot(act_buf[...], w_out[...], preferred_element_type=F32)
    mixed = mixed.reshape(QUAD, recv, long, width)
    own[...] = kept[...].astype(F32) + mixed[0]
    for number, out in enumerate(outs, 1):
        out[...] = mixed[number].astype(BF16)


def shards(
    frames, ln_gain, w_in, depth_kernel, bn_scale, bn_shift, w_out, lengths, destinations, offsets
):
    dp_count, fsdp_count = lax.axis_size("dp"), lax.axis_size("fsdp")
    devices = dp_count * fsdp_count
    highs = dp_count // QUAD
    dp_index = lax.axis_index("dp")
    quad = dp_index % QUAD
    line = dp_index // QUAD * fsdp_count + lax.axis_index("fsdp")
    recv = lengths.shape[2] // 3
    _, _, long, width = frames.shape
    depth = w_in.shape[0]
    chans = width // QUAD
    wide = 2 * chans
    taps = depth_kernel.shape[0]

    def swap(array, high=0, quad=0, fsdp=0):
        mask = (high * QUAD + quad) * fsdp_count + fsdp
        return lax.ppermute(array, ("dp", "fsdp"), [(at, at ^ mask) for at in range(devices)])

    def quad_swap(arrays):
        return [arrays[0]] + [swap(arrays[mask], quad=mask) for mask in range(1, QUAD)]

    def gated(arrays, others):
        return lax.optimization_barrier((arrays, others))[0]

    place = dp_index.astype(jnp.int32)[None]
    packed = jnp.stack([lengths[0], destinations[0], offsets[0]]).reshape(-1)
    small = jnp.concatenate([depth_kernel, bn_scale[None], bn_shift[None], ln_gain[None]])
    bits = [1 << at for at in range((highs * fsdp_count).bit_length() - 1)]
    chip_bits = [bit for bit in reversed(bits) if 1 < bit < fsdp_count]

    count = width // wide

    sent = call(
        functools.partial(send_kernel, dp_count),
        [like(BF16, highs * count * long + depth, wide)] * QUAD,
        [SMEM, SMEM, VMEM, VMEM],
        [VMEM] * QUAD,
        (place, packed, w_in, frames[0]),
        [like(BF16, QUAD, depth, wide)],
    )
    near = quad_swap(sent)

    w_out = gated(w_out, sent)
    outs = {0: w_out}

    def share_chips(parts, first):
        for bit in chip_bits:
            for shift in [shift for shift in parts if (shift >= fsdp_count) == first]:
                parts[shift ^ bit] = swap(parts[shift], fsdp=bit)

    for mask in range(1, highs):
        outs[mask * fsdp_count] = swap(w_out, high=mask)
    share_chips(outs, False)

    sources, lens, table, gain = call(
        functools.partial(table_kernel, dp_count, long),
        [like(jnp.int32, recv)] * 2 + [like(F32, taps + 2, chans), like(F32, 1, width)],
        [SMEM] * 2 + [VMEM],
        [SMEM, SMEM, VMEM, VMEM],
        (place, packed, small),
    )
    utts = like(BF16, recv, long, width)
    *far, own_in = call(
        functools.partial(merge_kernel, dp_count, long),
        [like(BF16, QUAD * depth + recv * count * long, wide)] * (highs - 1)
        + [like(BF16, QUAD, depth, wide)],
        [SMEM] * 2 + [VMEM] * QUAD,
        [VMEM] * highs,
        (gated(place, (lens, gain, outs)), packed, *near),
    )
    far = [swap(part, high=mask) for mask, part in enumerate(far, 1)]

    ins = {0: own_in}
    share_chips(ins, False)
    early = list(ins)
    share_chips(outs, True)
    order = sorted(outs)
    stacked = call(
        stack_kernel,
        like(BF16, len(order) * count, depth, wide),
        [VMEM] * len(order),
        VMEM,
        [outs[shift] for shift in order],
    )
    crossed = {shift: swap(ins[shift], fsdp=1) for shift in early}
    crossed_out = swap(stacked, fsdp=1)
    for mask, part in enumerate(far, 1):
        ins[mask * fsdp_count] = part[: QUAD * depth].reshape(QUAD, depth, wide)
    kept, normed = call(
        functools.partial(norm_kernel, QUAD * depth),
        [utts, utts],
        [SMEM] * 3 + [VMEM] * (QUAD + highs),
        [VMEM, VMEM],
        (place, sources, lens, gain, *near, *gated(far, (crossed, crossed_out))),
    )
    share_chips(ins, True)
    normed = quad_swap([normed] * QUAD)
    chip_mask = (fsdp_count - 1) ^ 1
    last = {at: ins[at] for at in ins if at & chip_mask and at not in early}
    last = gated(last, normed)
    for shift in ins:
        if shift not in crossed:
            crossed[shift] = swap(last.get(shift, ins[shift]), fsdp=1)
    pieces = list(ins.values()) + [stacked]
    layout = [[("in", shift, number) for number in range(QUAD)] for shift in ins]
    layout.append([("out", shift, half) for shift in order for half in range(count)])
    pieces += [crossed[shift] for shift in ins] + [crossed_out]
    layout += [[(kind, shift ^ 1, at) for kind, shift, at in slabs] for slabs in layout]

    out_rows = line ^ jnp.arange(highs * fsdp_count)
    in_rows = out_rows // fsdp_count * QUAD
    in_rows = in_rows[:, None] + (quad ^ jnp.arange(QUAD))[None, :]
    in_rows = in_rows * fsdp_count + (out_rows % fsdp_count)[:, None]
    where = jnp.concatenate([in_rows, out_rows[:, None]], 1).astype(jnp.int32)
    if depth % 16:
        slabs = {
            name: part[at]
            for part, names in zip(pieces, layout)
            for at, name in enumerate(names)
        }
        sides = range(highs * fsdp_count)
        flat = jnp.stack([slabs["in", at, number] for at in sides for number in range(QUAD)])
        all_in = jnp.zeros_like(flat).at[where[:, :QUAD].reshape(-1)].set(flat)
        flat = jnp.stack(
            [
                jnp.concatenate([slabs["out", at, half] for half in range(count)], axis=1)
                for at in sides
            ]
        )
        all_out = jnp.zeros_like(flat).at[where[:, QUAD]].set(flat)
        pieces = [all_in.reshape(width, wide), all_out.reshape(chans, width)]
        layout = []

    tall = QUAD * recv * long
    partial_sums = call(
        functools.partial(main_kernel, layout),
        [like(F32, recv, long, width)] + [utts] * (QUAD - 1),
        [SMEM] + [VMEM] * (2 + QUAD + len(pieces)),
        [VMEM] * QUAD,
        (where, kept, table, *normed, *pieces),
        [
            like(BF16, tall, width),
            like(BF16, width, wide),
            like(BF16, chans, width),
            like(F32, tall, chans),
            like(BF16, tall, chans),
        ],
        flops=6 * tall * width * chans,
    )
    own, *others = quad_swap(partial_sums)
    for part in others:
        own = own + part.astype(F32)
    live = jnp.arange(long, dtype=jnp.int32)[None, :, None] < lens[:, None, None]
    return jnp.where(live, own, 0.0).astype(BF16)[None]


def solution(mesh):
    return jax.shard_map(
        shards,
        mesh=mesh,
        in_specs=(
            P("fsdp", "dp", None, None),
            P(),
            P(("dp", "fsdp"), None),
            P(),
            P(),
            P(),
            P(("dp", "fsdp"), None),
            P("fsdp", None, None),
            P("fsdp", None, None),
            P("fsdp", None, None),
        ),
        out_specs=P("fsdp", "dp", None, None),
        check_vma=False,
    )
```

```python
import functools
import math

import jax
import jax.numpy as jnp
from jax import lax
from jax.experimental import pallas as pl
from jax.experimental.pallas import tpu as pltpu
from jax.sharding import PartitionSpec as P

QUAD = 4
SMEM = pl.BlockSpec(memory_space=pltpu.SMEM)
VMEM = pl.BlockSpec(memory_space=pltpu.VMEM)
BF16 = jnp.bfloat16
F32 = jnp.float32


def call(kernel, out_shape, in_specs, out_specs, operands, scratch=(), flops=0):
    shapes = list(operands) + list(jax.tree.leaves(out_shape)) + list(scratch)
    total = sum(math.prod(shape.shape) * shape.dtype.itemsize for shape in shapes)
    return pl.pallas_call(
        kernel,
        out_shape=out_shape,
        in_specs=in_specs,
        out_specs=out_specs,
        scratch_shapes=[pltpu.VMEM(shape.shape, shape.dtype) for shape in scratch],
        cost_estimate=pl.CostEstimate(flops=flops, bytes_accessed=total, transcendentals=0),
        compiler_params=pltpu.CompilerParams(
            vmem_limit_bytes=min(total + total // 2 + 4 * 2**20, 60 * 2**20)
        ),
    )(*operands)


def like(dtype, *shape):
    return jax.ShapeDtypeStruct(shape, dtype)


class Tables:
    def __init__(self, ref, sources):
        self.ref = ref
        self.slots = ref.shape[0] // (3 * sources)
        self.size = sources * self.slots

    def live_for(self, source, slot, target):
        at = source * self.slots + slot
        return jnp.logical_and(self.ref[self.size + at] == target, self.ref[at] > 0)

    def length(self, source, slot):
        return self.ref[source * self.slots + slot]

    def offset(self, source, slot):
        return self.ref[2 * self.size + source * self.slots + slot]


def own_columns(highs, weights, owner):
    width = weights.shape[1] // 2
    run = width // (highs * QUAD)
    parts = [
        weights[:, pl.ds(half * width + (high * QUAD + owner) * run, run)]
        for half in range(2)
        for high in range(highs)
    ]
    return jnp.concatenate(parts, axis=1)


def send_kernel(sources, place, packed, frames, *outs):
    tables = Tables(packed, sources)
    me = place[0]
    for number, out in enumerate(outs):
        for far in range(out.shape[0]):
            target = jnp.bitwise_xor(me, far * QUAD + number)
            found = jnp.int32(0)
            for slot in range(tables.slots):
                found = jnp.where(tables.live_for(me, slot, target), slot, found)
            out[far] = frames[found]


def merge_kernel(sources, place, packed, *refs):
    arrived, outs = refs[:QUAD], refs[QUAD:]
    tables = Tables(packed, sources)
    me = place[0]
    for far, out in enumerate(outs):
        long = out.shape[1]
        for number, ref in enumerate(arrived):
            source = jnp.bitwise_xor(me, number)
            target = jnp.bitwise_xor(me, far * QUAD)
            start = jnp.int32(-1)
            for slot in range(tables.slots):
                hit = tables.live_for(source, slot, target)
                start = jnp.where(hit, tables.offset(source, slot), start)

            @pl.when(start >= 0)
            def _():
                out[start // long] = ref[far]


def split_kernel(highs, place, weights, *refs):
    outs, buf = refs[:-1], refs[-1]
    for owner in range(QUAD):
        buf[owner] = own_columns(highs, weights, owner)
    for number, out in enumerate(outs):
        out[...] = buf[jnp.bitwise_xor(lax.rem(place[0], QUAD), number)]


def table_kernel(source_count, long, place, packed, small, sources, lens, table, gain):
    tables = Tables(packed, source_count)
    highs = source_count // QUAD
    me = place[0]

    def look(source, carry):
        for slot in range(tables.slots):

            @pl.when(tables.live_for(source, slot, me))
            def _():
                number = tables.offset(source, slot) // long
                sources[number] = source
                lens[number] = tables.length(source, slot)

        return carry

    lax.fori_loop(0, source_count, look, 0)
    count, width = small.shape
    run = width // (highs * QUAD)
    whole = small[...]
    gain[...] = whole[count - 1 :, :]
    for owner in range(QUAD):

        @pl.when(lax.rem(me, QUAD) == owner)
        def _():
            starts = [(high * QUAD + owner) * run for high in range(highs)]
            parts = [whole[: count - 1, at : at + run] for at in starts]
            table[...] = jnp.concatenate(parts, axis=1)


def norm_kernel(place, sources, lens, gain, *refs):
    arrived, (kept, normed) = refs[:-2], refs[-2:]
    for number in range(kept.shape[0]):
        shift = jnp.bitwise_xor(sources[number], place[0]) // QUAD
        for other, ref in enumerate(arrived):

            @pl.when(shift == other)
            def _():
                kept[number] = ref[number]

        wide = kept[number].astype(F32)
        mean = jnp.mean(wide, axis=1, keepdims=True)
        centred = wide - mean
        var = jnp.mean(centred * centred, axis=1, keepdims=True)
        value = centred * lax.rsqrt(var + 1e-05) * gain[...]
        steps = lax.broadcasted_iota(jnp.int32, value.shape, 0)
        normed[number] = jnp.where(steps < lens[number], value, 0.0).astype(BF16)


def conv_rows(block, taps):
    long, chans = block.shape
    count = taps.shape[0]
    front = (count - 1) // 2
    groups = long // 8
    pieces = [block[8 * at : 8 * at + 8, :] for at in range(groups)]
    total = None
    for residue in range(8):
        rows = []
        for at in range(groups + 1):
            value = None
            for step in range(-(count // 8) - 1, count // 8 + 2):
                tap = 8 * step + residue + front - 16
                source = at + step - 2
                if 0 <= tap < count and 0 <= source < groups:
                    term = pieces[source] * taps[tap : tap + 1, :]
                    value = term if value is None else value + term
            rows.append(jnp.zeros((8, chans), F32) if value is None else value)
        whole = jnp.concatenate(rows, axis=0)[residue : residue + long, :]
        total = whole if total is None else total + whole
    return total


def main_kernel(pieces, where, kept, table, *refs):
    normed, weights = refs[:QUAD], refs[QUAD : QUAD + pieces]
    own, outs = refs[QUAD + pieces], refs[QUAD + pieces + 1 : 2 * QUAD + pieces]
    rows_buf, in_buf, out_buf, glu_buf, act_buf = refs[2 * QUAD + pieces :]
    recv, long, width = kept.shape
    tall = recv * long
    chans = table.shape[1]
    taps = table[: table.shape[0] - 2, :]
    scale, shift = table[table.shape[0] - 2 : table.shape[0] - 1, :], table[table.shape[0] - 1 :, :]
    for number, ref in enumerate(normed):
        rows_buf[pl.ds(number * tall, tall), :] = ref[...].reshape(tall, width)
    if pieces == 2:
        w_in, w_out = weights
    else:
        w_in, w_out = in_buf, out_buf
        depth, wide = weights[0].shape[1:]
        for number, ref in enumerate(weights):
            for inner in range(QUAD):
                start = pl.multiple_of(where[number, inner] * depth, 16)
                in_buf[pl.ds(start, depth), :] = ref[inner]
            start = pl.multiple_of(where[number, QUAD] * depth, 16)
            for half in range(width // wide):
                out_buf[pl.ds(start, depth), half * wide : half * wide + wide] = ref[QUAD + half]
    glu_in = jnp.dot(rows_buf[...], w_in[...], preferred_element_type=F32)
    glu_buf[...] = glu_in[:, :chans] * jax.nn.sigmoid(glu_in[:, chans:])

    def utterance(at, carry):
        start = pl.multiple_of(at * long, long)
        moved = conv_rows(glu_buf[pl.ds(start, long), :], taps) * scale + shift
        act_buf[pl.ds(start, long), :] = (moved * jax.nn.sigmoid(moved)).astype(BF16)
        return carry

    lax.fori_loop(0, QUAD * recv, utterance, 0)
    mixed = jnp.dot(act_buf[...], w_out[...], preferred_element_type=F32)
    mixed = mixed.reshape(QUAD, recv, long, width)
    own[...] = kept[...].astype(F32) + mixed[0]
    for number, out in enumerate(outs, 1):
        out[...] = mixed[number].astype(BF16)


def shards(
    frames, ln_gain, w_in, depth_kernel, bn_scale, bn_shift, w_out, lengths, destinations, offsets
):
    dp_count, fsdp_count = lax.axis_size("dp"), lax.axis_size("fsdp")
    devices = dp_count * fsdp_count
    highs = dp_count // QUAD
    dp_index = lax.axis_index("dp")
    quad = dp_index % QUAD
    line = dp_index // QUAD * fsdp_count + lax.axis_index("fsdp")
    recv = lengths.shape[2] // 3
    _, _, long, width = frames.shape
    depth = w_in.shape[0]
    chans = width // QUAD
    wide = 2 * chans
    taps = depth_kernel.shape[0]

    def swap(array, high=0, quad=0, fsdp=0):
        mask = (high * QUAD + quad) * fsdp_count + fsdp
        return lax.ppermute(array, ("dp", "fsdp"), [(at, at ^ mask) for at in range(devices)])

    def quad_swap(arrays):
        return [arrays[0]] + [swap(arrays[mask], quad=mask) for mask in range(1, QUAD)]

    def gated(arrays, others):
        return lax.optimization_barrier((arrays, others))[0]

    place = dp_index.astype(jnp.int32)[None]
    packed = jnp.stack([lengths[0], destinations[0], offsets[0]]).reshape(-1)
    small = jnp.concatenate([depth_kernel, bn_scale[None], bn_shift[None], ln_gain[None]])
    bits = [1 << at for at in range((highs * fsdp_count).bit_length() - 1)]
    chip_bits = [bit for bit in reversed(bits) if 1 < bit < fsdp_count]

    if depth % 16 == 0:
        split = call(
            functools.partial(split_kernel, highs),
            [like(BF16, depth, wide)] * QUAD,
            [SMEM, VMEM],
            [VMEM] * QUAD,
            (place, w_in),
            [like(BF16, QUAD, depth, wide)],
        )
    else:
        by_owner = w_in.reshape(depth, 2, highs, QUAD, chans // highs).transpose(3, 0, 1, 2, 4)
        by_owner = by_owner.reshape(QUAD, depth, wide)
        split = [
            lax.dynamic_index_in_dim(by_owner, quad ^ mask, 0, keepdims=False)
            for mask in range(QUAD)
        ]
    columns = quad_swap(split)

    near = call(
        functools.partial(send_kernel, dp_count),
        [like(BF16, highs, long, width)] * QUAD,
        [SMEM, SMEM, VMEM],
        [VMEM] * QUAD,
        (place, packed, frames[0]),
    )
    near = quad_swap(near)
    columns = gated(columns, near[1])
    sources, lens, table, gain = call(
        functools.partial(table_kernel, dp_count, long),
        [like(jnp.int32, recv)] * 2 + [like(F32, taps + 2, chans), like(F32, 1, width)],
        [SMEM] * 2 + [VMEM],
        [SMEM, SMEM, VMEM, VMEM],
        (place, packed, small),
    )
    utts = like(BF16, recv, long, width)
    held, *far = call(
        functools.partial(merge_kernel, dp_count),
        [utts] * highs,
        [SMEM] * 2 + [VMEM] * QUAD,
        [VMEM] * highs,
        (gated(place, (lens, gain)), packed, *near),
    )
    merged = far
    far = [swap(part, high=mask) for mask, part in enumerate(far, 1)]

    halves = [w_out[:, at : at + wide] for at in range(0, width, wide)]
    pieces = [jnp.stack(columns + halves)]
    shifts = [mask * fsdp_count for mask in range(highs)]
    chip_first = [swap(pieces[0], fsdp=bit) for bit in chip_bits[:1]]
    crossing = [swap(pieces[0], high=mask) for mask in range(1, highs)]
    pieces += gated(crossing, (merged, chip_first))
    early = [swap(part, fsdp=1) for part in pieces[:1] + chip_first]
    far = gated(far, early)
    kept, normed = call(
        norm_kernel,
        [utts, utts],
        [SMEM] * 3 + [VMEM] * (1 + highs),
        [VMEM, VMEM],
        (place, sources, lens, gain, held, *far),
    )
    for bit in chip_bits:
        first = chip_first if bit == chip_bits[0] else []
        pieces = pieces + first + [swap(part, fsdp=bit) for part in pieces[len(first) :]]
        shifts = shifts + [shift ^ bit for shift in shifts]
    normed = quad_swap([normed] * QUAD)
    ends = len(shifts) // 2 + 1
    pieces[ends:] = gated(pieces[ends:], normed)
    cored = [swap(part, fsdp=1) for part in pieces]
    cored[0], cored[len(shifts) // 2] = early[0], early[-1]
    pieces = pieces + cored
    shifts = shifts + [shift ^ 1 for shift in shifts]

    out_rows = line ^ jnp.array(shifts)
    in_rows = out_rows // fsdp_count * QUAD
    in_rows = in_rows[:, None] + (quad ^ jnp.arange(QUAD))[None, :]
    in_rows = in_rows * fsdp_count + (out_rows % fsdp_count)[:, None]
    where = jnp.concatenate([in_rows, out_rows[:, None]], 1).astype(jnp.int32)
    if depth % 16:
        together = jnp.stack(pieces)
        flat = together[:, :QUAD].reshape(-1, depth, wide)
        all_in = jnp.zeros_like(flat).at[where[:, :QUAD].reshape(-1)].set(flat)
        flat = together[:, QUAD:].transpose(0, 2, 1, 3).reshape(-1, depth, width)
        all_out = jnp.zeros_like(flat).at[where[:, QUAD]].set(flat)
        pieces = [all_in.reshape(width, wide), all_out.reshape(chans, width)]

    tall = QUAD * recv * long
    partial_sums = call(
        functools.partial(main_kernel, len(pieces)),
        [like(F32, recv, long, width)] + [utts] * (QUAD - 1),
        [SMEM] + [VMEM] * (2 + QUAD + len(pieces)),
        [VMEM] * QUAD,
        (where, kept, table, *normed, *pieces),
        [
            like(BF16, tall, width),
            like(BF16, width, wide),
            like(BF16, chans, width),
            like(F32, tall, chans),
            like(BF16, tall, chans),
        ],
        flops=6 * tall * width * chans,
    )
    own, *others = quad_swap(partial_sums)
    for part in others:
        own = own + part.astype(F32)
    live = jnp.arange(long, dtype=jnp.int32)[None, :, None] < lens[:, None, None]
    return jnp.where(live, own, 0.0).astype(BF16)[None]


def solution(mesh):
    return jax.shard_map(
        shards,
        mesh=mesh,
        in_specs=(
            P("fsdp", "dp", None, None),
            P(),
            P(("dp", "fsdp"), None),
            P(),
            P(),
            P(),
            P(("dp", "fsdp"), None),
            P("fsdp", None, None),
            P("fsdp", None, None),
            P("fsdp", None, None),
        ),
        out_specs=P("fsdp", "dp", None, None),
        check_vma=False,
    )
```

```python
import functools
import math

import jax
import jax.numpy as jnp
from jax import lax
from jax.experimental import pallas as pl
from jax.experimental.pallas import tpu as pltpu
from jax.sharding import PartitionSpec as P

QUAD = 4
SMEM = pl.BlockSpec(memory_space=pltpu.SMEM)
VMEM = pl.BlockSpec(memory_space=pltpu.VMEM)
BF16 = jnp.bfloat16
F32 = jnp.float32


def call(kernel, out_shape, in_specs, out_specs, operands, scratch=(), flops=0):
    shapes = list(operands) + list(jax.tree.leaves(out_shape)) + list(scratch)
    total = sum(math.prod(shape.shape) * shape.dtype.itemsize for shape in shapes)
    return pl.pallas_call(
        kernel,
        out_shape=out_shape,
        in_specs=in_specs,
        out_specs=out_specs,
        scratch_shapes=[pltpu.VMEM(shape.shape, shape.dtype) for shape in scratch],
        cost_estimate=pl.CostEstimate(flops=flops, bytes_accessed=total, transcendentals=0),
        compiler_params=pltpu.CompilerParams(
            vmem_limit_bytes=min(total + total // 2 + 4 * 2**20, 60 * 2**20)
        ),
    )(*operands)


def like(dtype, *shape):
    return jax.ShapeDtypeStruct(shape, dtype)


class Tables:
    def __init__(self, ref, sources):
        self.ref = ref
        self.slots = ref.shape[0] // (3 * sources)
        self.size = sources * self.slots

    def live_for(self, source, slot, target):
        at = source * self.slots + slot
        return jnp.logical_and(self.ref[self.size + at] == target, self.ref[at] > 0)

    def length(self, source, slot):
        return self.ref[source * self.slots + slot]

    def offset(self, source, slot):
        return self.ref[2 * self.size + source * self.slots + slot]


def own_columns(highs, weights, owner):
    width = weights.shape[1] // 2
    run = width // (highs * QUAD)
    parts = [
        weights[:, pl.ds(half * width + (high * QUAD + owner) * run, run)]
        for half in range(2)
        for high in range(highs)
    ]
    return jnp.concatenate(parts, axis=1)


def send_kernel(sources, place, packed, frames, *outs):
    tables = Tables(packed, sources)
    me = place[0]
    for number, out in enumerate(outs):
        for far in range(out.shape[0]):
            target = jnp.bitwise_xor(me, far * QUAD + number)
            found = jnp.int32(0)
            for slot in range(tables.slots):
                found = jnp.where(tables.live_for(me, slot, target), slot, found)
            out[far] = frames[found]


def merge_kernel(sources, place, packed, *refs):
    arrived, outs = refs[:QUAD], refs[QUAD:]
    tables = Tables(packed, sources)
    me = place[0]
    for far, out in enumerate(outs):
        long = out.shape[1]
        for number, ref in enumerate(arrived):
            source = jnp.bitwise_xor(me, number)
            target = jnp.bitwise_xor(me, far * QUAD)
            start = jnp.int32(-1)
            for slot in range(tables.slots):
                hit = tables.live_for(source, slot, target)
                start = jnp.where(hit, tables.offset(source, slot), start)

            @pl.when(start >= 0)
            def _():
                out[start // long] = ref[far]


def split_kernel(highs, place, weights, *refs):
    outs, buf = refs[:-1], refs[-1]
    for owner in range(QUAD):
        buf[owner] = own_columns(highs, weights, owner)
    for number, out in enumerate(outs):
        out[...] = buf[jnp.bitwise_xor(lax.rem(place[0], QUAD), number)]


def table_kernel(source_count, long, place, packed, small, sources, lens, table, gain):
    tables = Tables(packed, source_count)
    highs = source_count // QUAD
    me = place[0]

    def look(source, carry):
        for slot in range(tables.slots):

            @pl.when(tables.live_for(source, slot, me))
            def _():
                number = tables.offset(source, slot) // long
                sources[number] = source
                lens[number] = tables.length(source, slot)

        return carry

    lax.fori_loop(0, source_count, look, 0)
    count, width = small.shape
    run = width // (highs * QUAD)
    whole = small[...]
    gain[...] = whole[count - 1 :, :]
    for owner in range(QUAD):

        @pl.when(lax.rem(me, QUAD) == owner)
        def _():
            starts = [(high * QUAD + owner) * run for high in range(highs)]
            parts = [whole[: count - 1, at : at + run] for at in starts]
            table[...] = jnp.concatenate(parts, axis=1)


def norm_kernel(place, sources, lens, gain, *refs):
    arrived, (kept, normed) = refs[:-2], refs[-2:]
    for number in range(kept.shape[0]):
        shift = jnp.bitwise_xor(sources[number], place[0]) // QUAD
        for other, ref in enumerate(arrived):

            @pl.when(shift == other)
            def _():
                kept[number] = ref[number]

        wide = kept[number].astype(F32)
        mean = jnp.mean(wide, axis=1, keepdims=True)
        centred = wide - mean
        var = jnp.mean(centred * centred, axis=1, keepdims=True)
        value = centred * lax.rsqrt(var + 1e-05) * gain[...]
        steps = lax.broadcasted_iota(jnp.int32, value.shape, 0)
        normed[number] = jnp.where(steps < lens[number], value, 0.0).astype(BF16)


def conv_rows(block, taps):
    long, chans = block.shape
    count = taps.shape[0]
    front = (count - 1) // 2
    groups = long // 8
    pieces = [block[8 * at : 8 * at + 8, :] for at in range(groups)]
    total = None
    for residue in range(8):
        rows = []
        for at in range(groups + 1):
            value = None
            for step in range(-(count // 8) - 1, count // 8 + 2):
                tap = 8 * step + residue + front - 16
                source = at + step - 2
                if 0 <= tap < count and 0 <= source < groups:
                    term = pieces[source] * taps[tap : tap + 1, :]
                    value = term if value is None else value + term
            rows.append(jnp.zeros((8, chans), F32) if value is None else value)
        whole = jnp.concatenate(rows, axis=0)[residue : residue + long, :]
        total = whole if total is None else total + whole
    return total


def main_kernel(pieces, where, kept, table, *refs):
    normed, weights = refs[:QUAD], refs[QUAD : QUAD + pieces]
    own, outs = refs[QUAD + pieces], refs[QUAD + pieces + 1 : 2 * QUAD + pieces]
    rows_buf, in_buf, out_buf, glu_buf, act_buf = refs[2 * QUAD + pieces :]
    recv, long, width = kept.shape
    tall = recv * long
    chans = table.shape[1]
    taps = table[: table.shape[0] - 2, :]
    scale, shift = table[table.shape[0] - 2 : table.shape[0] - 1, :], table[table.shape[0] - 1 :, :]
    for number, ref in enumerate(normed):
        rows_buf[pl.ds(number * tall, tall), :] = ref[...].reshape(tall, width)
    if pieces == 2:
        w_in, w_out = weights
    else:
        w_in, w_out = in_buf, out_buf
        depth, wide = weights[0].shape[1:]
        for number, ref in enumerate(weights):
            for inner in range(QUAD):
                start = pl.multiple_of(where[number, inner] * depth, 16)
                in_buf[pl.ds(start, depth), :] = ref[inner]
            start = pl.multiple_of(where[number, QUAD] * depth, 16)
            for half in range(width // wide):
                out_buf[pl.ds(start, depth), half * wide : half * wide + wide] = ref[QUAD + half]
    glu_in = jnp.dot(rows_buf[...], w_in[...], preferred_element_type=F32)
    glu_buf[...] = glu_in[:, :chans] * jax.nn.sigmoid(glu_in[:, chans:])

    def utterance(at, carry):
        start = pl.multiple_of(at * long, long)
        moved = conv_rows(glu_buf[pl.ds(start, long), :], taps) * scale + shift
        act_buf[pl.ds(start, long), :] = (moved * jax.nn.sigmoid(moved)).astype(BF16)
        return carry

    lax.fori_loop(0, QUAD * recv, utterance, 0)
    mixed = jnp.dot(act_buf[...], w_out[...], preferred_element_type=F32)
    mixed = mixed.reshape(QUAD, recv, long, width)
    own[...] = kept[...].astype(F32) + mixed[0]
    for number, out in enumerate(outs, 1):
        out[...] = mixed[number].astype(BF16)


def shards(
    frames, ln_gain, w_in, depth_kernel, bn_scale, bn_shift, w_out, lengths, destinations, offsets
):
    dp_count, fsdp_count = lax.axis_size("dp"), lax.axis_size("fsdp")
    devices = dp_count * fsdp_count
    highs = dp_count // QUAD
    dp_index = lax.axis_index("dp")
    quad = dp_index % QUAD
    line = dp_index // QUAD * fsdp_count + lax.axis_index("fsdp")
    recv = lengths.shape[2] // 3
    _, _, long, width = frames.shape
    depth = w_in.shape[0]
    chans = width // QUAD
    wide = 2 * chans
    taps = depth_kernel.shape[0]

    def swap(array, high=0, quad=0, fsdp=0):
        mask = (high * QUAD + quad) * fsdp_count + fsdp
        return lax.ppermute(array, ("dp", "fsdp"), [(at, at ^ mask) for at in range(devices)])

    def quad_swap(arrays):
        return [arrays[0]] + [swap(arrays[mask], quad=mask) for mask in range(1, QUAD)]

    def gated(arrays, others):
        return lax.optimization_barrier((arrays, others))[0]

    place = dp_index.astype(jnp.int32)[None]
    packed = jnp.stack([lengths[0], destinations[0], offsets[0]]).reshape(-1)
    small = jnp.concatenate([depth_kernel, bn_scale[None], bn_shift[None], ln_gain[None]])
    bits = [1 << at for at in range((highs * fsdp_count).bit_length() - 1)]
    chip_bits = [bit for bit in reversed(bits) if 1 < bit < fsdp_count]

    if depth % 16 == 0:
        split = call(
            functools.partial(split_kernel, highs),
            [like(BF16, depth, wide)] * QUAD,
            [SMEM, VMEM],
            [VMEM] * QUAD,
            (place, w_in),
            [like(BF16, QUAD, depth, wide)],
        )
    else:
        by_owner = w_in.reshape(depth, 2, highs, QUAD, chans // highs).transpose(3, 0, 1, 2, 4)
        by_owner = by_owner.reshape(QUAD, depth, wide)
        split = [
            lax.dynamic_index_in_dim(by_owner, quad ^ mask, 0, keepdims=False)
            for mask in range(QUAD)
        ]
    columns = quad_swap(split)

    near = call(
        functools.partial(send_kernel, dp_count),
        [like(BF16, highs, long, width)] * QUAD,
        [SMEM, SMEM, VMEM],
        [VMEM] * QUAD,
        (place, packed, frames[0]),
    )
    near = quad_swap(near)
    columns = gated(columns, near[1])
    sources, lens, table, gain = call(
        functools.partial(table_kernel, dp_count, long),
        [like(jnp.int32, recv)] * 2 + [like(F32, taps + 2, chans), like(F32, 1, width)],
        [SMEM] * 2 + [VMEM],
        [SMEM, SMEM, VMEM, VMEM],
        (place, packed, small),
    )
    utts = like(BF16, recv, long, width)
    held, *far = call(
        functools.partial(merge_kernel, dp_count),
        [utts] * highs,
        [SMEM] * 2 + [VMEM] * QUAD,
        [VMEM] * highs,
        (gated(place, (lens, gain)), packed, *near),
    )
    merged = far
    far = [swap(part, high=mask) for mask, part in enumerate(far, 1)]

    halves = [w_out[:, at : at + wide] for at in range(0, width, wide)]
    pieces = [jnp.stack(columns + halves)]
    shifts = [mask * fsdp_count for mask in range(highs)]
    waiting = gated(pieces[0], merged)
    chip_first = [swap(waiting, fsdp=bit) for bit in chip_bits[:1]]
    crossing = [swap(pieces[0], high=mask) for mask in range(1, highs)]
    pieces += gated(crossing, (merged, chip_first))
    early = [swap(part, fsdp=1) for part in pieces[:1] + chip_first]
    far = gated(far, early[:1])
    kept, normed = call(
        norm_kernel,
        [utts, utts],
        [SMEM] * 3 + [VMEM] * (1 + highs),
        [VMEM, VMEM],
        (place, sources, lens, gain, held, *far),
    )
    for bit in chip_bits:
        first = chip_first if bit == chip_bits[0] else []
        pieces = pieces + first + [swap(part, fsdp=bit) for part in pieces[len(first) :]]
        shifts = shifts + [shift ^ bit for shift in shifts]
    normed = quad_swap([normed] * QUAD)
    ends = len(shifts) // 2 + 1
    pieces[ends:] = gated(pieces[ends:], normed)
    cored = [swap(part, fsdp=1) for part in pieces]
    cored[0], cored[len(shifts) // 2] = early[0], early[-1]
    pieces = pieces + cored
    shifts = shifts + [shift ^ 1 for shift in shifts]

    out_rows = line ^ jnp.array(shifts)
    in_rows = out_rows // fsdp_count * QUAD
    in_rows = in_rows[:, None] + (quad ^ jnp.arange(QUAD))[None, :]
    in_rows = in_rows * fsdp_count + (out_rows % fsdp_count)[:, None]
    where = jnp.concatenate([in_rows, out_rows[:, None]], 1).astype(jnp.int32)
    if depth % 16:
        together = jnp.stack(pieces)
        flat = together[:, :QUAD].reshape(-1, depth, wide)
        all_in = jnp.zeros_like(flat).at[where[:, :QUAD].reshape(-1)].set(flat)
        flat = together[:, QUAD:].transpose(0, 2, 1, 3).reshape(-1, depth, width)
        all_out = jnp.zeros_like(flat).at[where[:, QUAD]].set(flat)
        pieces = [all_in.reshape(width, wide), all_out.reshape(chans, width)]

    tall = QUAD * recv * long
    partial_sums = call(
        functools.partial(main_kernel, len(pieces)),
        [like(F32, recv, long, width)] + [utts] * (QUAD - 1),
        [SMEM] + [VMEM] * (2 + QUAD + len(pieces)),
        [VMEM] * QUAD,
        (where, kept, table, *normed, *pieces),
        [
            like(BF16, tall, width),
            like(BF16, width, wide),
            like(BF16, chans, width),
            like(F32, tall, chans),
            like(BF16, tall, chans),
        ],
        flops=6 * tall * width * chans,
    )
    own, *others = quad_swap(partial_sums)
    for part in others:
        own = own + part.astype(F32)
    live = jnp.arange(long, dtype=jnp.int32)[None, :, None] < lens[:, None, None]
    return jnp.where(live, own, 0.0).astype(BF16)[None]


def solution(mesh):
    return jax.shard_map(
        shards,
        mesh=mesh,
        in_specs=(
            P("fsdp", "dp", None, None),
            P(),
            P(("dp", "fsdp"), None),
            P(),
            P(),
            P(),
            P(("dp", "fsdp"), None),
            P("fsdp", None, None),
            P("fsdp", None, None),
            P("fsdp", None, None),
        ),
        out_specs=P("fsdp", "dp", None, None),
        check_vma=False,
    )
```
